32 devices in a mesh: rep: 8 (over z, y), shard: 4 (over x, core).
Axes of the slice: x: 2, y: 2, z: 4, core: 2. Of those that a mesh axis runs over, the one named last changes fastest.
Arguments:
- tokens: bfloat16 [16, 1024, 1536], P('rep', 'shard'), may hold values from -6 to 6
- cotangent: bfloat16 [16, 1024, 1536], P('rep', 'shard'), may hold values from -6 to 6
- prefix_len: int32 [16], P('rep'), may hold values from 102 to 512
- adapter_index: int32 [16], P('rep'), may hold values from 0 to 7
- gain_attn: bfloat16 [1536], replicated, may hold values from 0.099609375 to 1.8984375
- gain_mlp: bfloat16 [1536], replicated, may hold values from 0.099609375 to 1.8984375
- query_weight: bfloat16 [1536, 1536], P('shard'), may hold values from -0.15625 to 0.15625
- key_weight: bfloat16 [1536, 768], P('shard'), may hold values from -0.15625 to 0.15625
- value_weight: bfloat16 [1536, 768], P('shard'), may hold values from -0.15625 to 0.15625
- output_weight: bfloat16 [1536, 1536], P('shard'), may hold values from -2.5 to 2.5
- gate_weight: bfloat16 [1536, 4096], P('shard'), may hold values from -0.15625 to 0.15625
- lift_weight: bfloat16 [1536, 4096], P('shard'), may hold values from -0.15625 to 0.15625
- drop_weight: bfloat16 [4096, 1536], P('shard'), may hold values from -0.09375 to 0.09375
- query_inner: bfloat16 [1536, 128], P('shard'), may hold values from -0.15625 to 0.15625
- query_outer: bfloat16 [128, 1536], P(None, 'shard'), may hold values from -0.75 to 0.75
- key_inner: bfloat16 [1536, 128], P('shard'), may hold values from -0.15625 to 0.15625
- key_outer: bfloat16 [128, 768], P(None, 'shard'), may hold values from -0.75 to 0.75
- value_inner: bfloat16 [1536, 128], P('shard'), may hold values from -0.15625 to 0.15625
- value_outer: bfloat16 [128, 768], P(None, 'shard'), may hold values from -0.75 to 0.75
- output_inner: bfloat16 [1536, 128], P('shard'), may hold values from -2.5 to 2.5
- output_outer: bfloat16 [128, 1536], P(None, 'shard'), may hold values from -0.75 to 0.75
- gate_inner: bfloat16 [1536, 128], P('shard'), may hold values from -0.15625 to 0.15625
- gate_outer: bfloat16 [128, 4096], P(None, 'shard'), may hold values from -0.75 to 0.75
- lift_inner: bfloat16 [1536, 128], P('shard'), may hold values from -0.15625 to 0.15625
- lift_outer: bfloat16 [128, 4096], P(None, 'shard'), may hold values from -0.75 to 0.75
- drop_inner: bfloat16 [4096, 128], P('shard'), may hold values from -0.09375 to 0.09375
- drop_outer: bfloat16 [128, 1536], P(None, 'shard'), may hold values from -0.75 to 0.75
Outputs:
- mixed: bfloat16 [16, 1024, 1536], P('rep', 'shard')
- input_grad: float32 [16, 1024, 1536], P('rep', 'shard')
- query_inner_grad: float32 [1536, 128], P('shard')
- query_outer_grad: float32 [128, 1536], P(None, 'shard')
- key_inner_grad: float32 [1536, 128], P('shard')
- key_outer_grad: float32 [128, 768], P(None, 'shard')
- value_inner_grad: float32 [1536, 128], P('shard')
- value_outer_grad: float32 [128, 768], P(None, 'shard')
- output_inner_grad: float32 [1536, 128], P('shard')
- output_outer_grad: float32 [128, 1536], P(None, 'shard')
- gate_inner_grad: float32 [1536, 128], P('shard')
- gate_outer_grad: float32 [128, 4096], P(None, 'shard')
- lift_inner_grad: float32 [1536, 128], P('shard')
- lift_outer_grad: float32 [128, 4096], P(None, 'shard')
- drop_inner_grad: float32 [4096, 128], P('shard')
- drop_outer_grad: float32 [128, 1536], P(None, 'shard')
The draws below stay inside these ranges and needn't reach their ends.
All inputs are finite; a program needn't handle non-finite values.
Results may differ from the reference program's by a relative error of at most 0.02.
Values may be sent and summed in bfloat16 or wider, within the bound.
No kernel may reach another device: no remote copies, remote signals or barrier semaphores. Data moves between devices by JAX's collectives and lax.ppermute only.
A program may use at most 208 MiB of HBM per device.

```python
import math
import jax
import jax.numpy as jnp
from jax import lax

D = 1536
HEADS = 16
KV_HEADS = 8
HEAD_DIM = 96
FF = 4096
RANK = 16
ADAPTERS = 8
LEN = 1024
SEQS = 16
KV = 768
MIX = 128


def plant(values, key, least, top_value):
    extent = values.shape
    index_at = [jax.random.randint(jax.random.fold_in(key, axis), (), 0, extent[axis]) for axis in range(len(extent))]
    values = values.at[tuple(index_at)].set(least)
    longest = extent.index(max(extent))
    index_at[longest] = (index_at[longest] + 1) % extent[longest]
    return values.at[tuple(index_at)].set(top_value)


def shard_levels(own_key, dims, pieces, low, largest):
    factor_of, own = 1.0, jax.random.fold_in(own_key, 6)
    for axis_at, shards_of in pieces:
        heights = jnp.exp(jax.random.uniform(jax.random.fold_in(own, axis_at), (shards_of,), jnp.float32, low / len(pieces), largest / len(pieces)))
        factor_of = factor_of * jnp.repeat(heights, dims[axis_at] // shards_of).reshape([-1 if axis == axis_at else 1 for axis in range(len(dims))])
    return factor_of


def normal_values(stream_key, extent, deviation, bound, cuts=(), held_as=jnp.bfloat16):
    gain = shard_levels(stream_key, extent, cuts, -0.22, 0.18) if cuts else 1.0
    entries = jax.random.normal(stream_key, extent, jnp.float32) * deviation * gain
    return jnp.minimum(jnp.maximum(entries, -bound), bound).astype(held_as)


def setup_inputs(seed: int = 0) -> dict:
    arg_keys = jax.random.split(jax.random.key(seed), 28)
    return {
        "tokens": normal_values(arg_keys[0], (SEQS, LEN, D), 1.0, 6.0, ((0, 8), (1, 4))),
        "cotangent": normal_values(arg_keys[1], (SEQS, LEN, D), 1.0, 6.0, ((0, 8), (1, 4))),
        "prefix_len": plant(jax.random.randint(arg_keys[2], (SEQS,), LEN // 10, LEN // 2 + 1), jax.random.fold_in(arg_keys[2], 1), LEN // 10, (LEN // 2 + 1) - 1).astype(jnp.int32),
        "adapter_index": plant(jax.random.randint(arg_keys[3], (SEQS,), 0, ADAPTERS), jax.random.fold_in(arg_keys[3], 1), 0, ADAPTERS - 1).astype(jnp.int32),
        "gain_attn": jnp.clip(1.0 + 0.18 * jax.random.normal(arg_keys[4], (D,), jnp.float32), 0.099609375, 1.8984375).astype(jnp.bfloat16),
        "gain_mlp": jnp.clip(1.0 + 0.18 * jax.random.normal(arg_keys[5], (D,), jnp.float32), 0.099609375, 1.8984375).astype(jnp.bfloat16),
        "query_weight": normal_values(arg_keys[6], (D, D), D ** -0.5, 0.15625, ((0, 4),)),
        "key_weight": normal_values(arg_keys[7], (D, KV), D ** -0.5, 0.15625, ((0, 4),)),
        "value_weight": normal_values(arg_keys[8], (D, KV), D ** -0.5, 0.15625, ((0, 4),)),
        "output_weight": normal_values(arg_keys[9], (D, D), (max(D // 256, 4)) ** -0.5, 2.5, ((0, 4),)),
        "gate_weight": normal_values(arg_keys[10], (D, FF), D ** -0.5, 0.15625, ((0, 4),)),
        "lift_weight": normal_values(arg_keys[11], (D, FF), D ** -0.5, 0.15625, ((0, 4),)),
        "drop_weight": normal_values(arg_keys[12], (FF, D), FF ** -0.5, 0.09375, ((0, 4),)),
        "query_inner": normal_values(arg_keys[13], (D, MIX), D ** -0.5, 0.15625, ((0, 4),)),
        "query_outer": normal_values(arg_keys[14], (MIX, D), (4 * RANK) ** -0.5, 0.75, ((1, 4),)),
        "key_inner": normal_values(arg_keys[15], (D, MIX), D ** -0.5, 0.15625, ((0, 4),)),
        "key_outer": normal_values(arg_keys[16], (MIX, KV), (4 * RANK) ** -0.5, 0.75, ((1, 4),)),
        "value_inner": normal_values(arg_keys[17], (D, MIX), D ** -0.5, 0.15625, ((0, 4),)),
        "value_outer": normal_values(arg_keys[18], (MIX, KV), (4 * RANK) ** -0.5, 0.75, ((1, 4),)),
        "output_inner": normal_values(arg_keys[19], (D, MIX), (max(D // 256, 4)) ** -0.5, 2.5, ((0, 4),)),
        "output_outer": normal_values(arg_keys[20], (MIX, D), (4 * RANK) ** -0.5, 0.75, ((1, 4),)),
        "gate_inner": normal_values(arg_keys[21], (D, MIX), D ** -0.5, 0.15625, ((0, 4),)),
        "gate_outer": normal_values(arg_keys[22], (MIX, FF), (4 * RANK) ** -0.5, 0.75, ((1, 4),)),
        "lift_inner": normal_values(arg_keys[23], (D, MIX), D ** -0.5, 0.15625, ((0, 4),)),
        "lift_outer": normal_values(arg_keys[24], (MIX, FF), (4 * RANK) ** -0.5, 0.75, ((1, 4),)),
        "drop_inner": normal_values(arg_keys[25], (FF, MIX), FF ** -0.5, 0.09375, ((0, 4),)),
        "drop_outer": normal_values(arg_keys[26], (MIX, D), (4 * RANK) ** -0.5, 0.75, ((1, 4),)),
    }


@jax.custom_vjp
def low(v):
    return lax.optimization_barrier(v.astype(jnp.bfloat16)).astype(jnp.float32)

@jax.custom_vjp
def low_back(v):
    return v

def low_keep(v):
    return (low(v), None)

def low_pass(kept, grad):
    return (grad,)

def back_keep(v):
    return (v, None)

def back_low(kept, grad):
    return (low(grad),)
low.defvjp(low_keep, low_pass)
low_back.defvjp(back_keep, back_low)
EPSILON = 1e-05
ROPE_BASE = 100000.0
MASKED_SCORE = -1e+30

def matmul(left, right):
    return jnp.dot(left, right, precision=lax.Precision.HIGHEST, preferred_element_type=jnp.float32)

def rotary_tables(positions, head_dim):
    half_dim = head_dim // 2
    freq_index = jnp.arange(half_dim).astype(jnp.float32)
    frequency = jnp.exp(freq_index * (-2.0 * math.log(ROPE_BASE) / head_dim))
    angles = positions[:, None] * frequency[None, :]
    return (jnp.cos(angles)[:, None, :], jnp.sin(angles)[:, None, :])

def rotate(inputs, cos_table, sine_table):
    half_dim = inputs.shape[-1] // 2
    first_half = inputs[..., :half_dim]
    second_half = inputs[..., half_dim:]
    return jnp.concatenate([first_half * cos_table - second_half * sine_table, second_half * cos_table + first_half * sine_table], axis=-1)

def rms_scale(inputs):
    return lax.rsqrt(lax.optimization_barrier(jnp.mean(inputs * inputs, axis=-1, keepdims=True)) + EPSILON)

def block_forward(inputs, adapter_set, weights, gain_pair, prefix, onehot):
    query_weight, key_weight, value_weight, output_weight, gate_weight, lift_weight, drop_weight = weights
    query_inner, query_outer, key_inner, key_outer, value_inner, value_outer, output_inner, output_outer, gate_inner, gate_outer, lift_inner, lift_outer, drop_inner, drop_outer = adapter_set
    length = inputs.shape[0]
    group_size = HEADS // KV_HEADS

    def project(source, weight, inner_mat, outer_mat):
        hidden = low(low_back(matmul(source, inner_mat)) * onehot)
        return matmul(source, weight) + matmul(hidden, outer_mat)
    normed = low(inputs * rms_scale(inputs) * gain_pair[0])
    positions = jnp.arange(length).astype(jnp.float32)
    cos_table, sine_table = rotary_tables(positions, HEAD_DIM)
    queries = low(rotate(low_back(project(normed, query_weight, query_inner, query_outer)).reshape(length, HEADS, HEAD_DIM), cos_table, sine_table))
    key_rot = low(rotate(low_back(project(normed, key_weight, key_inner, key_outer)).reshape(length, KV_HEADS, HEAD_DIM), cos_table, sine_table))
    values = low(low_back(project(normed, value_weight, value_inner, value_outer))).reshape(length, KV_HEADS, HEAD_DIM)
    grouped = queries.reshape(length, KV_HEADS, group_size, HEAD_DIM)
    scores = low_back(jnp.einsum('qkgd,jkd->kgqj', grouped, key_rot, precision=lax.Precision.HIGHEST) * HEAD_DIM ** (-0.5))
    places = jnp.arange(length)
    allowed = (places[None, :] <= places[:, None]) | (places[None, :] < prefix)
    probs_low = low(jax.nn.softmax(jnp.where(allowed, scores, MASKED_SCORE), axis=-1))
    attended = low(low_back(jnp.einsum('kgqj,jkd->qkgd', probs_low, values, precision=lax.Precision.HIGHEST))).reshape(length, HEADS * HEAD_DIM)
    middle = inputs + low_back(project(attended, output_weight, output_inner, output_outer))
    normed_mlp = low(middle * rms_scale(middle) * gain_pair[1])
    gate_act = low_back(project(normed_mlp, gate_weight, gate_inner, gate_outer))
    lift_act = low_back(project(normed_mlp, lift_weight, lift_inner, lift_outer))
    active = low(jax.nn.silu(gate_act) * lift_act)
    return middle + low_back(project(active, drop_weight, drop_inner, drop_outer))

def reference(tokens, cotangent, prefix_len, adapter_index, gain_attn, gain_mlp, query_weight, key_weight, value_weight, output_weight, gate_weight, lift_weight, drop_weight, query_inner, query_outer, key_inner, key_outer, value_inner, value_outer, output_inner, output_outer, gate_inner, gate_outer, lift_inner, lift_outer, drop_inner, drop_outer):
    weights = tuple((w_item.astype(jnp.float32) for w_item in (query_weight, key_weight, value_weight, output_weight, gate_weight, lift_weight, drop_weight)))
    gain_pair = (gain_attn.astype(jnp.float32), gain_mlp.astype(jnp.float32))
    adapter_set = tuple((a_item.astype(jnp.float32) for a_item in (query_inner, query_outer, key_inner, key_outer, value_inner, value_outer, output_inner, output_outer, gate_inner, gate_outer, lift_inner, lift_outer, drop_inner, drop_outer)))
    column_owner = (jnp.arange(ADAPTERS * RANK) // RANK).astype(jnp.int32)

    def per_sequence(totals, sequence_item):
        inputs, cot_item, prefix, chosen = sequence_item
        onehot = (column_owner == chosen.astype(jnp.int32)).astype(jnp.float32)

        def forward(field_in, adapters_in):
            return block_forward(field_in, adapters_in, weights, gain_pair, prefix, onehot)
        result, pullback = jax.vjp(forward, inputs.astype(jnp.float32), adapter_set)
        grad_in, adapter_grads = pullback(cot_item.astype(jnp.float32))
        totals = jax.tree.map(lambda total_grad, new_grad: total_grad + new_grad, totals, adapter_grads)
        return (totals, (result.astype(jnp.bfloat16), grad_in))
    zero_grads = tuple((jnp.zeros_like(a_item) for a_item in adapter_set))
    sums, (mixed, input_grad) = lax.scan(per_sequence, zero_grads, (tokens, cotangent, prefix_len, adapter_index))
    return (mixed, input_grad, sums[0], sums[1], sums[2], sums[3], sums[4], sums[5], sums[6], sums[7], sums[8], sums[9], sums[10], sums[11], sums[12], sums[13])
```

```python
import functools
import math
from typing import NamedTuple

import jax
import jax.numpy as jnp
from jax import lax
from jax.experimental import pallas as pl
from jax.experimental.pallas import tpu as pltpu
from jax.sharding import PartitionSpec as P

HEADS = 16
KV_HEADS = 8
HEAD_DIM = 96
RANK = 16
ADAPTERS = 8
EPSILON = 1e-05
ROPE_BASE = 100000.0
MASKED_SCORE = -1e30
AXES = ("rep", "shard")
F32 = jnp.float32
BF16 = jnp.bfloat16


def move(value, target):
    reps, shards = lax.axis_size("rep"), lax.axis_size("shard")
    pairs = []
    for r in range(reps):
        for s in range(shards):
            r2, s2 = target(r, s)
            pairs.append((r * shards + s, r2 * shards + s2))
    return lax.ppermute(value, AXES, pairs)


def to_core(value):
    return move(value, lambda r, s: (r, s ^ 1))


def to_chip(value):
    return move(value, lambda r, s: (r, s ^ 2))


def to_diag(value):
    return move(value, lambda r, s: (r, s ^ 3))


def to_y(value):
    return move(value, lambda r, s: (r ^ 1, s))


def to_z(value):
    return move(value, lambda r, s: (r ^ 2, s))


PANEL = 512


class Piece(NamedTuple):
    parts: tuple
    row: int
    rows: int
    target: int
    block: int
    to_row: int
    to_col: int


class Bundle(NamedTuple):
    first: tuple
    second: tuple
    shapes: tuple


def quarter_rows(pieces):
    return sum(p.rows for p in pieces) // 4


def make_bundles(width, kv_width, ff, chunks, shards):
    rows, drop_rows = width // shards, ff // shards // chunks
    panels = width // PANEL
    first = tuple(Piece(((0, c, PANEL),), 0, rows, 0, rows, 0, c) for c in range(0, width, PANEL))
    second = []
    for c in range(0, 2 * kv_width, PANEL):
        parts, at = [], c
        while at < c + PANEL:
            source = 1 if at < kv_width else 2
            base = (source - 1) * kv_width
            stop = min(c + PANEL, base + kv_width)
            parts.append((source, at - base, stop - at))
            at = stop
        second.append(Piece(tuple(parts), 0, rows, 0, rows, 0, width + c))
    found = [Bundle(first, tuple(second), ((width, width + 2 * kv_width),))]

    def halves(source, row, height, target, block):
        return [
            tuple(
                Piece(((source, i * PANEL, PANEL),), row + h * height // 2, height // 2, target, block,
                      h * height // 2, i * PANEL)
                for i in range(panels)
            )
            for h in range(2)
        ]

    top, bottom = halves(3, 0, rows, 0, rows)
    found.append(Bundle(top, bottom, ((width, width),)))
    part = ff // shards // chunks
    for u in range(chunks):
        sides = []
        for j in range(2):
            side = []
            for c in range(0, shards * part, PANEL):
                parts = tuple(
                    (4 + j, t * (ff // shards) + u * part, part)
                    for t in range(c // part, (c + PANEL) // part)
                )
                side.append(Piece(parts, 0, rows, 0, rows, 0, 2 * c + j * PANEL))
            sides.append(tuple(side))
        top, bottom = halves(6, u * drop_rows, drop_rows, 1, drop_rows)
        cols = shards * part
        found.append(
            Bundle(sides[0] + top, sides[1] + bottom, ((width, 2 * cols), (cols, width)))
        )
    return found


def run_copies(copies, sems):
    started = []
    for i, (src, dst) in enumerate(copies):
        started.append(pltpu.make_async_copy(src, dst, sems.at[i]))
        started[-1].start()
    for c in started:
        c.wait()


def pack(place, jobs, operands, out_shapes, name):
    count = []

    def kernel(place_ref, *refs):
        ins, outs, sems = refs[: len(operands)], refs[len(operands) : -1], refs[-1]
        run_copies(jobs(place_ref, ins, outs), sems)

    class Fake:
        def __init__(self):
            self.at = self

        def __getitem__(self, _):
            return self

    count = len(jobs(None, [Fake()] * len(operands), [Fake()] * len(out_shapes)))
    return pl.pallas_call(
        kernel,
        out_shape=[jax.ShapeDtypeStruct(sh, BF16) for sh in out_shapes],
        grid_spec=pltpu.PrefetchScalarGridSpec(
            num_scalar_prefetch=1,
            grid=(1,),
            in_specs=[pl.BlockSpec(memory_space=pl.ANY)] * len(operands),
            out_specs=[pl.BlockSpec(memory_space=pltpu.VMEM)] * len(out_shapes),
            scratch_shapes=[pltpu.SemaphoreType.DMA((count,))],
        ),
        compiler_params=pltpu.CompilerParams(vmem_limit_bytes=40 * 2**20),
        name=name,
    )(place, *operands)


def quarter_start(place_ref, flip, rows):
    if place_ref is None:
        return 0
    return pl.multiple_of((place_ref[1] ^ flip) * rows, 16)


class Relay:
    def __init__(self, place, weights, bundles):
        self.place, self.weights, self.bundles = place, weights, bundles
        self.direct, self.once, self.twice = {}, {}, {}
        self.far, self.far_near = {}, {}
        self.tick = 0

    def step(self, extra=(), ties=()):
        t, bundles = self.tick, self.bundles
        self.tick += 1
        operands, shapes, kinds = [], [], []

        def operand(array):
            for i, o in enumerate(operands):
                if o is array:
                    return i
            operands.append(array)
            return len(operands) - 1

        plans = []

        def out(kind, rows, cols=PANEL):
            shapes.append((rows, cols))
            kinds.append(kind)
            return len(shapes) - 1

        if t < len(bundles):
            b = bundles[t]
            o = out("x", quarter_rows(b.first + b.second))
            used = [(operand(self.weights[q[0]]), q, p) for p in b.first + b.second for q in p.parts]

            def plan_x(pr, ins, outs, o=o, used=used):
                copies, at, col = [], 0, 0
                for i, (_, c, n), p in used:
                    q = p.rows // 4
                    rows = pl.ds(pl.multiple_of(p.row + quarter_start(pr, 0, q), 16), q)
                    copies.append((ins[i].at[rows, pl.ds(c, n)],
                                   outs[o].at[pl.ds(at, q), pl.ds(col, n)]))
                    col += n
                    if col == PANEL:
                        at, col = at + q, 0
                return copies

            plans.append(plan_x)
        y_parts, z_parts = [], []
        b1, b2, b3 = t - 1, t - 2, t - 3
        if 0 <= b1 < len(bundles):
            qa, qb = quarter_rows(bundles[b1].first), quarter_rows(bundles[b1].second)
            y_parts.append(("first", b1, [(self.direct[b1], 0, qa)]))
            z_parts.append(("first", b1, [(self.direct[b1], qa, qb)]))
        if 0 <= b2 < len(bundles):
            qa, qb = quarter_rows(bundles[b2].first), quarter_rows(bundles[b2].second)
            (ya, yo), (za, zo) = self.once[b2]
            y_parts.append(("second", b2, [(self.direct[b2], qa, qb), (za, zo, qb)]))
            z_parts.append(("second", b2, [(self.direct[b2], 0, qa), (ya, yo, qa)]))
        for kind, parts in (("y", y_parts), ("z", z_parts)):
            if not parts:
                continue
            total = sum(n for _, _, l in parts for _, _, n in l)
            o = out(kind, total)
            flat = [(operand(a), r, n) for _, _, l in parts for a, r, n in l]

            def plan_n(pr, ins, outs, o=o, flat=flat):
                copies, at = [], 0
                for i, r, n in flat:
                    copies.append((ins[i].at[pl.ds(r, n)], outs[o].at[pl.ds(at, n)]))
                    at += n
                return copies

            plans.append(plan_n)
        if 0 <= b3 < len(bundles):
            b = bundles[b3]
            o = out("c", 4 * quarter_rows(b.first + b.second))
            qa = quarter_rows(b.first)
            qb = quarter_rows(b.second)
            (ya, yo), (za, zo) = self.once[b3]
            (ys, yso), (zs, zso) = self.twice[b3]
            d = operand(self.direct[b3])
            sides = [
                (b.first, [(0, d, 0), (1, operand(ya), yo), (2, operand(zs), zso), (3, operand(zs), zso + qa)]),
                (b.second, [(0, d, qa), (2, operand(za), zo), (1, operand(ys), yso), (3, operand(ys), yso + qb)]),
            ]

            def plan_c(pr, ins, outs, o=o, sides=sides):
                copies, base = [], 0
                for pieces, quarters in sides:
                    at = 0
                    for p in pieces:
                        q = p.rows // 4
                        for flip, i, r in quarters:
                            to = pl.multiple_of(base + quarter_start(pr, flip, q), 16)
                            copies.append((ins[i].at[pl.ds(r + at, q)], outs[o].at[pl.ds(to, q)]))
                        at += q
                        base += p.rows
                return copies

            plans.append(plan_c)
        for array, index in extra:
            o = out("d", array.shape[1], array.shape[2])
            i = operand(array)

            def plan_d(pr, ins, outs, o=o, i=i, index=index):
                which = 0 if pr is None else index(pr)
                return [(ins[i].at[which], outs[o])]

            plans.append(plan_d)
        for tie in ties:
            operand(tie)

        def jobs(pr, ins, outs):
            return [c for plan in plans for c in plan(pr, ins, outs)]

        bufs = pack(self.place, jobs, operands, shapes, f"pack_{t}")
        sent = []
        for kind, buf in zip(kinds, bufs):
            if kind == "x":
                self.direct[t] = to_chip(buf)
            elif kind == "c":
                self.far[b3], self.far_near[b3] = buf, to_core(buf)
            elif kind == "d":
                sent.append(to_diag(buf))
            else:
                got = (to_y if kind == "y" else to_z)(buf)
                at = 0
                for stage, bi, l in y_parts if kind == "y" else z_parts:
                    store = self.once if stage == "first" else self.twice
                    pair = store.setdefault(bi, [None, None])
                    pair[0 if kind == "y" else 1] = (got, at)
                    at += sum(n for _, _, n in l)
        return sent, bufs


def land_copies(place_ref, bundle, own, near, far, far_near, targets):
    copies = []
    shard = 0 if place_ref is None else place_ref[0]
    for slot, refs in enumerate((own, near, far, far_near)):
        base = 0
        for p in bundle.first + bundle.second:
            to = (shard ^ slot) * p.block + p.to_row
            to = pl.ds(pl.multiple_of(to, 16), p.rows)
            dst = targets[p.target]
            if slot < 2:
                col = p.to_col
                for source, c, n in p.parts:
                    copies.append((refs[source].at[pl.ds(p.row, p.rows), pl.ds(c, n)],
                                   dst.at[to, pl.ds(col, n)], (p.target, p.to_col, slot)))
                    col += n
            else:
                copies.append((refs.at[pl.ds(base, p.rows)], dst.at[to, pl.ds(p.to_col, PANEL)],
                               (p.target, p.to_col, slot)))
            base += p.rows
    return copies


def sources_of(bundle):
    return sorted({q[0] for p in bundle.first + bundle.second for q in p.parts})


def rotary_tables(positions, head_dim):
    half_dim = head_dim // 2
    freq_index = jnp.arange(half_dim).astype(F32)
    frequency = jnp.exp(freq_index * (-2.0 * math.log(ROPE_BASE) / head_dim))
    angles = positions[:, None] * frequency[None, :]
    return jnp.cos(angles), jnp.sin(angles)


def dot(left, right):
    return jnp.dot(left, right, preferred_element_type=F32)


def dot_nt(left, right):
    return lax.dot_general(left, right, (((1,), (1,)), ((), ())), preferred_element_type=F32)


def dot_tn(left, right):
    return lax.dot_general(left, right, (((0,), (0,)), ((), ())), preferred_element_type=F32)


LOG2E = 1.4426950408889634


def last_visible(place_ref, low, lanes, block):
    shard, prefix = place_ref[0], place_ref[2]
    low_block = (shard ^ (shard // 2)) & 1
    at = low_block if low else 3 - low_block
    position = at * block + lax.broadcasted_iota(jnp.int32, (1, lanes), 1) % block
    return jnp.maximum(position + 1, prefix)


def query_start(place_ref, low, block):
    chip = place_ref[0] // 2
    return pl.multiple_of((chip if low else 1 - chip) * block, block)


def natural_rows(place_ref, own, near, into, block):
    shard = place_ref[0]
    for slot, value in (
        (0, own[0, :block]),
        (3, own[0, block:]),
        (1, near[0, :block]),
        (2, near[0, block:]),
    ):
        into[pl.ds(pl.multiple_of((shard ^ slot) * block, block), block)] = value


def hide(scores, limit, first_key):
    keys = first_key + lax.broadcasted_iota(jnp.int32, scores.shape, 0)
    return jnp.where(keys < limit, scores, MASKED_SCORE)


def masked_by_part(low, scores, limit, block):
    if low:
        return hide(scores, limit, 0)
    half = 2 * block
    return jnp.concatenate([scores[:half], hide(scores[half:], limit, half)], axis=0)


def attend_kernel(place, q, k_own, k_near, v_own, v_near, out, lse, keys, values, *, scale):
    block = q.shape[1] // 2
    group = q.shape[0]
    natural_rows(place, k_own, k_near, keys, block)
    natural_rows(place, v_own, v_near, values, block)
    values_t = values[...].T
    for part, low in enumerate((True, False)):
        count = (2 if low else 4) * block
        rows = pl.ds(query_start(place, low, block), block)
        query = jnp.concatenate([q[j, rows] for j in range(group)], axis=0)
        limit = last_visible(place, low, group * block, block)
        scores = masked_by_part(low, dot_nt(keys[:count], query), limit, block)
        top = jnp.max(scores, axis=0, keepdims=True)
        base = scale * LOG2E
        expo = jnp.exp2(scores * base - top * base)
        total = jnp.sum(expo, axis=0, keepdims=True)
        lse[0, part] = (top * base + jnp.log2(total))[0]
        result = dot(values_t[:, :count], expo.astype(BF16)) / total
        result = result.T.astype(BF16)
        for j in range(group):
            out[j, rows] = result[j * block : (j + 1) * block]


def attend(place, queries, k_own, k_near, v_own, v_near):
    heads, rows, dim = queries.shape
    kv_heads = k_own.shape[0]
    group = heads // kv_heads
    q_spec = pl.BlockSpec((group, rows, dim), lambda g, p: (g, 0, 0))
    kv_spec = pl.BlockSpec((1, rows, dim), lambda g, p: (g, 0, 0))
    lse_shape = (kv_heads, 2, group * rows // 2)
    return pl.pallas_call(
        functools.partial(attend_kernel, scale=dim ** (-0.5)),
        out_shape=[
            jax.ShapeDtypeStruct(queries.shape, BF16),
            jax.ShapeDtypeStruct(lse_shape, F32),
        ],
        grid_spec=pltpu.PrefetchScalarGridSpec(
            num_scalar_prefetch=1,
            grid=(kv_heads,),
            in_specs=[q_spec] + [kv_spec] * 4,
            out_specs=[q_spec, pl.BlockSpec((1, *lse_shape[1:]), lambda g, p: (g, 0, 0))],
            scratch_shapes=[pltpu.VMEM((2 * rows, dim), BF16)] * 2,
        ),
        compiler_params=pltpu.CompilerParams(vmem_limit_bytes=40 * 2**20),
        name="attend",
    )(place, queries, k_own, k_near, v_own, v_near)


def attend_back_kernel(
    place, q, k_own, k_near, v_own, v_near, grad, lse, cos_t, sin_t,
    dq, dk_own, dk_send, dv_own, dv_send, keys, values, dk, dv, *, scale
):
    block = q.shape[1] // 2
    group = q.shape[0]
    half = q.shape[2] // 2
    natural_rows(place, k_own, k_near, keys, block)
    natural_rows(place, v_own, v_near, values, block)
    keys_t = keys[...].T
    for part, low in ((1, False), (0, True)):
        count = (2 if low else 4) * block
        start = query_start(place, low, block)
        rows = pl.ds(start, block)
        query = jnp.concatenate([q[j, rows] for j in range(group)], axis=0)
        out_grad = jnp.concatenate([grad[j, rows] for j in range(group)], axis=0)
        limit = last_visible(place, low, group * block, block)
        scores = masked_by_part(low, dot_nt(keys[:count], query), limit, block)
        probs = jnp.exp2(scores * (scale * LOG2E) - lse[0, part][None])
        probs_grad = dot_nt(values[:count], out_grad)
        mean = jnp.sum(probs * probs_grad, axis=0, keepdims=True)
        score_grad = (probs * (probs_grad - mean)).astype(BF16)
        v_part = dot(probs.astype(BF16), out_grad)
        k_part = dot(score_grad, query) * scale
        if low:
            dk[:count] += k_part
            dv[:count] += v_part
        else:
            dk[...] = k_part
            dv[...] = v_part
        turned = dot(keys_t[:, :count], score_grad) * scale
        cos = jnp.concatenate([cos_t[:, rows]] * group, axis=1)
        sin = jnp.concatenate([sin_t[:, rows]] * group, axis=1)
        u, w = turned[:half], turned[half:]
        turned = jnp.concatenate([u * cos + w * sin, w * cos - u * sin], axis=0)
        turned = turned.T.astype(BF16)
        for j in range(group):
            dq[j, rows] = turned[j * block : (j + 1) * block]
    shard = place[0]
    for slot, at, own in ((0, 0, True), (3, 1, True), (1, 0, False), (2, 1, False)):
        rows = pl.ds(pl.multiple_of((shard ^ slot) * block, block), block)
        to = slice(at * block, (at + 1) * block)
        (dk_own if own else dk_send)[0, to] = dk[rows].astype(F32 if own else BF16)
        (dv_own if own else dv_send)[0, to] = dv[rows].astype(F32 if own else BF16)


def attend_back(place, queries, k_own, k_near, v_own, v_near, grad, lse, cos_t, sin_t):
    heads, rows, dim = queries.shape
    kv_heads = k_own.shape[0]
    group = heads // kv_heads
    q_spec = pl.BlockSpec((group, rows, dim), lambda g, p: (g, 0, 0))
    kv_spec = pl.BlockSpec((1, rows, dim), lambda g, p: (g, 0, 0))
    whole = pl.BlockSpec(cos_t.shape, lambda g, p: (0, 0))
    return pl.pallas_call(
        functools.partial(attend_back_kernel, scale=dim ** (-0.5)),
        out_shape=[
            jax.ShapeDtypeStruct(queries.shape, BF16),
            jax.ShapeDtypeStruct(k_own.shape, F32),
            jax.ShapeDtypeStruct(k_own.shape, BF16),
            jax.ShapeDtypeStruct(k_own.shape, F32),
            jax.ShapeDtypeStruct(k_own.shape, BF16),
        ],
        grid_spec=pltpu.PrefetchScalarGridSpec(
            num_scalar_prefetch=1,
            grid=(kv_heads,),
            in_specs=[q_spec] + [kv_spec] * 4
            + [q_spec, pl.BlockSpec((1, *lse.shape[1:]), lambda g, p: (g, 0, 0)), whole, whole],
            out_specs=[q_spec] + [kv_spec] * 4,
            scratch_shapes=[pltpu.VMEM((2 * rows, dim), BF16)] * 2
            + [pltpu.VMEM((2 * rows, dim), F32)] * 2,
        ),
        compiler_params=pltpu.CompilerParams(vmem_limit_bytes=40 * 2**20),
        name="attend_back",
    )(place, queries, k_own, k_near, v_own, v_near, grad, lse, cos_t, sin_t)


class Landing:
    def __init__(self, place, bundle, refs, targets, sems):
        used = sources_of(bundle)
        n = len(used)
        own, near = dict(zip(used, refs[:n])), dict(zip(used, refs[n : 2 * n]))
        listed = land_copies(place, bundle, own, near, refs[2 * n], refs[2 * n + 1], targets)
        self.copies = [
            (key, pltpu.make_async_copy(src, dst, sems.at[i])) for i, (src, dst, key) in enumerate(listed)
        ]
        self.copies.sort(key=lambda c: c[0])
        for _, c in self.copies:
            c.start()

    def wait(self, wanted=None):
        left = []
        for key, c in self.copies:
            if wanted is None or wanted(key):
                c.wait()
            else:
                left.append((key, c))
        self.copies = left


def landing_operands(bundle, weights, near, far, far_near):
    used = sources_of(bundle)
    return [weights[i] for i in used] + [near[i] for i in used] + [far, far_near]


def landing_count(bundle):
    return sum(2 * len(p.parts) + 2 for p in bundle.first + bundle.second)


def kernel_call(body, place, bundle, landing, operands, outs, scratch, name, aliases=None, flops=0):
    n_land, n_in, n_out, n_w = len(landing), len(operands), len(outs), len(bundle.shapes)

    def kernel(place_ref, *refs):
        land, refs = refs[:n_land], refs[n_land:]
        ins, refs = refs[:n_in], refs[n_in:]
        out, refs = refs[:n_out], refs[n_out:]
        body(place_ref, land, ins, out, refs[:n_w], refs[n_w], refs[n_w + 1 :])

    def spec(where):
        return pl.BlockSpec(memory_space=where)

    return pl.pallas_call(
        kernel,
        out_shape=[o for o, _ in outs],
        grid_spec=pltpu.PrefetchScalarGridSpec(
            num_scalar_prefetch=1,
            grid=(1,),
            in_specs=[spec(pl.ANY)] * n_land + [spec(w) for _, w in operands],
            out_specs=[spec(w) for _, w in outs],
            scratch_shapes=[pltpu.VMEM(sh, BF16) for sh in bundle.shapes]
            + [pltpu.SemaphoreType.DMA((landing_count(bundle),))]
            + list(scratch),
        ),
        input_output_aliases={1 + n_land + i: o for i, o in (aliases or {}).items()},
        compiler_params=pltpu.CompilerParams(vmem_limit_bytes=58 * 2**20),
        cost_estimate=pl.CostEstimate(flops=flops, bytes_accessed=20 * 2**20, transcendentals=0),
        name=name,
    )(place, *landing, *[a for a, _ in operands])


VM = pltpu.VMEM


def like(shape, dtype):
    return jax.ShapeDtypeStruct(shape, dtype)


def turn(value, cos_full, sin_signed, half):
    swapped = jnp.concatenate([value[:, half:], value[:, :half]], axis=1)
    return value * cos_full + swapped * sin_signed


def qkv_forward(place, bundle, landing, tokens_kept, tokens_back, gain, inner, outer, cos, sin):
    block, width = tokens_kept.shape
    rows = 2 * block
    total = bundle.shapes[0][1]
    kv = (total - width) // 2
    wide = 8 * HEAD_DIM
    half = HEAD_DIM // 2

    def body(pr, land_refs, ins, outs, weights, sems, scratch):
        kept, back, gain_ref, inner_ref, outer_ref, cos_ref, sin_ref = ins
        q, k, v, hidden_ref, normed_ref, x_ref = outs
        (w,) = weights
        landing = Landing(pr, bundle, land_refs, weights, sems)
        x_ref[:block] = kept[...]
        x_ref[block:] = back[...]
        x = x_ref[...].astype(F32)
        scale = lax.rsqrt(jnp.mean(x * x, axis=-1, keepdims=True) + EPSILON)
        normed_ref[...] = (x * scale * gain_ref[...].astype(F32)).astype(BF16)
        hidden_ref[...] = dot_nt(normed_ref[...], inner_ref[...]).astype(BF16)

        def columns(at):
            cols = pl.ds(at, wide)
            return dot(normed_ref[...], w[:, cols]) + dot(hidden_ref[...], outer_ref[:, cols])

        landing.wait(lambda key: key[1] < width)
        for i in range(width // wide):
            acc = columns(i * wide)
            for h in range(8):
                one = acc[:, h * HEAD_DIM : (h + 1) * HEAD_DIM]
                q[8 * i + h] = turn(one, cos_ref[...], sin_ref[...], half).astype(BF16)
        landing.wait()
        acc = columns(width)
        for h in range(8):
            one = acc[:, h * HEAD_DIM : (h + 1) * HEAD_DIM]
            k[h] = turn(one, cos_ref[...], sin_ref[...], half).astype(BF16)
        acc = columns(width + kv)
        for h in range(8):
            v[h] = acc[:, h * HEAD_DIM : (h + 1) * HEAD_DIM].astype(BF16)

    heads = width // HEAD_DIM
    return kernel_call(
        body, place, bundle, landing,
        [(tokens_kept, VM), (tokens_back, VM), (gain, VM), (inner, VM), (outer, VM), (cos, VM), (sin, VM)],
        [
            (like((heads, rows, HEAD_DIM), BF16), VM),
            (like((kv // HEAD_DIM, rows, HEAD_DIM), BF16), VM),
            (like((kv // HEAD_DIM, rows, HEAD_DIM), BF16), VM),
            (like((rows, inner.shape[0]), BF16), VM),
            (like((rows, width), BF16), VM),
            (like((rows, width), BF16), VM),
        ],
        [], "qkv_forward", flops=2 * rows * width * total,
    )


def out_forward(place, bundle, landing, heads_out, x, gain, inner, outer):
    rows, width = x.shape
    heads = heads_out.shape[0]

    def body(pr, land_refs, ins, outs, weights, sems, scratch):
        heads_ref, x_ref, gain_ref, inner_ref, outer_ref = ins
        middle, normed, attended, hidden = outs
        landing = Landing(pr, bundle, land_refs, weights, sems)
        for h in range(heads):
            attended[:, h * HEAD_DIM : (h + 1) * HEAD_DIM] = heads_ref[h]
        hidden[...] = dot_nt(attended[...], inner_ref[...]).astype(BF16)
        landing.wait()
        wide = width // 2
        squares = jnp.zeros((rows, 1), F32)
        for i in range(2):
            cols = pl.ds(i * wide, wide)
            branch = dot(attended[...], weights[0][:, cols]) + dot(hidden[...], outer_ref[:, cols])
            value = x_ref[:, cols].astype(F32) + branch
            middle[:, cols] = value
            squares += jnp.sum(value * value, axis=-1, keepdims=True)
        scale = lax.rsqrt(squares / width + EPSILON)
        normed[...] = (middle[...] * scale * gain_ref[...].astype(F32)).astype(BF16)

    return kernel_call(
        body, place, bundle, landing,
        [(heads_out, VM), (x, VM), (gain, VM), (inner, VM), (outer, VM)],
        [
            (like((rows, width), F32), VM),
            (like((rows, width), BF16), VM),
            (like((rows, width), BF16), VM),
            (like((rows, RANK), BF16), VM),
        ],
        [], "out_forward", flops=2 * rows * width * width,
    )


def mlp_chunk(place, bundle, landing, normed, cot, inner_gl, outer_gl, drop_a, drop_b, sums, name):
    rows, width = normed.shape
    units = bundle.shapes[1][0]
    steps = units // PANEL
    first = sums is None

    def body(pr, land_refs, ins, outs, weights, sems, scratch):
        normed_ref, cot_ref, igl, ogl, da, db = ins[:6]
        drop_sum, e_sum, thin, g_gate, g_lift, g_drop = outs
        w_gl, w_d = weights
        landing = Landing(pr, bundle, land_refs, weights, sems)
        h_gl = dot_nt(normed_ref[...], igl[...]).astype(BF16)
        h_d = dot_nt(cot_ref[...], db[...]).astype(BF16)
        h_g, h_l = h_gl[:, :RANK], h_gl[:, RANK:]
        g_t, l_t, d_t = h_g.T, h_l.T, h_d.T
        for i in range(steps):
            landing.wait(lambda key: key[0] == 1 or key[1] < 2 * (i + 1) * PANEL)
            cols = slice(i * PANEL, (i + 1) * PANEL)
            both = pl.ds(2 * i * PANEL, 2 * PANEL)
            acts = dot(normed_ref[...], w_gl[:, both])
            gate = acts[:, :PANEL] + dot(h_g, ogl[:RANK, cols])
            lift = acts[:, PANEL:] + dot(h_l, ogl[RANK:, cols])
            a_grad = dot_nt(cot_ref[...], w_d[cols]) + dot(h_d, da[:, cols])
            sig = 1.0 / (1.0 + jnp.exp(-gate))
            silu = gate * sig
            active = (silu * lift).astype(BF16)
            gate_grad = (a_grad * lift * sig * (1.0 + gate * (1.0 - sig))).astype(BF16)
            lift_grad = (a_grad * silu).astype(BF16)
            grads = jnp.concatenate([gate_grad, lift_grad], axis=1)
            down = dot(active, w_d[cols])
            back = dot_nt(grads, w_gl[:, both])
            t0 = dot_nt(active, da[:, cols])
            t1 = dot_nt(gate_grad, ogl[:RANK, cols])
            t2 = dot_nt(lift_grad, ogl[RANK:, cols])
            if i == 0 and first:
                drop_sum[...] = down
                e_sum[...] = back
                thin[0], thin[1], thin[2] = t0, t1, t2
            elif i == 0:
                drop_sum[...] = ins[6][...] + down
                e_sum[...] = ins[7][...] + back
                thin[0], thin[1], thin[2] = ins[8][0] + t0, ins[8][1] + t1, ins[8][2] + t2
            else:
                drop_sum[...] += down
                e_sum[...] += back
                thin[0] += t0
                thin[1] += t1
                thin[2] += t2
            g_gate[:, cols] = dot(g_t, gate_grad)
            g_lift[:, cols] = dot(l_t, lift_grad)
            g_drop[:, cols] = dot(d_t, active)

    operands = [(normed, VM), (cot, VM), (inner_gl, VM), (outer_gl, VM), (drop_a, VM), (drop_b, VM)]
    if not first:
        operands += [(s, VM) for s in sums]
    return kernel_call(
        body, place, bundle, landing, operands,
        [
            (like((rows, width), F32), VM),
            (like((rows, width), F32), VM),
            (like((3, rows, RANK), F32), VM),
            (like((RANK, units), F32), VM),
            (like((RANK, units), F32), VM),
            (like((RANK, units), F32), VM),
        ],
        [], name, flops=12 * rows * width * units,
    )


def out_backward(place, bundle, landing, sums, middle, cot, gain, normed, attended, hidden, factors):
    rows, width = middle.shape
    heads = width // HEAD_DIM

    def body(pr, land_refs, ins, outs, weights, sems, scratch):
        drop_sum, e_sum, thin, middle_ref, cot_ref, gain_ref, normed_ref, att, hid, drop_b, igl, o_a, o_b = ins
        mixed, mid_grad, branch, out_heads, g_drop, g_gl, g_oa, g_ob = outs
        (w,) = weights
        landing = Landing(pr, bundle, land_refs, weights, sems)
        d_hid = thin[0].astype(BF16)
        gl_grad = jnp.concatenate([thin[1].astype(BF16), thin[2].astype(BF16)], axis=1)
        e_in = (e_sum[...] + dot(gl_grad, igl[...])) * gain_ref[...].astype(F32)
        mid = middle_ref[...]
        scale = lax.rsqrt(jnp.mean(mid * mid, axis=-1, keepdims=True) + EPSILON)
        n = mid * scale
        mean = jnp.mean(e_in * n, axis=-1, keepdims=True)
        mid_grad[...] = cot_ref[...].astype(F32) + scale * (e_in - n * mean)
        branch[...] = mid_grad[...].astype(BF16)
        hgrad = dot_nt(branch[...], o_b[...]).astype(BF16)
        landing.wait()
        wide = 8 * HEAD_DIM
        for i in range(heads // 8):
            part = slice(i * wide, (i + 1) * wide)
            grad = dot_nt(branch[...], w[part]) + dot(hgrad, o_a[:, part])
            for h in range(8):
                out_heads[8 * i + h] = grad[:, h * HEAD_DIM : (h + 1) * HEAD_DIM].astype(BF16)
        mixed[...] = (mid + drop_sum[...] + dot(d_hid, drop_b[...])).astype(BF16)
        g_drop[...] = dot(d_hid.T, cot_ref[...])
        g_gl[...] = dot(gl_grad.T, normed_ref[...])
        g_oa[...] = dot(hgrad.T, att[...])
        g_ob[...] = dot(hid[...].T, branch[...])

    thin_shape = (like((RANK, width), F32), VM)
    return kernel_call(
        body, place, bundle, landing,
        [(v, VM) for v in (*sums, middle, cot, gain, normed, attended, hidden, *factors)],
        [
            (like((rows, width), BF16), VM),
            (like((rows, width), F32), VM),
            (like((rows, width), BF16), VM),
            (like((heads, rows, HEAD_DIM), BF16), VM),
            thin_shape,
            (like((2 * RANK, width), F32), VM),
            thin_shape,
            thin_shape,
        ],
        [], "out_backward", flops=2 * rows * width * width,
    )


def qkv_backward(place, bundle, landing, dq, dk, dv, cos, sin, x, mid_grad, gain, normed, hidden, inner, outer):
    rows, width = x.shape
    total = bundle.shapes[0][1]
    kv = (total - width) // 2
    half = HEAD_DIM // 2
    block = rows // 2

    def body(pr, land_refs, ins, outs, weights, sems, scratch):
        dq_ref, dk_ref, dk_got, dv_ref, dv_got, cos_ref, sin_ref, x_ref, mg, gain_ref, nrm, hid, a, b = ins
        kept, back, g_inner, g_outer = outs
        (w,) = weights
        (g,) = scratch
        landing = Landing(pr, bundle, land_refs, weights, sems)
        for h in range(width // HEAD_DIM):
            g[:, h * HEAD_DIM : (h + 1) * HEAD_DIM] = dq_ref[h]
        for h in range(kv // HEAD_DIM):
            one = dk_ref[h] + dk_got[h].astype(F32)
            at = width + h * HEAD_DIM
            g[:, at : at + HEAD_DIM] = turn(one, cos_ref[...], -sin_ref[...], half).astype(BF16)
            at += kv
            g[:, at : at + HEAD_DIM] = (dv_ref[h] + dv_got[h].astype(F32)).astype(BF16)
        hgrad = dot_nt(g[...], b[...]).astype(BF16)
        g_inner[...] = dot(hgrad.T, nrm[...])
        g_outer[...] = dot(hid[...].T, g[...])
        landing.wait()
        e_in = (dot_nt(g[...], w[...]) + dot(hgrad, a[...])) * gain_ref[...].astype(F32)
        xf = x_ref[...].astype(F32)
        scale = lax.rsqrt(jnp.mean(xf * xf, axis=-1, keepdims=True) + EPSILON)
        n = xf * scale
        mean = jnp.mean(e_in * n, axis=-1, keepdims=True)
        result = mg[...] + scale * (e_in - n * mean)
        kept[...] = result[:block]
        back[...] = result[block:].astype(BF16)

    return kernel_call(
        body, place, bundle, landing,
        [(v, VM) for v in (dq, *dk, *dv, cos, sin, x, mid_grad, gain, normed, hidden, inner, outer)],
        [
            (like((block, width), F32), VM),
            (like((block, width), BF16), VM),
            (like((inner.shape[0], width), F32), VM),
            (like((inner.shape[0], total), F32), VM),
        ],
        [pltpu.VMEM((rows, total), BF16)], "qkv_backward", flops=2 * rows * width * total,
    )


def local(
    tokens,
    cotangent,
    prefix_len,
    adapter_index,
    gain_attn,
    gain_mlp,
    query_weight,
    key_weight,
    value_weight,
    output_weight,
    gate_weight,
    lift_weight,
    drop_weight,
    *factors,
):
    _, block, width = tokens.shape
    rep, shard = lax.axis_index("rep"), lax.axis_index("shard")
    chip, core = shard // 2, shard % 2
    member = rep % 4
    place = jnp.stack([shard, member, prefix_len[chip]]).astype(jnp.int32)
    rows = 2 * block
    kv_width = KV_HEADS * HEAD_DIM

    def pick(pair, index):
        return lax.dynamic_index_in_dim(pair, index, 0, keepdims=False)

    def swap_out(kept, back, dtype):
        back = to_diag(back.astype(BF16)).astype(dtype)
        return jnp.where(chip == 0, jnp.stack([kept, back]), jnp.stack([back, kept]))

    inners, outers = factors[0::2], factors[1::2]
    widths = [a.shape[0] for a in inners] + [b.shape[1] for b in outers]

    def pack(sequence):
        at = adapter_index[sequence] * RANK
        parts = [lax.dynamic_slice_in_dim(a, at, RANK, 1).T for a in inners]
        parts += [lax.dynamic_slice_in_dim(b, at, RANK, 0) for b in outers]
        return jnp.concatenate(parts, axis=1)

    mine = pack(chip)
    slot_two = to_chip(pack(1 - chip))
    slots = jnp.stack([mine, to_core(mine), slot_two, to_core(slot_two)])
    packed = jnp.take(slots, shard ^ jnp.arange(4), axis=0)
    factor_list, at = [], 0
    for w in widths:
        factor_list.append(
            packed[:, :, at : at + w].transpose(1, 0, 2).reshape(RANK, 4 * w)
        )
        at += w
    inner_t, outer = factor_list[:7], factor_list[7:]

    weights = (query_weight, key_weight, value_weight, output_weight, gate_weight, lift_weight, drop_weight)
    chunks = 4
    ff = gate_weight.shape[1]
    bundles = make_bundles(width, kv_width, ff, chunks, 4)
    near = [to_core(w) for w in weights]
    relay = Relay(place, weights, bundles)
    other_pair = lambda pr: 1 - pr[0] // 2
    relay.step()
    (tokens_back,), _ = relay.step([(tokens, other_pair)])
    relay.step()
    relay.step()
    (cot_back,), _ = relay.step([(cotangent, other_pair)])
    cot = jnp.concatenate([pick(cotangent, chip), cot_back], axis=0)
    for _ in range(len(bundles) - 2):
        relay.step()

    def landing(i):
        return landing_operands(bundles[i], weights, near, relay.far[i], relay.far_near[i])

    positions = jnp.concatenate(
        [shard * block + jnp.arange(block), (shard ^ 3) * block + jnp.arange(block)]
    )
    cos_table, sine_table = rotary_tables(positions.astype(F32), HEAD_DIM)
    cos_full = jnp.concatenate([cos_table, cos_table], axis=1)
    sin_full = jnp.concatenate([-sine_table, sine_table], axis=1)
    gain_one, gain_two = gain_attn[None], gain_mlp[None]

    inner_qkv = jnp.concatenate(inner_t[:3], axis=0)
    zeros = lambda w: jnp.zeros((RANK, w), BF16)
    outer_qkv = jnp.concatenate(
        [
            jnp.concatenate([outer[0], zeros(2 * kv_width)], axis=1),
            jnp.concatenate([zeros(width), outer[1], zeros(kv_width)], axis=1),
            jnp.concatenate([zeros(width + kv_width), outer[2]], axis=1),
        ],
        axis=0,
    )
    queries, k_own, v_own, hidden_qkv, normed_attn, x = qkv_forward(
        place, bundles[0], landing(0), pick(tokens, chip), tokens_back, gain_one,
        inner_qkv, outer_qkv, cos_full, sin_full,
    )
    k_near, v_near = to_core(k_own), to_core(v_own)
    heads_out, lse = attend(place, queries, k_own, k_near, v_own, v_near)
    middle, normed_mlp, attended, output_hidden = out_forward(
        place, bundles[1], landing(1), heads_out, x, gain_two, inner_t[3], outer[3]
    )

    def chunk_of(factor, i):
        return factor.reshape(factor.shape[0], 4, chunks, -1)[:, :, i].reshape(factor.shape[0], -1)

    def whole_of(parts):
        return jnp.stack([p.reshape(RANK, 4, -1) for p in parts], axis=2).reshape(RANK, -1)

    inner_gl = jnp.concatenate([inner_t[4], inner_t[5]], axis=0)
    outer_gl = jnp.concatenate([outer[4], outer[5]], axis=0)
    sums, grads_mlp = None, []
    for u in range(chunks):
        *sums, gg, gl, gd = mlp_chunk(
            place, bundles[2 + u], landing(2 + u), normed_mlp, cot, inner_gl,
            chunk_of(outer_gl, u), chunk_of(inner_t[6], u), outer[6], sums, f"mlp_{u}",
        )
        grads_mlp.append((gg, gl, gd))
    gate_outer_grad, lift_outer_grad, drop_inner_grad = map(whole_of, zip(*grads_mlp))
    mixed, middle_grad, branch_grad, grad_heads, drop_outer_grad, gl_inner, output_inner_grad, output_outer_grad = (
        out_backward(
            place, bundles[1], landing(1), sums, middle, cot, gain_two, normed_mlp, attended, output_hidden,
            (outer[6], inner_gl, inner_t[3], outer[3]),
        )
    )
    gate_inner_grad, lift_inner_grad = gl_inner[:RANK], gl_inner[RANK:]
    mixed = swap_out(mixed[:block], mixed[block:], BF16)

    column_owner = jnp.arange(ADAPTERS * RANK)

    def reduce_grads(inner_list, outer_list):
        parts = [v.reshape(RANK, 4, -1).transpose(1, 0, 2) for v in inner_list + outer_list]
        widths_here = [v.shape[2] for v in parts]
        everything = jnp.concatenate(parts, axis=2)
        keep = jnp.take(everything, core + jnp.array([0, 2]), axis=0)
        send = jnp.take(everything, (core ^ 1) + jnp.array([0, 2]), axis=0)
        summed = keep + to_core(send.astype(BF16)).astype(F32)
        own = pick(summed, chip).astype(BF16)
        other = to_chip(pick(summed, 1 - chip).astype(BF16))
        both = jnp.concatenate([own, other], axis=0)
        ids = jnp.stack([adapter_index[chip], adapter_index[1 - chip]])
        tag = jnp.broadcast_to(jnp.repeat(ids, RANK)[:, None], (2 * RANK, 128)).astype(BF16)
        gathered = lax.all_gather(jnp.concatenate([both, tag], axis=1), "rep", axis=0, tiled=True)
        owner = gathered[:, -1].astype(jnp.int32) * RANK + jnp.arange(gathered.shape[0]) % RANK
        choose = (column_owner[:, None] == owner[None, :]).astype(BF16)
        total = dot(choose, gathered[:, :-128])
        out, at = [], 0
        for w in widths_here:
            out.append(total[:, at : at + w])
            at += w
        n = len(inner_list)
        return [v.T for v in out[:n]], out[n:]

    inner_late, outer_late = reduce_grads(
        [output_inner_grad, gate_inner_grad, lift_inner_grad, drop_inner_grad],
        [output_outer_grad, gate_outer_grad, lift_outer_grad, drop_outer_grad],
    )

    dq, dk_own, dk_send, dv_own, dv_send = attend_back(
        place, queries, k_own, k_near, v_own, v_near, grad_heads, lse, cos_table.T, sine_table.T
    )
    input_kept, input_back, g_inner, g_outer = qkv_backward(
        place, bundles[0], landing(0), dq, (dk_own, to_core(dk_send)), (dv_own, to_core(dv_send)),
        cos_full, sin_full, x, middle_grad, gain_one, normed_attn, hidden_qkv, inner_qkv, outer_qkv,
    )
    input_grad = swap_out(input_kept, input_back, F32)
    stops = (0, width, width + kv_width, width + 2 * kv_width)
    inner_first, outer_first = reduce_grads(
        [g_inner[i * RANK : (i + 1) * RANK] for i in range(3)],
        [g_outer[i * RANK : (i + 1) * RANK, stops[i] : stops[i + 1]] for i in range(3)],
    )
    inner_out = inner_first + inner_late
    outer_out = outer_first + outer_late
    grads = [g for pair in zip(inner_out, outer_out) for g in pair]
    return (mixed, input_grad, *grads)


def solution(mesh):
    token_place = P("rep", "shard", None)
    row, col = P("shard", None), P(None, "shard")
    return jax.shard_map(
        local,
        mesh=mesh,
        in_specs=(token_place, token_place, P("rep"), P("rep"), P(), P()) + (row,) * 7 + (row, col) * 7,
        out_specs=(token_place, token_place) + (row, col) * 7,
        check_vma=False,
    )
```

```python
import functools
import math
from typing import NamedTuple

import jax
import jax.numpy as jnp
from jax import lax
from jax.experimental import pallas as pl
from jax.experimental.pallas import tpu as pltpu
from jax.sharding import PartitionSpec as P

HEADS = 16
KV_HEADS = 8
HEAD_DIM = 96
RANK = 16
ADAPTERS = 8
EPSILON = 1e-05
ROPE_BASE = 100000.0
MASKED_SCORE = -1e30
AXES = ("rep", "shard")
F32 = jnp.float32
BF16 = jnp.bfloat16


def move(value, target):
    reps, shards = lax.axis_size("rep"), lax.axis_size("shard")
    pairs = []
    for r in range(reps):
        for s in range(shards):
            r2, s2 = target(r, s)
            pairs.append((r * shards + s, r2 * shards + s2))
    return lax.ppermute(value, AXES, pairs)


def to_core(value):
    return move(value, lambda r, s: (r, s ^ 1))


def to_chip(value):
    return move(value, lambda r, s: (r, s ^ 2))


def to_diag(value):
    return move(value, lambda r, s: (r, s ^ 3))


def to_y(value):
    return move(value, lambda r, s: (r ^ 1, s))


def to_z(value):
    return move(value, lambda r, s: (r ^ 2, s))


PANEL = 512
LANES = 128


class Piece(NamedTuple):
    parts: tuple
    row: int
    rows: int
    target: int
    block: int
    to_row: int
    to_col: int


class Bundle(NamedTuple):
    first: tuple
    second: tuple
    shapes: tuple


def quarter_rows(pieces):
    return sum(p.rows for p in pieces) // 4


def make_bundles(width, kv_width, ff, chunks, shards):
    rows, drop_rows = width // shards, ff // shards // chunks
    panels = width // PANEL
    first = tuple(Piece(((0, c, PANEL),), 0, rows, 0, rows, 0, c) for c in range(0, width, PANEL))
    second = []
    for c in range(0, 2 * kv_width, PANEL):
        parts, at = [], c
        while at < c + PANEL:
            source = 1 if at < kv_width else 2
            base = (source - 1) * kv_width
            stop = min(c + PANEL, base + kv_width)
            parts.append((source, at - base, stop - at))
            at = stop
        second.append(Piece(tuple(parts), 0, rows, 0, rows, 0, width + c))
    found = [Bundle(first, tuple(second), ((width, width + 2 * kv_width),))]

    def halves(source, row, height, target, block):
        return [
            tuple(
                Piece(((source, i * PANEL, PANEL),), row + h * height // 2, height // 2, target, block,
                      h * height // 2, i * PANEL)
                for i in range(panels)
            )
            for h in range(2)
        ]

    top, bottom = halves(3, 0, rows, 0, rows)
    found.append(Bundle(top, bottom, ((width, width),)))
    part = ff // shards // chunks
    for u in range(chunks):
        sides = []
        for j in range(2):
            side = []
            for c in range(0, shards * part, PANEL):
                parts = tuple(
                    (4 + j, t * (ff // shards) + u * part, part)
                    for t in range(c // part, (c + PANEL) // part)
                )
                side.append(Piece(parts, 0, rows, 0, rows, 0, 2 * c + j * PANEL))
            sides.append(tuple(side))
        top, bottom = halves(6, u * drop_rows, drop_rows, 1, drop_rows)
        cols = shards * part
        found.append(
            Bundle(sides[0] + top, sides[1] + bottom, ((width, 2 * cols), (cols, width)))
        )
    return found


def run_copies(copies, sems):
    started = []
    for i, (src, dst) in enumerate(copies):
        started.append(pltpu.make_async_copy(src, dst, sems.at[i]))
        started[-1].start()
    for c in started:
        c.wait()


def work(microseconds):
    return pl.CostEstimate(flops=int(microseconds * 1.1e9), bytes_accessed=2**20, transcendentals=0)


def pack(place, jobs, operands, out_shapes, name):
    count = []

    def kernel(place_ref, *refs):
        ins, outs, sems = refs[: len(operands)], refs[len(operands) : -1], refs[-1]
        run_copies(jobs(place_ref, ins, outs), sems)

    class Fake:
        def __init__(self):
            self.at = self

        def __getitem__(self, _):
            return self

    count = len(jobs(None, [Fake()] * len(operands), [Fake()] * len(out_shapes)))
    return pl.pallas_call(
        kernel,
        out_shape=[jax.ShapeDtypeStruct(sh, BF16) for sh in out_shapes],
        grid_spec=pltpu.PrefetchScalarGridSpec(
            num_scalar_prefetch=1,
            grid=(1,),
            in_specs=[pl.BlockSpec(memory_space=pltpu.HBM)] * len(operands),
            out_specs=[pl.BlockSpec(memory_space=pltpu.VMEM)] * len(out_shapes),
            scratch_shapes=[pltpu.SemaphoreType.DMA((count,))],
        ),
        compiler_params=pltpu.CompilerParams(vmem_limit_bytes=64 * 2**20),
        cost_estimate=work(4),
        name=name,
    )(place, *operands)


def quarter_start(place_ref, flip, rows):
    if place_ref is None:
        return 0
    return pl.multiple_of((place_ref[1] ^ flip) * rows, 16)


class Relay:
    def __init__(self, place, weights, bundles):
        self.place, self.weights, self.bundles = place, weights, bundles
        self.direct, self.once, self.twice = {}, {}, {}
        self.here, self.there = {}, {}
        self.tick = 0

    def step(self, extra=(), ties=()):
        t, bundles = self.tick, self.bundles
        self.tick += 1
        operands, shapes, kinds = [], [], []

        def operand(array):
            for i, o in enumerate(operands):
                if o is array:
                    return i
            operands.append(array)
            return len(operands) - 1

        plans = []

        def out(kind, rows, cols=PANEL):
            shapes.append((rows, cols))
            kinds.append(kind)
            return len(shapes) - 1

        if t < len(bundles):
            b = bundles[t]
            o = out("x", quarter_rows(b.first + b.second))
            used = [(operand(self.weights[q[0]]), q, p) for p in b.first + b.second for q in p.parts]

            def plan_x(pr, ins, outs, o=o, used=used):
                copies, at, col = [], 0, 0
                for i, (_, c, n), p in used:
                    q = p.rows // 4
                    rows = pl.ds(pl.multiple_of(p.row + quarter_start(pr, 0, q), 16), q)
                    copies.append((ins[i].at[rows, pl.ds(c, n)],
                                   outs[o].at[pl.ds(at, q), pl.ds(col, n)]))
                    col += n
                    if col == PANEL:
                        at, col = at + q, 0
                return copies

            plans.append(plan_x)
        y_parts, z_parts = [], []
        b1, b2, b3 = t - 1, t - 2, t - 3
        if 0 <= b1 < len(bundles):
            qa, qb = quarter_rows(bundles[b1].first), quarter_rows(bundles[b1].second)
            y_parts.append(("first", b1, [(self.direct[b1], 0, qa)]))
            z_parts.append(("first", b1, [(self.direct[b1], qa, qb)]))
        if 0 <= b2 < len(bundles):
            qa, qb = quarter_rows(bundles[b2].first), quarter_rows(bundles[b2].second)
            (ya, yo), (za, zo) = self.once[b2]
            y_parts.append(("second", b2, [(self.direct[b2], qa, qb), (za, zo, qb)]))
            z_parts.append(("second", b2, [(self.direct[b2], 0, qa), (ya, yo, qa)]))
        for kind, parts in (("y", y_parts), ("z", z_parts)):
            if not parts:
                continue
            total = sum(n for _, _, l in parts for _, _, n in l)
            o = out(kind, total)
            flat = [(operand(a), r, n) for _, _, l in parts for a, r, n in l]

            def plan_n(pr, ins, outs, o=o, flat=flat):
                copies, at = [], 0
                for i, r, n in flat:
                    copies.append((ins[i].at[pl.ds(r, n)], outs[o].at[pl.ds(at, n)]))
                    at += n
                return copies

            plans.append(plan_n)
        if 0 <= b3 < len(bundles):
            b = bundles[b3]
            total = 4 * quarter_rows(b.first + b.second)
            o = out("c", 2 * total)
            used = [(operand(self.weights[q[0]]), q, p) for p in b.first + b.second for q in p.parts]
            qa = quarter_rows(b.first)
            qb = quarter_rows(b.second)
            (ya, yo), (za, zo) = self.once[b3]
            (ys, yso), (zs, zso) = self.twice[b3]
            d = operand(self.direct[b3])
            sides = [
                (b.first, [(0, d, 0), (1, operand(ya), yo), (2, operand(zs), zso), (3, operand(zs), zso + qa)]),
                (b.second, [(0, d, qa), (2, operand(za), zo), (1, operand(ys), yso), (3, operand(ys), yso + qb)]),
            ]

            def plan_c(pr, ins, outs, o=o, sides=sides, used=used, total=total):
                copies, base, at, col = [], total, 0, 0
                for i, (_, c, n), p in used:
                    copies.append((ins[i].at[pl.ds(p.row, p.rows), pl.ds(c, n)],
                                   outs[o].at[pl.ds(at, p.rows), pl.ds(col, n)]))
                    col += n
                    if col == PANEL:
                        at, col = at + p.rows, 0
                for pieces, quarters in sides:
                    at = 0
                    for p in pieces:
                        q = p.rows // 4
                        for flip, i, r in quarters:
                            to = pl.multiple_of(base + quarter_start(pr, flip, q), 16)
                            copies.append((ins[i].at[pl.ds(r + at, q)], outs[o].at[pl.ds(to, q)]))
                        at += q
                        base += p.rows
                return copies

            plans.append(plan_c)
        for array, start, count in extra:
            o = out("d", count, array.shape[2])
            i = operand(array)

            def plan_d(pr, ins, outs, o=o, i=i, start=start, count=count):
                which = 0 if pr is None else 1 - pr[0] // 2
                return [(ins[i].at[which, pl.ds(start, count)], outs[o])]

            plans.append(plan_d)
        for tie in ties:
            operand(tie)

        def jobs(pr, ins, outs):
            return [c for plan in plans for c in plan(pr, ins, outs)]

        bufs = pack(self.place, jobs, operands, shapes, f"pack_{t}")
        sent = []
        for kind, buf in zip(kinds, bufs):
            if kind == "x":
                self.direct[t] = to_chip(buf)
            elif kind == "c":
                self.here[b3], self.there[b3] = buf, to_core(buf)
            elif kind == "d":
                sent.append(to_diag(buf))
            else:
                got = (to_y if kind == "y" else to_z)(buf)
                at = 0
                for stage, bi, l in y_parts if kind == "y" else z_parts:
                    store = self.once if stage == "first" else self.twice
                    pair = store.setdefault(bi, [None, None])
                    pair[0 if kind == "y" else 1] = (got, at)
                    at += sum(n for _, _, n in l)
        return sent, bufs


def land_copies(place_ref, bundle, own, here, there, targets):
    copies = []
    shard = 0 if place_ref is None else place_ref[0]
    pieces = bundle.first + bundle.second
    total = sum(p.rows for p in pieces)
    for slot, (ref, base) in enumerate(((None, 0), (there, 0), (here, total), (there, total))):
        for p in pieces:
            to = (shard ^ slot) * p.block + p.to_row
            to = pl.ds(pl.multiple_of(to, 16), p.rows)
            dst = targets[p.target]
            key = (p.target, p.to_col)
            if slot == 0:
                col = p.to_col
                for source, c, n in p.parts:
                    copies.append((own[source].at[pl.ds(p.row, p.rows), pl.ds(c, n)],
                                   dst.at[to, pl.ds(col, n)], key))
                    col += n
            else:
                copies.append((ref.at[pl.ds(base, p.rows)], dst.at[to, pl.ds(p.to_col, PANEL)], key))
            base += p.rows
    return copies


def sources_of(bundle):
    return sorted({q[0] for p in bundle.first + bundle.second for q in p.parts})


def rotary_tables(positions, head_dim):
    half_dim = head_dim // 2
    freq_index = jnp.arange(half_dim).astype(F32)
    frequency = jnp.exp(freq_index * (-2.0 * math.log(ROPE_BASE) / head_dim))
    angles = positions[:, None] * frequency[None, :]
    return jnp.cos(angles), jnp.sin(angles)


def dot(left, right):
    return jnp.dot(left, right, preferred_element_type=F32)


def dot_nt(left, right):
    return lax.dot_general(left, right, (((1,), (1,)), ((), ())), preferred_element_type=F32)


def dot_tn(left, right):
    return lax.dot_general(left, right, (((0,), (0,)), ((), ())), preferred_element_type=F32)


LOG2E = 1.4426950408889634


def last_visible(place_ref, low, lanes, block):
    shard, prefix = place_ref[0], place_ref[2]
    low_block = (shard ^ (shard // 2)) & 1
    at = low_block if low else 3 - low_block
    position = at * block + lax.broadcasted_iota(jnp.int32, (1, lanes), 1) % block
    return jnp.maximum(position + 1, prefix)


def query_start(place_ref, low, block):
    chip = place_ref[0] // 2
    return pl.multiple_of((chip if low else 1 - chip) * block, block)


def natural_rows(place_ref, own, near, into, block):
    shard = place_ref[0]
    for slot, value in (
        (0, own[0, :block]),
        (3, own[0, block:]),
        (1, near[0, :block]),
        (2, near[0, block:]),
    ):
        into[pl.ds(pl.multiple_of((shard ^ slot) * block, block), block)] = value


def hide(scores, limit, first_key):
    keys = first_key + lax.broadcasted_iota(jnp.int32, scores.shape, 0)
    return jnp.where(keys < limit, scores, MASKED_SCORE)


def masked_by_part(low, scores, limit, block):
    if low:
        return hide(scores, limit, 0)
    half = 2 * block
    return jnp.concatenate([scores[:half], hide(scores[half:], limit, half)], axis=0)


def attend_kernel(place, q, k_own, k_near, v_own, v_near, out, lse, keys, values, *, scale):
    block = q.shape[1] // 2
    group = q.shape[0]
    natural_rows(place, k_own, k_near, keys, block)
    natural_rows(place, v_own, v_near, values, block)
    values_t = values[...].T
    for part, low in enumerate((True, False)):
        count = (2 if low else 4) * block
        rows = pl.ds(query_start(place, low, block), block)
        query = jnp.concatenate([q[j, rows] for j in range(group)], axis=0)
        limit = last_visible(place, low, group * block, block)
        scores = masked_by_part(low, dot_nt(keys[:count], query), limit, block)
        top = jnp.max(scores, axis=0, keepdims=True)
        base = scale * LOG2E
        expo = jnp.exp2(scores * base - top * base)
        total = jnp.sum(expo, axis=0, keepdims=True)
        lse[0, part] = (top * base + jnp.log2(total))[0]
        result = dot(values_t[:, :count], expo.astype(BF16)) / total
        result = result.T.astype(BF16)
        for j in range(group):
            out[j, rows] = result[j * block : (j + 1) * block]


def attend(place, queries, kv_own, kv_near):
    heads, rows, dim = queries.shape
    kv_heads = kv_own.shape[0] // 2
    group = heads // kv_heads
    q_spec = pl.BlockSpec((group, rows, dim), lambda g, p: (g, 0, 0))
    kv_spec = pl.BlockSpec((1, rows, dim), lambda g, p: (g, 0, 0))
    v_spec = pl.BlockSpec((1, rows, dim), lambda g, p: (g + kv_heads, 0, 0))
    lse_shape = (kv_heads, 2, group * rows // 2)
    return pl.pallas_call(
        functools.partial(attend_kernel, scale=HEAD_DIM ** (-0.5)),
        out_shape=[
            jax.ShapeDtypeStruct(queries.shape, BF16),
            jax.ShapeDtypeStruct(lse_shape, F32),
        ],
        grid_spec=pltpu.PrefetchScalarGridSpec(
            num_scalar_prefetch=1,
            grid=(kv_heads,),
            in_specs=[q_spec, kv_spec, kv_spec, v_spec, v_spec],
            out_specs=[q_spec, pl.BlockSpec((1, *lse_shape[1:]), lambda g, p: (g, 0, 0))],
            scratch_shapes=[pltpu.VMEM((2 * rows, dim), BF16)] * 2,
        ),
        compiler_params=pltpu.CompilerParams(vmem_limit_bytes=64 * 2**20),
        cost_estimate=work(16),
        name="attend",
    )(place, queries, kv_own, kv_near, kv_own, kv_near)


def attend_back_kernel(
    place, q, k_own, k_near, v_own, v_near, grad, lse, cos_t, sin_t, *rest, scale
):
    dq, own_out, send_out, keys, values, dk, dv = rest[-7:]
    block = q.shape[1] // 2
    group = q.shape[0]
    half = HEAD_DIM // 2
    natural_rows(place, k_own, k_near, keys, block)
    natural_rows(place, v_own, v_near, values, block)
    keys_t = keys[...].T
    for part, low in ((1, False), (0, True)):
        count = (2 if low else 4) * block
        start = query_start(place, low, block)
        rows = pl.ds(start, block)
        query = jnp.concatenate([q[j, rows] for j in range(group)], axis=0)
        out_grad = jnp.concatenate([grad[j, rows] for j in range(group)], axis=0)
        limit = last_visible(place, low, group * block, block)
        scores = masked_by_part(low, dot_nt(keys[:count], query), limit, block)
        probs = jnp.exp2(scores * (scale * LOG2E) - lse[0, part][None])
        probs_grad = dot_nt(values[:count], out_grad)
        mean = jnp.sum(probs * probs_grad, axis=0, keepdims=True)
        score_grad = (probs * (probs_grad - mean)).astype(BF16)
        v_part = dot(probs.astype(BF16), out_grad)
        k_part = dot(score_grad, query) * scale
        if low:
            dk[:count] += k_part
            dv[:count] += v_part
        else:
            dk[...] = k_part
            dv[...] = v_part
        turned = dot(keys_t[:, :count], score_grad) * scale
        cos = jnp.concatenate([cos_t[:, rows]] * group, axis=1)
        sin = jnp.concatenate([sin_t[:, rows]] * group, axis=1)
        u, w = turned[:half], turned[half : 2 * half]
        pad = jnp.zeros((q.shape[2] - 2 * half, u.shape[1]), F32)
        turned = jnp.concatenate([u * cos + w * sin, w * cos - u * sin, pad], axis=0)
        turned = turned.T.astype(BF16)
        for j in range(group):
            dq[j, rows] = turned[j * block : (j + 1) * block]
    shard = place[0]
    for slot, at, own in ((0, 0, True), (3, 1, True), (1, 0, False), (2, 1, False)):
        rows = pl.ds(pl.multiple_of((shard ^ slot) * block, block), block)
        to = slice(at * block, (at + 1) * block)
        out = own_out if own else send_out
        out[0, 0, to] = dk[rows].astype(out.dtype)
        out[1, 0, to] = dv[rows].astype(out.dtype)


def attend_back(place, queries, kv_own, kv_near, grad, lse, cos_t, sin_t, ties=()):
    heads, rows, dim = queries.shape
    kv_heads = kv_own.shape[0] // 2
    group = heads // kv_heads
    q_spec = pl.BlockSpec((group, rows, dim), lambda g, p: (g, 0, 0))
    kv_spec = pl.BlockSpec((1, rows, dim), lambda g, p: (g, 0, 0))
    v_spec = pl.BlockSpec((1, rows, dim), lambda g, p: (g + kv_heads, 0, 0))
    whole = pl.BlockSpec(cos_t.shape, lambda g, p: (0, 0))
    return pl.pallas_call(
        functools.partial(attend_back_kernel, scale=HEAD_DIM ** (-0.5)),
        out_shape=[
            jax.ShapeDtypeStruct(queries.shape, BF16),
            jax.ShapeDtypeStruct((2, kv_heads, rows, dim), F32),
            jax.ShapeDtypeStruct((2, kv_heads, rows, dim), BF16),
        ],
        grid_spec=pltpu.PrefetchScalarGridSpec(
            num_scalar_prefetch=1,
            grid=(kv_heads,),
            in_specs=[q_spec, kv_spec, kv_spec, v_spec, v_spec]
            + [q_spec, pl.BlockSpec((1, *lse.shape[1:]), lambda g, p: (g, 0, 0)), whole, whole]
            + [pl.BlockSpec(memory_space=pltpu.HBM)] * len(ties),
            out_specs=[q_spec] + [pl.BlockSpec((2, 1, rows, dim), lambda g, p: (0, g, 0, 0))] * 2,
            scratch_shapes=[pltpu.VMEM((2 * rows, dim), BF16)] * 2
            + [pltpu.VMEM((2 * rows, dim), F32)] * 2,
        ),
        compiler_params=pltpu.CompilerParams(vmem_limit_bytes=64 * 2**20),
        cost_estimate=work(24),
        name="attend_back",
    )(place, queries, kv_own, kv_near, kv_own, kv_near, grad, lse, cos_t, sin_t, *ties)


class Landing:
    def __init__(self, place, bundle, refs, targets, sems):
        used = sources_of(bundle)
        n = len(used)
        own = dict(zip(used, refs[:n]))
        listed = land_copies(place, bundle, own, refs[n], refs[n + 1], targets)
        self.copies = [
            (key, pltpu.make_async_copy(src, dst, sems.at[i])) for i, (src, dst, key) in enumerate(listed)
        ]
        self.copies.sort(key=lambda c: c[0])
        for _, c in self.copies:
            c.start()

    def wait(self, wanted=None):
        left = []
        for key, c in self.copies:
            if wanted is None or wanted(key):
                c.wait()
            else:
                left.append((key, c))
        self.copies = left


def landing_operands(bundle, weights, here, there):
    return [weights[i] for i in sources_of(bundle)] + [here, there]


def landing_count(bundle):
    return sum(len(p.parts) + 3 for p in bundle.first + bundle.second)


NO_BUNDLE = Bundle((), (), ())


def kernel_call(body, place, bundle, landing, operands, outs, scratch, name, time=3, ties=()):
    operands = [*operands, *((t, HB) for t in ties)]
    n_land, n_in, n_out, n_w = len(landing), len(operands), len(outs), len(bundle.shapes)

    def kernel(place_ref, *refs):
        land, refs = refs[:n_land], refs[n_land:]
        ins, refs = refs[: n_in - len(ties)], refs[n_in:]
        out, refs = refs[:n_out], refs[n_out:]
        body(place_ref, land, ins, out, refs[:n_w], refs[n_w], refs[n_w + 1 :])

    def spec(where):
        return where if isinstance(where, pl.BlockSpec) else pl.BlockSpec(memory_space=where)

    return pl.pallas_call(
        kernel,
        out_shape=[o for o, _ in outs],
        grid_spec=pltpu.PrefetchScalarGridSpec(
            num_scalar_prefetch=1,
            grid=(1,),
            in_specs=[spec(pltpu.HBM)] * n_land + [spec(w) for _, w in operands],
            out_specs=[spec(w) for _, w in outs],
            scratch_shapes=[pltpu.VMEM(sh, BF16) for sh in bundle.shapes]
            + [pltpu.SemaphoreType.DMA((max(landing_count(bundle), 1),))]
            + list(scratch),
        ),
        compiler_params=pltpu.CompilerParams(vmem_limit_bytes=64 * 2**20),
        cost_estimate=work(time),
        name=name,
    )(place, *landing, *[a for a, _ in operands])


VM = pltpu.VMEM
HB = pltpu.HBM


def like(shape, dtype):
    return jax.ShapeDtypeStruct(shape, dtype)


def turn(value, cos_full, sin_signed, half):
    swapped = jnp.concatenate([value[:, half:], value[:, :half]], axis=1)
    return value * cos_full + swapped * sin_signed


def padded(value):
    return jnp.concatenate([value, jnp.zeros((value.shape[0], LANES - HEAD_DIM), value.dtype)], axis=1)


def one_of_pair(block, width):
    return pl.BlockSpec((None, block, width), lambda i, p: (p[0] // 2, 0, 0))


def qkv_forward(place, bundle, landing, tokens, tokens_back, gain, inner, outer, cos, sin, ties):
    _, block, width = tokens.shape
    rows = 2 * block
    total = bundle.shapes[0][1]
    kv = (total - width) // 2
    wide = 8 * HEAD_DIM
    half = HEAD_DIM // 2

    def body(pr, land_refs, ins, outs, weights, sems, scratch):
        kept, *backs, gain_ref, inner_ref, outer_ref, cos_ref, sin_ref = ins
        q, kv_ref, hidden_ref, normed_ref, x_ref = outs
        (w,) = weights
        landing = Landing(pr, bundle, land_refs, weights, sems)
        x_ref[:block] = kept[...]
        at = block
        for back in backs:
            x_ref[at : at + back.shape[0]] = back[...]
            at += back.shape[0]
        x = x_ref[...].astype(F32)
        scale = lax.rsqrt(jnp.mean(x * x, axis=-1, keepdims=True) + EPSILON)
        normed_ref[...] = (x * scale * gain_ref[...].astype(F32)).astype(BF16)
        hidden_ref[...] = dot_nt(normed_ref[...], inner_ref[...]).astype(BF16)

        def columns(at):
            cols = pl.ds(at, wide)
            return dot(normed_ref[...], w[:, cols]) + dot(hidden_ref[...], outer_ref[:, cols])

        landing.wait(lambda key: key[1] < width)
        for i in range(width // wide):
            acc = columns(i * wide)
            for h in range(8):
                one = acc[:, h * HEAD_DIM : (h + 1) * HEAD_DIM]
                q[8 * i + h] = padded(turn(one, cos_ref[...], sin_ref[...], half)).astype(BF16)
        landing.wait()
        acc = columns(width)
        for h in range(8):
            one = acc[:, h * HEAD_DIM : (h + 1) * HEAD_DIM]
            kv_ref[h] = padded(turn(one, cos_ref[...], sin_ref[...], half)).astype(BF16)
        acc = columns(width + kv)
        for h in range(8):
            kv_ref[8 + h] = padded(acc[:, h * HEAD_DIM : (h + 1) * HEAD_DIM]).astype(BF16)

    heads = width // HEAD_DIM
    return kernel_call(
        body, place, bundle, landing,
        [(tokens, one_of_pair(block, width)), *((t, VM) for t in tokens_back), (gain, VM), (inner, VM), (outer, VM), (cos, VM), (sin, VM)],
        [
            (like((heads, rows, LANES), BF16), VM),
            (like((2 * kv // HEAD_DIM, rows, LANES), BF16), VM),
            (like((rows, inner.shape[0]), BF16), VM),
            (like((rows, width), BF16), VM),
            (like((rows, width), BF16), VM),
        ],
        [], "qkv_forward", time=16, ties=ties,
    )


def out_forward(place, bundle, landing, heads_out, x, gain, inner, outer, cot, cot_back, inner_gl, drop_b):
    rows, width = x.shape
    heads = heads_out.shape[0]

    def body(pr, land_refs, ins, outs, weights, sems, scratch):
        heads_ref, x_ref, gain_ref, inner_ref, outer_ref, cot_kept, *cot_got, igl, db = ins
        middle, normed, attended, hidden, cot_ref, h_gl, h_d = outs
        landing = Landing(pr, bundle, land_refs, weights, sems)
        for h in range(heads):
            attended[:, h * HEAD_DIM : (h + 1) * HEAD_DIM] = heads_ref[h, :, :HEAD_DIM]
        hidden[...] = dot_nt(attended[...], inner_ref[...]).astype(BF16)
        cot_ref[: rows // 2] = cot_kept[...]
        at = rows // 2
        for got in cot_got:
            cot_ref[at : at + got.shape[0]] = got[...]
            at += got.shape[0]
        h_d[...] = dot_nt(cot_ref[...], db[...]).astype(BF16)
        landing.wait()
        wide = width // 2
        squares = jnp.zeros((rows, 1), F32)
        for i in range(2):
            cols = pl.ds(i * wide, wide)
            branch = dot(attended[...], weights[0][:, cols]) + dot(hidden[...], outer_ref[:, cols])
            value = x_ref[:, cols].astype(F32) + branch
            middle[:, cols] = value
            squares += jnp.sum(value * value, axis=-1, keepdims=True)
        scale = lax.rsqrt(squares / width + EPSILON)
        normed[...] = (middle[...] * scale * gain_ref[...].astype(F32)).astype(BF16)
        h_gl[...] = dot_nt(normed[...], igl[...]).astype(BF16)

    return kernel_call(
        body, place, bundle, landing,
        [(heads_out, VM), (x, VM), (gain, VM), (inner, VM), (outer, VM),
         (cot, one_of_pair(rows // 2, width)), *((c, VM) for c in cot_back), (inner_gl, VM), (drop_b, VM)],
        [
            (like((rows, width), F32), VM),
            (like((rows, width), BF16), VM),
            (like((rows, width), BF16), VM),
            (like((rows, RANK), BF16), VM),
            (like((rows, width), BF16), VM),
            (like((rows, 2 * RANK), BF16), VM),
            (like((rows, RANK), BF16), VM),
        ],
        [], "out_forward", time=13,
    )


def mlp_chunk(place, bundle, landing, normed, cot, hidden_gl, hidden_d, outer_gl, drop_a, chunk, sums, name):
    rows, width = normed.shape
    units = bundle.shapes[1][0]
    steps = units // PANEL
    first = sums is None
    part = units // 4

    def body(pr, land_refs, ins, outs, weights, sems, scratch):
        normed_ref, cot_ref, hgl_ref, hd_ref, ogl, da = ins[:6]
        drop_sum, e_sum, thin, packed = outs
        w_gl, w_d = weights
        landing = Landing(pr, bundle, land_refs, weights, sems)
        h_d = hd_ref[...]
        h_g, h_l = hgl_ref[:, :RANK], hgl_ref[:, RANK:]
        g_t, l_t, d_t = h_g.T, h_l.T, h_d.T
        for i in range(steps):
            landing.wait(lambda key: key[0] == 1 or key[1] < 2 * (i + 1) * PANEL)
            cols = slice(i * PANEL, (i + 1) * PANEL)
            both = pl.ds(2 * i * PANEL, 2 * PANEL)
            acts = dot(normed_ref[...], w_gl[:, both])
            gate = acts[:, :PANEL] + dot(h_g, ogl[:RANK, cols])
            lift = acts[:, PANEL:] + dot(h_l, ogl[RANK:, cols])
            a_grad = dot_nt(cot_ref[...], w_d[cols]) + dot(h_d, da[:, cols])
            sig = 1.0 / (1.0 + jnp.exp(-gate))
            silu = gate * sig
            active = (silu * lift).astype(BF16)
            gate_grad = (a_grad * lift * sig * (1.0 + gate * (1.0 - sig))).astype(BF16)
            lift_grad = (a_grad * silu).astype(BF16)
            grads = jnp.concatenate([gate_grad, lift_grad], axis=1)
            down = dot(active, w_d[cols])
            back = dot_nt(grads, w_gl[:, both])
            t0 = dot_nt(active, da[:, cols])
            t1 = dot_nt(gate_grad, ogl[:RANK, cols])
            t2 = dot_nt(lift_grad, ogl[RANK:, cols])
            if i == 0 and first:
                drop_sum[...] = down
                e_sum[...] = back
                thin[0], thin[1], thin[2] = t0, t1, t2
            elif i == 0:
                drop_sum[...] = ins[6][...] + down
                e_sum[...] = ins[7][...] + back
                thin[0], thin[1], thin[2] = ins[8][0] + t0, ins[8][1] + t1, ins[8][2] + t2
            else:
                drop_sum[...] += down
                e_sum[...] += back
                thin[0] += t0
                thin[1] += t1
                thin[2] += t2
            per = PANEL // part
            for j, g in enumerate((dot(g_t, gate_grad), dot(l_t, lift_grad), dot(d_t, active))):
                for o in range(per):
                    packed[i * per + o, :, j * part : (j + 1) * part] = g[:, o * part : (o + 1) * part]

    at_chunk = lambda i, p: (chunk, 0, 0)
    operands = [
        (normed, VM), (cot, VM), (hidden_gl, VM), (hidden_d, VM),
        (outer_gl, pl.BlockSpec((None, *outer_gl.shape[1:]), at_chunk)),
        (drop_a, pl.BlockSpec((None, *drop_a.shape[1:]), at_chunk)),
    ]
    if not first:
        operands += [(s, VM) for s in sums]
    return kernel_call(
        body, place, bundle, landing, operands,
        [
            (like((rows, width), F32), VM),
            (like((rows, width), F32), VM),
            (like((3, rows, RANK), F32), VM),
            (like((4, RANK, 3 * part), F32), VM),
        ],
        [], name, time=20,
    )


def split_by_core(place_ref, whole, keep, send):
    core = place_ref[0] % 2
    for j in range(2):
        keep[j] = whole[core + 2 * j]
        send[j] = whole[1 - core + 2 * j].astype(BF16)


def out_backward(place, bundle, landing, sums, packs, middle, cot, gain, normed, attended, hidden, factors):
    rows, width = middle.shape
    heads = width // HEAD_DIM

    def body(pr, land_refs, ins, outs, weights, sems, scratch):
        chunk_refs, ins = ins[: len(packs)], ins[len(packs) :]
        drop_sum, e_sum, thin, middle_ref, cot_ref, gain_ref, normed_ref, att, hid, drop_b, igl, o_a, o_b = ins
        mixed_kept, mixed_back, mid_grad, out_heads, keep, send = outs
        (w,) = weights
        branch, whole = scratch
        landing = Landing(pr, bundle, land_refs, weights, sems)
        d_hid = thin[0].astype(BF16)
        gl_grad = jnp.concatenate([thin[1].astype(BF16), thin[2].astype(BF16)], axis=1)
        e_in = (e_sum[...] + dot(gl_grad, igl[...])) * gain_ref[...].astype(F32)
        mid = middle_ref[...]
        scale = lax.rsqrt(jnp.mean(mid * mid, axis=-1, keepdims=True) + EPSILON)
        n = mid * scale
        mean = jnp.mean(e_in * n, axis=-1, keepdims=True)
        mid_grad[...] = cot_ref[...].astype(F32) + scale * (e_in - n * mean)
        branch[...] = mid_grad[...].astype(BF16)
        hgrad = dot_nt(branch[...], o_b[...]).astype(BF16)
        landing.wait()
        wide = 8 * HEAD_DIM
        for i in range(heads // 8):
            part = slice(i * wide, (i + 1) * wide)
            grad = dot_nt(branch[...], w[part]) + dot(hgrad, o_a[:, part])
            for h in range(8):
                out_heads[8 * i + h] = padded(grad[:, h * HEAD_DIM : (h + 1) * HEAD_DIM]).astype(BF16)
        mixed = (mid + drop_sum[...] + dot(d_hid, drop_b[...])).astype(BF16)
        mixed_kept[...] = mixed[: rows // 2]
        mixed_back[...] = mixed[rows // 2 :]
        gl = dot(gl_grad.T, normed_ref[...])
        own = (
            dot(d_hid.T, cot_ref[...]), gl[:RANK], gl[RANK:],
            dot(hgrad.T, att[...]), dot(hid[...].T, branch[...]),
        )
        for t in range(4):
            for u, ref in enumerate(chunk_refs):
                whole[t, :, u * chunk_cols : (u + 1) * chunk_cols] = ref[t]
            for j, g in enumerate(own):
                at = len(packs) * chunk_cols + j * quarter
                whole[t, :, at : at + quarter] = g[:, t * quarter : (t + 1) * quarter]
        split_by_core(pr, whole, keep, send)

    quarter = width // 4
    chunk_cols = packs[0].shape[2]
    cols = len(packs) * chunk_cols + 5 * quarter
    return kernel_call(
        body, place, bundle, landing,
        [(v, VM) for v in (*packs, *sums, middle, cot, gain, normed, attended, hidden, *factors)],
        [
            (like((rows // 2, width), BF16), VM),
            (like((rows // 2, width), BF16), VM),
            (like((rows, width), F32), VM),
            (like((heads, rows, LANES), BF16), VM),
            (like((2, RANK, cols), F32), VM),
            (like((2, RANK, cols), BF16), VM),
        ],
        [pltpu.VMEM((rows, width), BF16), pltpu.VMEM((4, RANK, cols), F32)], "out_backward", time=15,
    )


def qkv_gradients(place, dq, dkv, dkv_got, cos, sin, normed, hidden, outer):
    rows, width = normed.shape
    total = outer.shape[1]
    kv = (total - width) // 2
    half = HEAD_DIM // 2
    rank3 = outer.shape[0]
    quarter, kv_quarter = width // 4, kv // 4
    cols = 4 * quarter + 2 * kv_quarter

    def body(pr, land_refs, ins, outs, weights, sems, scratch):
        dq_ref, dkv_ref, got_ref, cos_ref, sin_ref, nrm, hid, b = ins
        g, hgrad_ref, keep, send = outs
        (whole,) = scratch
        for h in range(width // HEAD_DIM):
            g[:, h * HEAD_DIM : (h + 1) * HEAD_DIM] = dq_ref[h, :, :HEAD_DIM]
        for h in range(kv // HEAD_DIM):
            one = (dkv_ref[0, h] + got_ref[0, h].astype(F32))[:, :HEAD_DIM]
            at = width + h * HEAD_DIM
            g[:, at : at + HEAD_DIM] = turn(one, cos_ref[...], -sin_ref[...], half).astype(BF16)
            at += kv
            g[:, at : at + HEAD_DIM] = (dkv_ref[1, h] + got_ref[1, h].astype(F32))[:, :HEAD_DIM].astype(BF16)
        hgrad_ref[...] = dot_nt(g[...], b[...]).astype(BF16)
        g_in = dot(hgrad_ref[...].T, nrm[...])
        g_out = dot(hid[...].T, g[...])
        for t in range(4):
            for i in range(3):
                whole[t, :, i * quarter : (i + 1) * quarter] = g_in[
                    i * RANK : (i + 1) * RANK, t * quarter : (t + 1) * quarter
                ]
            whole[t, :, 3 * quarter : 4 * quarter] = g_out[:RANK, t * quarter : (t + 1) * quarter]
            for i in range(2):
                at, start = 4 * quarter + i * kv_quarter, width + i * kv + t * kv_quarter
                whole[t, :, at : at + kv_quarter] = g_out[
                    (1 + i) * RANK : (2 + i) * RANK, start : start + kv_quarter
                ]
        split_by_core(pr, whole, keep, send)

    return kernel_call(
        body, place, NO_BUNDLE, [],
        [(v, VM) for v in (dq, dkv, dkv_got, cos, sin, normed, hidden, outer)],
        [
            (like((rows, total), BF16), VM),
            (like((rows, rank3), BF16), VM),
            (like((2, RANK, cols), F32), VM),
            (like((2, RANK, cols), BF16), VM),
        ],
        [pltpu.VMEM((4, RANK, cols), F32)], "qkv_gradients", time=10,
    )


def qkv_backward(place, bundle, landing, g, hgrad, x, mid_grad, gain, inner, ties):
    rows, width = x.shape
    total = bundle.shapes[0][1]
    block = rows // 2

    def body(pr, land_refs, ins, outs, weights, sems, scratch):
        g_ref, hg, x_ref, mg, gain_ref, a = ins
        kept, back = outs
        (w,) = weights
        landing = Landing(pr, bundle, land_refs, weights, sems)
        xf = x_ref[...].astype(F32)
        scale = lax.rsqrt(jnp.mean(xf * xf, axis=-1, keepdims=True) + EPSILON)
        n = xf * scale
        thin = dot(hg[...], a[...])
        landing.wait()
        e_in = (dot_nt(g_ref[...], w[...]) + thin) * gain_ref[...].astype(F32)
        mean = jnp.mean(e_in * n, axis=-1, keepdims=True)
        result = mg[...] + scale * (e_in - n * mean)
        kept[...] = result[:block]
        back[...] = result[block:].astype(BF16)

    return kernel_call(
        body, place, bundle, landing,
        [(v, VM) for v in (g, hgrad, x, mid_grad, gain, inner)],
        [(like((block, width), F32), VM), (like((block, width), BF16), VM)],
        [], "qkv_backward", time=14, ties=ties,
    )


def pack_factors(place, inners, outers):
    widths = [a.shape[0] for a in inners] + [b.shape[1] for b in outers]
    n = len(inners)
    mix = outers[0].shape[0]

    def body(pr, land_refs, ins, outs, weights, sems, scratch):
        for which, out in enumerate(outs):
            row = lax.broadcasted_iota(jnp.int32, (RANK, mix), 0) + pr[3 + which] * RANK
            choose = (row == lax.broadcasted_iota(jnp.int32, (RANK, mix), 1)).astype(F32).astype(BF16)
            at = 0
            for i, ref in enumerate(ins):
                part = dot_nt(choose, ref[...]) if i < n else dot(choose, ref[...])
                out[:, at : at + widths[i]] = part.astype(BF16)
                at += widths[i]

    shape = (like((RANK, sum(widths)), BF16), VM)
    return kernel_call(
        body, place, NO_BUNDLE, [], [(v, VM) for v in (*inners, *outers)], [shape, shape], [], "pack_factors"
    )


def unpack_factors(place, slots, widths, chunks):
    inner_w, outer_w = widths[:7], widths[7:]
    width, kv = 4 * outer_w[0], 4 * outer_w[1]
    part = outer_w[4] // chunks
    starts = [sum(widths[:i]) for i in range(len(widths))]

    def body(pr, land_refs, ins, outs, weights, sems, scratch):
        iq, oq, io, oo, igl, ogl, da, db = outs
        (nat,) = scratch
        mine, two, got = ins
        nat[pr[0]] = mine[...]
        nat[pr[0] ^ 2] = two[...]
        nat[pr[0] ^ 1] = got[:RANK]
        nat[pr[0] ^ 3] = got[RANK:]
        oq[...] = jnp.zeros(oq.shape, BF16)
        for t in range(4):
            get = lambda i, a=0, n=None: nat[t, :, starts[i] + a : starts[i] + a + (n or widths[i])]
            w = inner_w[0]
            here = slice(t * w, (t + 1) * w)
            for i in range(3):
                iq[i * RANK : (i + 1) * RANK, here] = get(i)
            io[:, here] = get(3)
            igl[:RANK, here] = get(4)
            igl[RANK:, here] = get(5)
            base = 0
            for i in range(3):
                n = outer_w[i]
                oq[i * RANK : (i + 1) * RANK, base + t * n : base + (t + 1) * n] = get(7 + i)
                base += 4 * n
            oo[:, here] = get(10)
            db[:, here] = get(13)
            for u in range(chunks):
                there = slice(t * part, (t + 1) * part)
                ogl[u, :RANK, there] = get(11, u * part, part)
                ogl[u, RANK:, there] = get(12, u * part, part)
                da[u, :, there] = get(6, u * part, part)

    shapes = [
        (3 * RANK, width), (3 * RANK, width + 2 * kv), (RANK, width), (RANK, width), (2 * RANK, width),
        (chunks, 2 * RANK, 4 * part), (chunks, RANK, 4 * part), (RANK, width),
    ]
    return kernel_call(
        body, place, NO_BUNDLE, [], [(v, VM) for v in slots], [(like(sh, BF16), VM) for sh in shapes],
        [pltpu.VMEM((4, *slots[0].shape), BF16)], "unpack_factors",
    )


def fold_cores(place, keep, got, name):
    _, rank, cols = keep.shape

    def body(pr, land_refs, ins, outs, weights, sems, scratch):
        keep_ref, got_ref = ins
        chip = pr[0] // 2
        for out, which in zip(outs, (chip, 1 - chip)):
            out[:, :cols] = (keep_ref[which] + got_ref[which].astype(F32)).astype(BF16)
            out[:, cols:] = jnp.full((rank, LANES), pr[3], jnp.int32).astype(F32).astype(BF16)

    shape = (like((rank, cols + LANES), BF16), VM)
    return kernel_call(
        body, place, NO_BUNDLE, [], [(keep, VM), (got, VM)], [shape, shape], [], name
    )


def spread_sums(place, gathered, pieces, mix, name):
    count = gathered.shape[0]
    cols = gathered.shape[1] - LANES

    def body(pr, land_refs, ins, outs, weights, sems, scratch):
        (got,) = ins
        tag = got[:, cols:].astype(F32).astype(jnp.int32) * RANK
        spot = tag + lax.broadcasted_iota(jnp.int32, (count, LANES), 0) % RANK
        choose = (spot == lax.broadcasted_iota(jnp.int32, (count, LANES), 1)).astype(F32).astype(BF16)
        choose_t = choose.T
        for out, (is_inner, runs) in zip(outs, pieces):
            at = 0
            for start, n in runs:
                if is_inner:
                    out[at : at + n] = dot_tn(got[:, start : start + n], choose)
                else:
                    out[:, at : at + n] = dot(choose_t, got[:, start : start + n])
                at += n

    outs = []
    for is_inner, runs in pieces:
        n = sum(c for _, c in runs)
        outs.append((like((n, mix) if is_inner else (mix, n), F32), VM))
    return kernel_call(body, place, NO_BUNDLE, [], [(gathered, VM)], outs, [], name)


def local(
    tokens,
    cotangent,
    prefix_len,
    adapter_index,
    gain_attn,
    gain_mlp,
    query_weight,
    key_weight,
    value_weight,
    output_weight,
    gate_weight,
    lift_weight,
    drop_weight,
    *factors,
):
    _, block, width = tokens.shape
    rep, shard = lax.axis_index("rep"), lax.axis_index("shard")
    chip = shard // 2
    rows = 2 * block
    kv_width = KV_HEADS * HEAD_DIM
    place = jnp.stack(
        [shard, rep % 4, prefix_len[chip], adapter_index[chip], adapter_index[1 - chip]]
    ).astype(jnp.int32)

    def swap_out(kept, back, dtype):
        back = to_diag(back).astype(dtype)
        return jnp.where(chip == 0, jnp.stack([kept, back]), jnp.stack([back, kept]))

    weights = (query_weight, key_weight, value_weight, output_weight, gate_weight, lift_weight, drop_weight)
    inners, outers = factors[0::2], factors[1::2]
    widths = [a.shape[0] for a in inners] + [b.shape[1] for b in outers]
    chunks = 4
    ff = gate_weight.shape[1]
    bundles = make_bundles(width, kv_width, ff, chunks, 4)
    relay = Relay(place, weights, bundles)
    half = block // 2
    relay.step()
    mine, others = pack_factors(place, inners, outers)
    slot_two = to_chip(others)
    (tokens_a,), _ = relay.step([(tokens, 0, half)])
    got = to_core(jnp.concatenate([mine, slot_two], axis=0))
    (tokens_b,), _ = relay.step([(tokens, half, half)], ties=(slot_two, tokens_a))
    relay.step(ties=(tokens_b,))
    inner_qkv, outer_qkv, inner_o, outer_o, inner_gl, outer_gl, drop_a, drop_b = unpack_factors(
        place, (mine, slot_two, got), widths, chunks
    )
    positions = jnp.concatenate(
        [shard * block + jnp.arange(block), (shard ^ 3) * block + jnp.arange(block)]
    )
    cos_table, sine_table = rotary_tables(positions.astype(F32), HEAD_DIM)
    cos_full = jnp.concatenate([cos_table, cos_table], axis=1)
    sin_full = jnp.concatenate([-sine_table, sine_table], axis=1)
    gain_one, gain_two = gain_attn[None], gain_mlp[None]

    def landing(i):
        return landing_operands(bundles[i], weights, relay.here[i], relay.there[i])

    (cot_a,), begun = relay.step([(cotangent, 0, half)], ties=(got,))
    queries, kv_own, hidden_qkv, normed_attn, x = qkv_forward(
        place, bundles[0], landing(0), tokens, (tokens_a, tokens_b), gain_one,
        inner_qkv, outer_qkv, cos_full, sin_full, begun[:1],
    )
    kv_near = to_core(kv_own)
    (cot_b,), _ = relay.step([(cotangent, half, half)], ties=(x, cot_a))
    heads_out, lse = attend(place, queries, kv_own, kv_near)
    middle, normed_mlp, attended, output_hidden, cot, hidden_gl, hidden_d = out_forward(
        place, bundles[1], landing(1), heads_out, x, gain_two, inner_o, outer_o,
        cotangent, (cot_a, cot_b), inner_gl, drop_b,
    )
    relay.step(ties=(normed_mlp,))
    sums, packs = None, []
    for u in range(chunks):
        *sums, packed = mlp_chunk(
            place, bundles[2 + u], landing(2 + u), normed_mlp, cot, hidden_gl, hidden_d,
            outer_gl, drop_a, u, sums, f"mlp_{u}",
        )
        packs.append(packed)
        if u < 2:
            relay.step(ties=(packed,))
    mixed_kept, mixed_back, middle_grad, grad_heads, keep, send = out_backward(
        place, bundles[1], landing(1), sums, packs, middle, cot, gain_two, normed_mlp, attended,
        output_hidden, (drop_b, inner_gl, inner_o, outer_o),
    )

    def gather_sums(keep, send, name):
        own, other = fold_cores(place, keep, to_core(send), name)
        both = jnp.concatenate([own, to_chip(other)], axis=0)
        return both, lax.all_gather(both, "rep", axis=0, tiled=True)

    both, late = gather_sums(keep, send, "fold_late")
    mixed = swap_out(mixed_kept, mixed_back, BF16)
    dq, dkv, dkv_send = attend_back(
        place, queries, kv_own, kv_near, grad_heads, lse, cos_table.T, sine_table.T,
        ties=(both,),
    )
    g, hgrad, keep, send = qkv_gradients(
        place, dq, dkv, to_core(dkv_send),
        cos_full, sin_full, normed_attn, hidden_qkv, outer_qkv,
    )
    _, first = gather_sums(keep, send, "fold_first")
    input_kept, input_back = qkv_backward(
        place, bundles[0], landing(0), g, hgrad, x, middle_grad, gain_one, inner_qkv, (late,)
    )
    input_grad = swap_out(input_kept, input_back, F32)

    mix = ADAPTERS * RANK
    w, kw = width // 4, kv_width // 4
    q_in, k_in, v_in, q_out, k_out, v_out = spread_sums(
        place, first,
        [(True, [(0, w)]), (True, [(w, w)]), (True, [(2 * w, w)]), (False, [(3 * w, w)]),
         (False, [(4 * w, kw)]), (False, [(4 * w + kw, kw)])],
        mix, "spread_first",
    )
    part = ff // 4 // chunks
    runs = lambda j: [(u * 3 * part + j * part, part) for u in range(chunks)]
    base = chunks * 3 * part
    g_out, l_out, d_in, d_out, g_in, l_in, o_in, o_out = spread_sums(
        place, late,
        [(False, runs(0)), (False, runs(1)), (True, runs(2)), (False, [(base, w)]), (True, [(base + w, w)]),
         (True, [(base + 2 * w, w)]), (True, [(base + 3 * w, w)]), (False, [(base + 4 * w, w)])],
        mix, "spread_late",
    )
    return (mixed, input_grad, q_in, q_out, k_in, k_out, v_in, v_out, o_in, o_out,
            g_in, g_out, l_in, l_out, d_in, d_out)


def solution(mesh):
    token_place = P("rep", "shard", None)
    row, col = P("shard", None), P(None, "shard")
    return jax.shard_map(
        local,
        mesh=mesh,
        in_specs=(token_place, token_place, P("rep"), P("rep"), P(), P()) + (row,) * 7 + (row, col) * 7,
        out_specs=(token_place, token_place) + (row, col) * 7,
        check_vma=False,
    )
```

```python
import functools
import math
from typing import NamedTuple

import jax
import jax.numpy as jnp
from jax import lax
from jax.experimental import pallas as pl
from jax.experimental.pallas import tpu as pltpu
from jax.sharding import PartitionSpec as P

HEADS = 16
KV_HEADS = 8
HEAD_DIM = 96
RANK = 16
ADAPTERS = 8
EPSILON = 1e-05
ROPE_BASE = 100000.0
MASKED_SCORE = -1e30
AXES = ("rep", "shard")
F32 = jnp.float32
BF16 = jnp.bfloat16


def move(value, target):
    reps, shards = lax.axis_size("rep"), lax.axis_size("shard")
    pairs = []
    for r in range(reps):
        for s in range(shards):
            r2, s2 = target(r, s)
            pairs.append((r * shards + s, r2 * shards + s2))
    return lax.ppermute(value, AXES, pairs)


def to_core(value):
    return move(value, lambda r, s: (r, s ^ 1))


def to_chip(value):
    return move(value, lambda r, s: (r, s ^ 2))


def to_diag(value):
    return move(value, lambda r, s: (r, s ^ 3))


def to_y(value):
    return move(value, lambda r, s: (r ^ 1, s))


def to_z(value):
    return move(value, lambda r, s: (r ^ 2, s))


PANEL = 512
LANES = 128
EST = 5
PACK_EST = 0.1


class Piece(NamedTuple):
    parts: tuple
    row: int
    rows: int
    target: int
    block: int
    to_row: int
    to_col: int


class Bundle(NamedTuple):
    first: tuple
    second: tuple
    shapes: tuple


def quarter_rows(pieces):
    return sum(p.rows for p in pieces) // 4


def make_bundles(width, kv_width, ff, chunks, shards):
    rows, drop_rows = width // shards, ff // shards // chunks
    panels = width // PANEL
    first = tuple(Piece(((0, c, PANEL),), 0, rows, 0, rows, 0, c) for c in range(0, width, PANEL))
    second = []
    for c in range(0, 2 * kv_width, PANEL):
        parts, at = [], c
        while at < c + PANEL:
            source = 1 if at < kv_width else 2
            base = (source - 1) * kv_width
            stop = min(c + PANEL, base + kv_width)
            parts.append((source, at - base, stop - at))
            at = stop
        second.append(Piece(tuple(parts), 0, rows, 0, rows, 0, width + c))
    found = [Bundle(first, tuple(second), ((width, width + 2 * kv_width),))]

    def halves(source, row, height, target, block):
        return [
            tuple(
                Piece(((source, i * PANEL, PANEL),), row + h * height // 2, height // 2, target, block,
                      h * height // 2, i * PANEL)
                for i in range(panels)
            )
            for h in range(2)
        ]

    top, bottom = halves(3, 0, rows, 0, rows)
    found.append(Bundle(top, bottom, ((width, width),)))
    part = ff // shards // chunks
    for u in range(chunks):
        sides = []
        for j in range(2):
            side = []
            for c in range(0, shards * part, PANEL):
                parts = tuple(
                    (4 + j, t * (ff // shards) + u * part, part)
                    for t in range(c // part, (c + PANEL) // part)
                )
                side.append(Piece(parts, 0, rows, 0, rows, 0, 2 * c + j * PANEL))
            sides.append(tuple(side))
        top, bottom = halves(6, u * drop_rows, drop_rows, 1, drop_rows)
        cols = shards * part
        found.append(
            Bundle(sides[0] + top, sides[1] + bottom, ((width, 2 * cols), (cols, width)))
        )
    return found


def work(microseconds):
    return pl.CostEstimate(flops=int(microseconds * 1.1e9), bytes_accessed=2**20, transcendentals=0)


def pack(place, jobs, operands, out_shapes, name):
    n_in, n_out = len(operands), len(out_shapes)

    def kernel(place_ref, *refs):
        ins, refs = refs[:n_in], refs[n_in:]
        outs, held, sems = refs[:n_out], refs[n_out : 2 * n_out], refs[-1]
        arriving, leaving = [], []
        for i, (src, o, *spot) in enumerate(jobs(place_ref, ins)):
            here = held[o].at[tuple(spot)]
            arriving.append(pltpu.make_async_copy(src, here, sems.at[0, i]))
            leaving.append(pltpu.make_async_copy(here, outs[o].at[tuple(spot)], sems.at[1, i]))
        for c in arriving:
            c.start()
        for c, d in zip(arriving, leaving):
            c.wait()
            d.start()
        for d in leaving:
            d.wait()

    class Fake:
        def __init__(self):
            self.at = self

        def __getitem__(self, _):
            return self

    count = len(jobs(None, [Fake()] * n_in))
    hbm = pl.BlockSpec(memory_space=pltpu.HBM)
    return pl.pallas_call(
        kernel,
        out_shape=[jax.ShapeDtypeStruct(sh, BF16) for sh in out_shapes],
        grid_spec=pltpu.PrefetchScalarGridSpec(
            num_scalar_prefetch=1,
            grid=(1,),
            in_specs=[hbm] * n_in,
            out_specs=[hbm] * n_out,
            scratch_shapes=[pltpu.VMEM(sh, BF16) for sh in out_shapes]
            + [pltpu.SemaphoreType.DMA((2, count))],
        ),
        compiler_params=pltpu.CompilerParams(vmem_limit_bytes=64 * 2**20),
        cost_estimate=work(PACK_EST),
        name=name,
    )(place, *operands)


def gate(value, ties):
    return pl.pallas_call(
        lambda *refs: None,
        out_shape=jax.ShapeDtypeStruct(value.shape, value.dtype),
        in_specs=[pl.BlockSpec(memory_space=pltpu.HBM)] * (1 + len(ties)),
        out_specs=pl.BlockSpec(memory_space=pltpu.HBM),
        input_output_aliases={0: 0},
        compiler_params=pltpu.CompilerParams(vmem_limit_bytes=64 * 2**20),
        name="gate",
    )(value, *ties)


def quarter_start(place_ref, flip, rows):
    if place_ref is None:
        return 0
    return pl.multiple_of((place_ref[1] ^ flip) * rows, 16)


class Relay:
    def __init__(self, place, weights, bundles):
        self.place, self.weights, self.bundles = place, weights, bundles
        self.direct, self.once, self.twice = {}, {}, {}
        self.here, self.there = {}, {}
        self.tick = 0

    def step(self, extra=(), ties=()):
        t, bundles = self.tick, self.bundles
        self.tick += 1
        operands, shapes, kinds = [], [], []

        def operand(array):
            for i, o in enumerate(operands):
                if o is array:
                    return i
            operands.append(array)
            return len(operands) - 1

        plans = []

        def out(kind, rows, cols=PANEL):
            shapes.append((rows, cols))
            kinds.append(kind)
            return len(shapes) - 1

        if t < len(bundles):
            b = bundles[t]
            o = out("x", quarter_rows(b.first + b.second))
            used = [(operand(self.weights[q[0]]), q, p) for p in b.first + b.second for q in p.parts]

            def plan_x(pr, ins, o=o, used=used):
                copies, at, col = [], 0, 0
                for i, (_, c, n), p in used:
                    q = p.rows // 4
                    rows = pl.ds(pl.multiple_of(p.row + quarter_start(pr, 0, q), 16), q)
                    copies.append((ins[i].at[rows, pl.ds(c, n)],
                                   o, pl.ds(at, q), pl.ds(col, n)))
                    col += n
                    if col == PANEL:
                        at, col = at + q, 0
                return copies

            plans.append(plan_x)
        y_parts, z_parts = [], []
        b1, b2, b3 = t - 1, t - 2, t - 3
        if 0 <= b1 < len(bundles):
            qa, qb = quarter_rows(bundles[b1].first), quarter_rows(bundles[b1].second)
            y_parts.append(("first", b1, [(self.direct[b1], 0, qa)]))
            z_parts.append(("first", b1, [(self.direct[b1], qa, qb)]))
        if 0 <= b2 < len(bundles):
            qa, qb = quarter_rows(bundles[b2].first), quarter_rows(bundles[b2].second)
            (ya, yo), (za, zo) = self.once[b2]
            y_parts.append(("second", b2, [(self.direct[b2], qa, qb), (za, zo, qb)]))
            z_parts.append(("second", b2, [(self.direct[b2], 0, qa), (ya, yo, qa)]))
        for kind, parts in (("y", y_parts), ("z", z_parts)):
            if not parts:
                continue
            total = sum(n for _, _, l in parts for _, _, n in l)
            o = out(kind, total)
            flat = [(operand(a), r, n) for _, _, l in parts for a, r, n in l]

            def plan_n(pr, ins, o=o, flat=flat):
                copies, at = [], 0
                for i, r, n in flat:
                    copies.append((ins[i].at[pl.ds(r, n)], o, pl.ds(at, n), slice(None)))
                    at += n
                return copies

            plans.append(plan_n)
        for array, start, count in extra:
            o = out("d", count, array.shape[2])
            i = operand(array)

            def plan_d(pr, ins, o=o, i=i, start=start, count=count):
                which = 0 if pr is None else 1 - pr[0] // 2
                return [(ins[i].at[which, pl.ds(start, count)], o, slice(None), slice(None))]

            plans.append(plan_d)
        for tie in ties:
            operand(tie)

        def jobs(pr, ins):
            return [c for plan in plans for c in plan(pr, ins)]

        bufs = pack(self.place, jobs, operands, shapes, f"pack_{t}") if shapes else []
        sent = []
        for kind, buf in zip(kinds, bufs):
            if kind == "x":
                self.direct[t] = to_chip(buf)
            elif kind == "d":
                sent.append(to_diag(buf))
            else:
                got = (to_y if kind == "y" else to_z)(buf)
                at = 0
                for stage, bi, l in y_parts if kind == "y" else z_parts:
                    store = self.once if stage == "first" else self.twice
                    pair = store.setdefault(bi, [None, None])
                    pair[0 if kind == "y" else 1] = (got, at)
                    at += sum(n for _, _, n in l)
        if 0 <= b3 < len(bundles):
            self.across(b3, bufs[:1] if bufs else ties)
        return sent, bufs

    def across(self, b3, ties):
        b = self.bundles[b3]
        operands, shapes = [], []

        def operand(array):
            for i, o in enumerate(operands):
                if o is array:
                    return i
            operands.append(array)
            return len(operands) - 1

        plans = []

        def out(kind, rows, cols=PANEL):
            shapes.append((rows, cols))
            return len(shapes) - 1

        total = 4 * quarter_rows(b.first + b.second)
        o = out("c", 2 * total)
        used = [(operand(self.weights[q[0]]), q, p) for p in b.first + b.second for q in p.parts]
        qa = quarter_rows(b.first)
        qb = quarter_rows(b.second)
        (ya, yo), (za, zo) = self.once[b3]
        (ys, yso), (zs, zso) = self.twice[b3]
        d = operand(self.direct[b3])
        sides = [
            (b.first, [(0, d, 0), (1, operand(ya), yo), (2, operand(zs), zso), (3, operand(zs), zso + qa)]),
            (b.second, [(0, d, qa), (2, operand(za), zo), (1, operand(ys), yso), (3, operand(ys), yso + qb)]),
        ]

        def plan_c(pr, ins, o=o, sides=sides, used=used, total=total):
            copies, base, at, col = [], total, 0, 0
            for i, (_, c, n), p in used:
                copies.append((ins[i].at[pl.ds(p.row, p.rows), pl.ds(c, n)],
                               o, pl.ds(at, p.rows), pl.ds(col, n)))
                col += n
                if col == PANEL:
                    at, col = at + p.rows, 0
            for pieces, quarters in sides:
                at = 0
                for p in pieces:
                    q = p.rows // 4
                    for flip, i, r in quarters:
                        to = pl.multiple_of(base + quarter_start(pr, flip, q), 16)
                        copies.append((ins[i].at[pl.ds(r + at, q)], o, pl.ds(to, q), slice(None)))
                    at += q
                    base += p.rows
            return copies

        plans.append(plan_c)

        for tie in ties:
            operand(tie)
        jobs = lambda pr, ins: plans[0](pr, ins)
        (buf,) = pack(self.place, jobs, operands, shapes, f"across_{b3}")
        self.here[b3], self.there[b3] = buf, to_core(buf)


def land_copies(place_ref, bundle, own, here, there, targets):
    copies = []
    shard = 0 if place_ref is None else place_ref[0]
    pieces = bundle.first + bundle.second
    total = sum(p.rows for p in pieces)
    for slot, (ref, base) in enumerate(((None, 0), (there, 0), (here, total), (there, total))):
        for p in pieces:
            to = (shard ^ slot) * p.block + p.to_row
            to = pl.ds(pl.multiple_of(to, 16), p.rows)
            dst = targets[p.target]
            key = (p.target, p.to_col)
            if slot == 0:
                col = p.to_col
                for source, c, n in p.parts:
                    copies.append((own[source].at[pl.ds(p.row, p.rows), pl.ds(c, n)],
                                   dst.at[to, pl.ds(col, n)], key))
                    col += n
            else:
                copies.append((ref.at[pl.ds(base, p.rows)], dst.at[to, pl.ds(p.to_col, PANEL)], key))
            base += p.rows
    return copies


def sources_of(bundle):
    return sorted({q[0] for p in bundle.first + bundle.second for q in p.parts})


def rotary_tables(positions, head_dim):
    half_dim = head_dim // 2
    freq_index = jnp.arange(half_dim).astype(F32)
    frequency = jnp.exp(freq_index * (-2.0 * math.log(ROPE_BASE) / head_dim))
    angles = positions[:, None] * frequency[None, :]
    return jnp.cos(angles), jnp.sin(angles)


def dot(left, right):
    return jnp.dot(left, right, preferred_element_type=F32)


def dot_nt(left, right):
    return lax.dot_general(left, right, (((1,), (1,)), ((), ())), preferred_element_type=F32)


def dot_tn(left, right):
    return lax.dot_general(left, right, (((0,), (0,)), ((), ())), preferred_element_type=F32)


LOG2E = 1.4426950408889634


def last_visible(place_ref, low, lanes, block):
    shard, prefix = place_ref[0], place_ref[2]
    low_block = (shard ^ (shard // 2)) & 1
    at = low_block if low else 3 - low_block
    position = at * block + lax.broadcasted_iota(jnp.int32, (1, lanes), 1) % block
    return jnp.maximum(position + 1, prefix)


def query_start(place_ref, low, block):
    chip = place_ref[0] // 2
    return pl.multiple_of((chip if low else 1 - chip) * block, block)


def natural_rows(place_ref, own, near, into, block):
    shard = place_ref[0]
    for slot, value in (
        (0, own[0, :block]),
        (3, own[0, block:]),
        (1, near[0, :block]),
        (2, near[0, block:]),
    ):
        into[pl.ds(pl.multiple_of((shard ^ slot) * block, block), block)] = value


def hide(scores, limit, first_key):
    keys = first_key + lax.broadcasted_iota(jnp.int32, scores.shape, 0)
    return jnp.where(keys < limit, scores, MASKED_SCORE)


def masked_by_part(low, scores, limit, block):
    if low:
        return hide(scores, limit, 0)
    half = 2 * block
    return jnp.concatenate([scores[:half], hide(scores[half:], limit, half)], axis=0)


def attend_kernel(place, q, k_own, k_near, v_own, v_near, out, lse, keys, values, *, scale):
    block = q.shape[1] // 2
    group = q.shape[0]
    natural_rows(place, k_own, k_near, keys, block)
    natural_rows(place, v_own, v_near, values, block)
    values_t = values[...].T
    for part, low in enumerate((True, False)):
        count = (2 if low else 4) * block
        rows = pl.ds(query_start(place, low, block), block)
        query = jnp.concatenate([q[j, rows] for j in range(group)], axis=0)
        limit = last_visible(place, low, group * block, block)
        scores = masked_by_part(low, dot_nt(keys[:count], query), limit, block)
        top = jnp.max(scores, axis=0, keepdims=True)
        base = scale * LOG2E
        expo = jnp.exp2(scores * base - top * base)
        total = jnp.sum(expo, axis=0, keepdims=True)
        lse[0, part] = (top * base + jnp.log2(total))[0]
        result = dot(values_t[:, :count], expo.astype(BF16)) / total
        result = result.T.astype(BF16)
        for j in range(group):
            out[j, rows] = result[j * block : (j + 1) * block]


def attend(place, queries, kv_own, kv_near):
    heads, rows, dim = queries.shape
    kv_heads = kv_own.shape[0] // 2
    group = heads // kv_heads
    q_spec = pl.BlockSpec((group, rows, dim), lambda g, p: (g, 0, 0))
    kv_spec = pl.BlockSpec((1, rows, dim), lambda g, p: (g, 0, 0))
    v_spec = pl.BlockSpec((1, rows, dim), lambda g, p: (g + kv_heads, 0, 0))
    lse_shape = (kv_heads, 2, group * rows // 2)
    return pl.pallas_call(
        functools.partial(attend_kernel, scale=HEAD_DIM ** (-0.5)),
        out_shape=[
            jax.ShapeDtypeStruct(queries.shape, BF16),
            jax.ShapeDtypeStruct(lse_shape, F32),
        ],
        grid_spec=pltpu.PrefetchScalarGridSpec(
            num_scalar_prefetch=1,
            grid=(kv_heads,),
            in_specs=[q_spec, kv_spec, kv_spec, v_spec, v_spec],
            out_specs=[q_spec, pl.BlockSpec((1, *lse_shape[1:]), lambda g, p: (g, 0, 0))],
            scratch_shapes=[pltpu.VMEM((2 * rows, dim), BF16)] * 2,
        ),
        compiler_params=pltpu.CompilerParams(vmem_limit_bytes=64 * 2**20),
        cost_estimate=work(EST),
        name="attend",
    )(place, queries, kv_own, kv_near, kv_own, kv_near)


def attend_back_kernel(
    place, q, k_own, k_near, v_own, v_near, grad, lse, cos_t, sin_t, *rest, scale
):
    dq, own_out, send_out, keys, values, dk, dv = rest[-7:]
    block = q.shape[1] // 2
    group = q.shape[0]
    half = HEAD_DIM // 2
    natural_rows(place, k_own, k_near, keys, block)
    natural_rows(place, v_own, v_near, values, block)
    keys_t = keys[...].T
    for part, low in ((1, False), (0, True)):
        count = (2 if low else 4) * block
        start = query_start(place, low, block)
        rows = pl.ds(start, block)
        query = jnp.concatenate([q[j, rows] for j in range(group)], axis=0)
        out_grad = jnp.concatenate([grad[j, rows] for j in range(group)], axis=0)
        limit = last_visible(place, low, group * block, block)
        scores = masked_by_part(low, dot_nt(keys[:count], query), limit, block)
        probs = jnp.exp2(scores * (scale * LOG2E) - lse[0, part][None])
        probs_grad = dot_nt(values[:count], out_grad)
        mean = jnp.sum(probs * probs_grad, axis=0, keepdims=True)
        score_grad = (probs * (probs_grad - mean)).astype(BF16)
        v_part = dot(probs.astype(BF16), out_grad)
        k_part = dot(score_grad, query) * scale
        if low:
            dk[:count] += k_part
            dv[:count] += v_part
        else:
            dk[...] = k_part
            dv[...] = v_part
        turned = dot(keys_t[:, :count], score_grad) * scale
        cos = jnp.concatenate([cos_t[:, rows]] * group, axis=1)
        sin = jnp.concatenate([sin_t[:, rows]] * group, axis=1)
        u, w = turned[:half], turned[half : 2 * half]
        pad = jnp.zeros((q.shape[2] - 2 * half, u.shape[1]), F32)
        turned = jnp.concatenate([u * cos + w * sin, w * cos - u * sin, pad], axis=0)
        turned = turned.T.astype(BF16)
        for j in range(group):
            dq[j, rows] = turned[j * block : (j + 1) * block]
    shard = place[0]
    for slot, at, own in ((0, 0, True), (3, 1, True), (1, 0, False), (2, 1, False)):
        rows = pl.ds(pl.multiple_of((shard ^ slot) * block, block), block)
        to = slice(at * block, (at + 1) * block)
        out = own_out if own else send_out
        out[0, 0, to] = dk[rows].astype(out.dtype)
        out[1, 0, to] = dv[rows].astype(out.dtype)


def attend_back(place, queries, kv_own, kv_near, grad, lse, cos_t, sin_t, part, parts, ties):
    heads, rows, dim = queries.shape
    kv_heads = kv_own.shape[0] // 2
    group = heads // kv_heads
    count = kv_heads // parts
    base = part * count
    q_spec = pl.BlockSpec((group, rows, dim), lambda g, p: (g + base, 0, 0))
    kv_spec = pl.BlockSpec((1, rows, dim), lambda g, p: (g + base, 0, 0))
    v_spec = pl.BlockSpec((1, rows, dim), lambda g, p: (g + base + kv_heads, 0, 0))
    whole = pl.BlockSpec(cos_t.shape, lambda g, p: (0, 0))
    return pl.pallas_call(
        functools.partial(attend_back_kernel, scale=HEAD_DIM ** (-0.5)),
        out_shape=[
            jax.ShapeDtypeStruct((heads // parts, rows, dim), BF16),
            jax.ShapeDtypeStruct((2, count, rows, dim), F32),
            jax.ShapeDtypeStruct((2, count, rows, dim), BF16),
        ],
        grid_spec=pltpu.PrefetchScalarGridSpec(
            num_scalar_prefetch=1,
            grid=(count,),
            in_specs=[q_spec, kv_spec, kv_spec, v_spec, v_spec]
            + [q_spec, pl.BlockSpec((1, *lse.shape[1:]), lambda g, p: (g + base, 0, 0)), whole, whole]
            + [pl.BlockSpec(memory_space=pltpu.HBM)] * len(ties),
            out_specs=[pl.BlockSpec((group, rows, dim), lambda g, p: (g, 0, 0))] + [pl.BlockSpec((2, 1, rows, dim), lambda g, p: (0, g, 0, 0))] * 2,
            scratch_shapes=[pltpu.VMEM((2 * rows, dim), BF16)] * 2
            + [pltpu.VMEM((2 * rows, dim), F32)] * 2,
        ),
        compiler_params=pltpu.CompilerParams(vmem_limit_bytes=64 * 2**20),
        cost_estimate=work(24 // parts),
        name=f"attend_back_{part}",
    )(place, queries, kv_own, kv_near, kv_own, kv_near, grad, lse, cos_t, sin_t, *ties)


class Landing:
    def __init__(self, place, bundle, refs, targets, sems):
        used = sources_of(bundle)
        n = len(used)
        own = dict(zip(used, refs[:n]))
        listed = land_copies(place, bundle, own, refs[n], refs[n + 1], targets)
        self.copies = [
            (key, pltpu.make_async_copy(src, dst, sems.at[i])) for i, (src, dst, key) in enumerate(listed)
        ]
        self.copies.sort(key=lambda c: c[0])
        for _, c in self.copies:
            c.start()

    def wait(self, wanted=None):
        left = []
        for key, c in self.copies:
            if wanted is None or wanted(key):
                c.wait()
            else:
                left.append((key, c))
        self.copies = left


def landing_operands(bundle, weights, here, there):
    return [weights[i] for i in sources_of(bundle)] + [here, there]


def landing_count(bundle):
    return sum(len(p.parts) + 3 for p in bundle.first + bundle.second)


NO_BUNDLE = Bundle((), (), ())


def kernel_call(body, place, bundle, landing, operands, outs, scratch, name, time=3, ties=()):
    operands = [*operands, *((t, HB) for t in ties)]
    n_land, n_in, n_out, n_w = len(landing), len(operands), len(outs), len(bundle.shapes)

    def kernel(place_ref, *refs):
        land, refs = refs[:n_land], refs[n_land:]
        ins, refs = refs[: n_in - len(ties)], refs[n_in:]
        out, refs = refs[:n_out], refs[n_out:]
        body(place_ref, land, ins, out, refs[:n_w], refs[n_w], refs[n_w + 1 :])

    def spec(where):
        return where if isinstance(where, pl.BlockSpec) else pl.BlockSpec(memory_space=where)

    return pl.pallas_call(
        kernel,
        out_shape=[o for o, _ in outs],
        grid_spec=pltpu.PrefetchScalarGridSpec(
            num_scalar_prefetch=1,
            grid=(1,),
            in_specs=[spec(pltpu.HBM)] * n_land + [spec(w) for _, w in operands],
            out_specs=[spec(w) for _, w in outs],
            scratch_shapes=[pltpu.VMEM(sh, BF16) for sh in bundle.shapes]
            + [pltpu.SemaphoreType.DMA((max(landing_count(bundle), 1),))]
            + list(scratch),
        ),
        compiler_params=pltpu.CompilerParams(vmem_limit_bytes=64 * 2**20),
        cost_estimate=work(time),
        name=name,
    )(place, *landing, *[a for a, _ in operands])


VM = pltpu.VMEM
HB = pltpu.HBM


def like(shape, dtype):
    return jax.ShapeDtypeStruct(shape, dtype)


def turn(value, cos_full, sin_signed, half):
    swapped = jnp.concatenate([value[:, half:], value[:, :half]], axis=1)
    return value * cos_full + swapped * sin_signed


def padded(value):
    return jnp.concatenate([value, jnp.zeros((value.shape[0], LANES - HEAD_DIM), value.dtype)], axis=1)


def one_of_pair(block, width):
    return pl.BlockSpec((None, block, width), lambda i, p: (p[0] // 2, 0, 0))


def qkv_forward(place, bundle, landing, tokens, tokens_back, gain, inner, outer, cos, sin, ties):
    _, block, width = tokens.shape
    rows = 2 * block
    total = bundle.shapes[0][1]
    kv = (total - width) // 2
    wide = 8 * HEAD_DIM
    half = HEAD_DIM // 2

    def body(pr, land_refs, ins, outs, weights, sems, scratch):
        kept, *backs, gain_ref, inner_ref, outer_ref, cos_ref, sin_ref = ins
        q, kv_ref, hidden_ref, normed_ref, x_ref = outs
        (w,) = weights
        landing = Landing(pr, bundle, land_refs, weights, sems)
        x_ref[:block] = kept[...]
        at = block
        for back in backs:
            x_ref[at : at + back.shape[0]] = back[...]
            at += back.shape[0]
        x = x_ref[...].astype(F32)
        scale = lax.rsqrt(jnp.mean(x * x, axis=-1, keepdims=True) + EPSILON)
        normed_ref[...] = (x * scale * gain_ref[...].astype(F32)).astype(BF16)
        hidden_ref[...] = dot_nt(normed_ref[...], inner_ref[...]).astype(BF16)

        def columns(at):
            cols = pl.ds(at, wide)
            return dot(normed_ref[...], w[:, cols]) + dot(hidden_ref[...], outer_ref[:, cols])

        landing.wait(lambda key: key[1] < width)
        for i in range(width // wide):
            acc = columns(i * wide)
            for h in range(8):
                one = acc[:, h * HEAD_DIM : (h + 1) * HEAD_DIM]
                q[8 * i + h] = padded(turn(one, cos_ref[...], sin_ref[...], half)).astype(BF16)
        landing.wait()
        acc = columns(width)
        for h in range(8):
            one = acc[:, h * HEAD_DIM : (h + 1) * HEAD_DIM]
            kv_ref[h] = padded(turn(one, cos_ref[...], sin_ref[...], half)).astype(BF16)
        acc = columns(width + kv)
        for h in range(8):
            kv_ref[8 + h] = padded(acc[:, h * HEAD_DIM : (h + 1) * HEAD_DIM]).astype(BF16)

    heads = width // HEAD_DIM
    return kernel_call(
        body, place, bundle, landing,
        [(tokens, one_of_pair(block, width)), *((t, VM) for t in tokens_back), (gain, VM), (inner, VM), (outer, VM), (cos, VM), (sin, VM)],
        [
            (like((heads, rows, LANES), BF16), VM),
            (like((2 * kv // HEAD_DIM, rows, LANES), BF16), VM),
            (like((rows, inner.shape[0]), BF16), VM),
            (like((rows, width), BF16), VM),
            (like((rows, width), BF16), VM),
        ],
        [], "qkv_forward", time=EST, ties=ties,
    )


def out_forward(place, bundle, landing, heads_out, x, gain, inner, outer, cot, cot_back, inner_gl, drop_b):
    rows, width = x.shape
    heads = heads_out.shape[0]

    def body(pr, land_refs, ins, outs, weights, sems, scratch):
        heads_ref, x_ref, gain_ref, inner_ref, outer_ref, cot_kept, *cot_got, igl, db = ins
        middle, normed, attended, hidden, cot_ref, h_gl, h_d = outs
        landing = Landing(pr, bundle, land_refs, weights, sems)
        for h in range(heads):
            attended[:, h * HEAD_DIM : (h + 1) * HEAD_DIM] = heads_ref[h, :, :HEAD_DIM]
        hidden[...] = dot_nt(attended[...], inner_ref[...]).astype(BF16)
        cot_ref[: rows // 2] = cot_kept[...]
        at = rows // 2
        for got in cot_got:
            cot_ref[at : at + got.shape[0]] = got[...]
            at += got.shape[0]
        h_d[...] = dot_nt(cot_ref[...], db[...]).astype(BF16)
        landing.wait()
        wide = width // 2
        squares = jnp.zeros((rows, 1), F32)
        for i in range(2):
            cols = pl.ds(i * wide, wide)
            branch = dot(attended[...], weights[0][:, cols]) + dot(hidden[...], outer_ref[:, cols])
            value = x_ref[:, cols].astype(F32) + branch
            middle[:, cols] = value
            squares += jnp.sum(value * value, axis=-1, keepdims=True)
        scale = lax.rsqrt(squares / width + EPSILON)
        normed[...] = (middle[...] * scale * gain_ref[...].astype(F32)).astype(BF16)
        h_gl[...] = dot_nt(normed[...], igl[...]).astype(BF16)

    return kernel_call(
        body, place, bundle, landing,
        [(heads_out, VM), (x, VM), (gain, VM), (inner, VM), (outer, VM),
         (cot, one_of_pair(rows // 2, width)), *((c, VM) for c in cot_back), (inner_gl, VM), (drop_b, VM)],
        [
            (like((rows, width), F32), VM),
            (like((rows, width), BF16), VM),
            (like((rows, width), BF16), VM),
            (like((rows, RANK), BF16), VM),
            (like((rows, width), BF16), VM),
            (like((rows, 2 * RANK), BF16), VM),
            (like((rows, RANK), BF16), VM),
        ],
        [], "out_forward", time=EST,
    )


def mlp_chunk(place, bundle, landing, normed, cot, hidden_gl, hidden_d, outer_gl, drop_a, chunk, sums, name):
    rows, width = normed.shape
    units = bundle.shapes[1][0]
    steps = units // PANEL
    first = sums is None
    part = units // 4

    def body(pr, land_refs, ins, outs, weights, sems, scratch):
        normed_ref, cot_ref, hgl_ref, hd_ref, ogl, da = ins[:6]
        drop_sum, e_sum, thin, packed = outs
        w_gl, w_d = weights
        landing = Landing(pr, bundle, land_refs, weights, sems)
        h_d = hd_ref[...]
        h_g, h_l = hgl_ref[:, :RANK], hgl_ref[:, RANK:]
        g_t, l_t, d_t = h_g.T, h_l.T, h_d.T
        for i in range(steps):
            landing.wait(lambda key: key[0] == 1 or key[1] < 2 * (i + 1) * PANEL)
            cols = slice(i * PANEL, (i + 1) * PANEL)
            both = pl.ds(2 * i * PANEL, 2 * PANEL)
            acts = dot(normed_ref[...], w_gl[:, both])
            gate = acts[:, :PANEL] + dot(h_g, ogl[:RANK, cols])
            lift = acts[:, PANEL:] + dot(h_l, ogl[RANK:, cols])
            a_grad = dot_nt(cot_ref[...], w_d[cols]) + dot(h_d, da[:, cols])
            sig = 1.0 / (1.0 + jnp.exp(-gate))
            silu = gate * sig
            active = (silu * lift).astype(BF16)
            gate_grad = (a_grad * lift * sig * (1.0 + gate * (1.0 - sig))).astype(BF16)
            lift_grad = (a_grad * silu).astype(BF16)
            grads = jnp.concatenate([gate_grad, lift_grad], axis=1)
            down = dot(active, w_d[cols])
            back = dot_nt(grads, w_gl[:, both])
            t0 = dot_nt(active, da[:, cols])
            t1 = dot_nt(gate_grad, ogl[:RANK, cols])
            t2 = dot_nt(lift_grad, ogl[RANK:, cols])
            if i == 0 and first:
                drop_sum[...] = down
                e_sum[...] = back
                thin[0], thin[1], thin[2] = t0, t1, t2
            elif i == 0:
                drop_sum[...] = ins[6][...] + down
                e_sum[...] = ins[7][...] + back
                thin[0], thin[1], thin[2] = ins[8][0] + t0, ins[8][1] + t1, ins[8][2] + t2
            else:
                drop_sum[...] += down
                e_sum[...] += back
                thin[0] += t0
                thin[1] += t1
                thin[2] += t2
            per = PANEL // part
            for j, g in enumerate((dot(g_t, gate_grad), dot(l_t, lift_grad), dot(d_t, active))):
                for o in range(per):
                    packed[i * per + o, :, j * part : (j + 1) * part] = g[:, o * part : (o + 1) * part]

    at_chunk = lambda i, p: (chunk, 0, 0)
    operands = [
        (normed, VM), (cot, VM), (hidden_gl, VM), (hidden_d, VM),
        (outer_gl, pl.BlockSpec((None, *outer_gl.shape[1:]), at_chunk)),
        (drop_a, pl.BlockSpec((None, *drop_a.shape[1:]), at_chunk)),
    ]
    if not first:
        operands += [(s, VM) for s in sums]
    return kernel_call(
        body, place, bundle, landing, operands,
        [
            (like((rows, width), F32), VM),
            (like((rows, width), F32), VM),
            (like((3, rows, RANK), F32), VM),
            (like((4, RANK, 3 * part), F32), VM),
        ],
        [], name, time=EST,
    )


def split_by_core(place_ref, whole, keep, send):
    core = place_ref[0] % 2
    for j in range(2):
        keep[j] = whole[core + 2 * j]
        send[j] = whole[1 - core + 2 * j].astype(BF16)


def out_backward(place, bundle, landing, sums, packs, middle, cot, gain, normed, attended, hidden, factors):
    rows, width = middle.shape
    heads = width // HEAD_DIM

    def body(pr, land_refs, ins, outs, weights, sems, scratch):
        chunk_refs, ins = ins[: len(packs)], ins[len(packs) :]
        drop_sum, e_sum, thin, middle_ref, cot_ref, gain_ref, normed_ref, att, hid, drop_b, igl, o_a, o_b = ins
        mixed_kept, mixed_back, mid_grad, out_heads, keep, send = outs
        (w,) = weights
        branch, whole = scratch
        landing = Landing(pr, bundle, land_refs, weights, sems)
        d_hid = thin[0].astype(BF16)
        gl_grad = jnp.concatenate([thin[1].astype(BF16), thin[2].astype(BF16)], axis=1)
        e_in = (e_sum[...] + dot(gl_grad, igl[...])) * gain_ref[...].astype(F32)
        mid = middle_ref[...]
        scale = lax.rsqrt(jnp.mean(mid * mid, axis=-1, keepdims=True) + EPSILON)
        n = mid * scale
        mean = jnp.mean(e_in * n, axis=-1, keepdims=True)
        mid_grad[...] = cot_ref[...].astype(F32) + scale * (e_in - n * mean)
        branch[...] = mid_grad[...].astype(BF16)
        hgrad = dot_nt(branch[...], o_b[...]).astype(BF16)
        landing.wait()
        wide = 8 * HEAD_DIM
        for i in range(heads // 8):
            part = slice(i * wide, (i + 1) * wide)
            grad = dot_nt(branch[...], w[part]) + dot(hgrad, o_a[:, part])
            for h in range(8):
                out_heads[8 * i + h] = padded(grad[:, h * HEAD_DIM : (h + 1) * HEAD_DIM]).astype(BF16)
        mixed = (mid + drop_sum[...] + dot(d_hid, drop_b[...])).astype(BF16)
        mixed_kept[...] = mixed[: rows // 2]
        mixed_back[...] = mixed[rows // 2 :]
        gl = dot(gl_grad.T, normed_ref[...])
        own = (
            dot(d_hid.T, cot_ref[...]), gl[:RANK], gl[RANK:],
            dot(hgrad.T, att[...]), dot(hid[...].T, branch[...]),
        )
        for t in range(4):
            for u, ref in enumerate(chunk_refs):
                whole[t, :, u * chunk_cols : (u + 1) * chunk_cols] = ref[t]
            for j, g in enumerate(own):
                at = len(packs) * chunk_cols + j * quarter
                whole[t, :, at : at + quarter] = g[:, t * quarter : (t + 1) * quarter]
        split_by_core(pr, whole, keep, send)

    quarter = width // 4
    chunk_cols = packs[0].shape[2]
    cols = len(packs) * chunk_cols + 5 * quarter
    return kernel_call(
        body, place, bundle, landing,
        [(v, VM) for v in (*packs, *sums, middle, cot, gain, normed, attended, hidden, *factors)],
        [
            (like((2, rows // 2, width), BF16), one_of_pair(rows // 2, width)),
            (like((rows // 2, width), BF16), VM),
            (like((rows, width), F32), VM),
            (like((heads, rows, LANES), BF16), VM),
            (like((2, RANK, cols), F32), VM),
            (like((2, RANK, cols), BF16), VM),
        ],
        [pltpu.VMEM((rows, width), BF16), pltpu.VMEM((4, RANK, cols), F32)], "out_backward", time=15,
    )


def qkv_gradients(place, parts, cos, sin, normed, hidden, outer):
    rows, width = normed.shape
    total = outer.shape[1]
    kv = (total - width) // 2
    half = HEAD_DIM // 2
    rank3 = outer.shape[0]
    quarter, kv_quarter = width // 4, kv // 4
    cols = 4 * quarter + 2 * kv_quarter
    q_count, kv_count = parts[0][0].shape[0], parts[0][1].shape[1]

    def body(pr, land_refs, ins, outs, weights, sems, scratch):
        *part_refs, cos_ref, sin_ref, nrm, hid, b = ins
        dq_refs, dkv_refs, got_refs = part_refs[0::3], part_refs[1::3], part_refs[2::3]
        g, hgrad_ref, keep, send = outs
        (whole,) = scratch
        for h in range(width // HEAD_DIM):
            ref, i = dq_refs[h // q_count], h % q_count
            g[:, h * HEAD_DIM : (h + 1) * HEAD_DIM] = ref[i, :, :HEAD_DIM]
        for h in range(kv // HEAD_DIM):
            dkv_ref, got_ref, i = dkv_refs[h // kv_count], got_refs[h // kv_count], h % kv_count
            one = (dkv_ref[0, i] + got_ref[0, i].astype(F32))[:, :HEAD_DIM]
            at = width + h * HEAD_DIM
            g[:, at : at + HEAD_DIM] = turn(one, cos_ref[...], -sin_ref[...], half).astype(BF16)
            at += kv
            g[:, at : at + HEAD_DIM] = (dkv_ref[1, i] + got_ref[1, i].astype(F32))[:, :HEAD_DIM].astype(BF16)
        hgrad_ref[...] = dot_nt(g[...], b[...]).astype(BF16)
        g_in = dot(hgrad_ref[...].T, nrm[...])
        g_out = dot(hid[...].T, g[...])
        for t in range(4):
            for i in range(3):
                whole[t, :, i * quarter : (i + 1) * quarter] = g_in[
                    i * RANK : (i + 1) * RANK, t * quarter : (t + 1) * quarter
                ]
            whole[t, :, 3 * quarter : 4 * quarter] = g_out[:RANK, t * quarter : (t + 1) * quarter]
            for i in range(2):
                at, start = 4 * quarter + i * kv_quarter, width + i * kv + t * kv_quarter
                whole[t, :, at : at + kv_quarter] = g_out[
                    (1 + i) * RANK : (2 + i) * RANK, start : start + kv_quarter
                ]
        split_by_core(pr, whole, keep, send)

    return kernel_call(
        body, place, NO_BUNDLE, [],
        [(v, VM) for v in (*[v for p in parts for v in p], cos, sin, normed, hidden, outer)],
        [
            (like((rows, total), BF16), VM),
            (like((rows, rank3), BF16), VM),
            (like((2, RANK, cols), F32), VM),
            (like((2, RANK, cols), BF16), VM),
        ],
        [pltpu.VMEM((4, RANK, cols), F32)], "qkv_gradients", time=10,
    )


def qkv_backward(place, bundle, landing, g, hgrad, x, mid_grad, gain, inner, ties):
    rows, width = x.shape
    total = bundle.shapes[0][1]
    block = rows // 2

    def body(pr, land_refs, ins, outs, weights, sems, scratch):
        g_ref, hg, x_ref, mg, gain_ref, a = ins
        kept, back = outs
        (w,) = weights
        landing = Landing(pr, bundle, land_refs, weights, sems)
        xf = x_ref[...].astype(F32)
        scale = lax.rsqrt(jnp.mean(xf * xf, axis=-1, keepdims=True) + EPSILON)
        n = xf * scale
        thin = dot(hg[...], a[...])
        landing.wait()
        e_in = (dot_nt(g_ref[...], w[...]) + thin) * gain_ref[...].astype(F32)
        mean = jnp.mean(e_in * n, axis=-1, keepdims=True)
        result = mg[...] + scale * (e_in - n * mean)
        kept[...] = result[:block]
        back[...] = result[block:].astype(BF16)

    return kernel_call(
        body, place, bundle, landing,
        [(v, VM) for v in (g, hgrad, x, mid_grad, gain, inner)],
        [(like((2, block, width), F32), one_of_pair(block, width)), (like((block, width), BF16), VM)],
        [], "qkv_backward", time=14, ties=ties,
    )


def complete(place, partial, back, ties, name):
    _, block, width = partial.shape

    def kernel(place_ref, partial_ref, back_ref, *rest):
        rest[-1][...] = back_ref[...].astype(partial.dtype)

    return pl.pallas_call(
        kernel,
        out_shape=jax.ShapeDtypeStruct(partial.shape, partial.dtype),
        grid_spec=pltpu.PrefetchScalarGridSpec(
            num_scalar_prefetch=1,
            grid=(1,),
            in_specs=[pl.BlockSpec(memory_space=pltpu.HBM), pl.BlockSpec(memory_space=pltpu.VMEM)]
            + [pl.BlockSpec(memory_space=pltpu.HBM)] * len(ties),
            out_specs=pl.BlockSpec((None, block, width), lambda i, p: (1 - p[0] // 2, 0, 0)),
        ),
        input_output_aliases={1: 0},
        compiler_params=pltpu.CompilerParams(vmem_limit_bytes=64 * 2**20),
        cost_estimate=work(2),
        name=name,
    )(place, partial, back, *ties)


def pack_factors(place, inners, outers):
    widths = [a.shape[0] for a in inners] + [b.shape[1] for b in outers]
    n = len(inners)
    mix = outers[0].shape[0]
    narrow = (n + 1, n + 2)

    def body(pr, land_refs, ins, outs, weights, sems, scratch):
        for which, out in enumerate(outs):
            row = lax.broadcasted_iota(jnp.int32, (RANK, mix), 0) + pr[3 + which] * RANK
            choose = (row == lax.broadcasted_iota(jnp.int32, (RANK, mix), 1)).astype(F32).astype(BF16)
            at = 0
            for i, ref in enumerate(ins):
                part = dot_nt(choose, ref[...]) if i < n or i in narrow else dot(choose, ref[...])
                out[:, at : at + widths[i]] = part.astype(BF16)
                at += widths[i]

    shape = (like((RANK, sum(widths)), BF16), VM)
    return kernel_call(
        body, place, NO_BUNDLE, [], [(v.T if i in narrow else v, VM) for i, v in enumerate((*inners, *outers))],
        [shape, shape], [], "pack_factors",
    )


def unpack_factors(place, slots, widths, chunks):
    inner_w, outer_w = widths[:7], widths[7:]
    width, kv = 4 * outer_w[0], 4 * outer_w[1]
    part = outer_w[4] // chunks
    starts = [sum(widths[:i]) for i in range(len(widths))]

    def body(pr, land_refs, ins, outs, weights, sems, scratch):
        iq, oq, io, oo, igl, ogl, da, db = outs
        (nat,) = scratch
        mine, two, got = ins
        nat[pr[0]] = mine[...]
        nat[pr[0] ^ 2] = two[...]
        nat[pr[0] ^ 1] = got[:RANK]
        nat[pr[0] ^ 3] = got[RANK:]
        oq[...] = jnp.zeros(oq.shape, BF16)
        for t in range(4):
            get = lambda i, a=0, n=None: nat[t, :, starts[i] + a : starts[i] + a + (n or widths[i])]
            w = inner_w[0]
            here = slice(t * w, (t + 1) * w)
            for i in range(3):
                iq[i * RANK : (i + 1) * RANK, here] = get(i)
            io[:, here] = get(3)
            igl[:RANK, here] = get(4)
            igl[RANK:, here] = get(5)
            base = 0
            for i in range(3):
                n = outer_w[i]
                oq[i * RANK : (i + 1) * RANK, base + t * n : base + (t + 1) * n] = get(7 + i)
                base += 4 * n
            oo[:, here] = get(10)
            db[:, here] = get(13)
            for u in range(chunks):
                there = slice(t * part, (t + 1) * part)
                ogl[u, :RANK, there] = get(11, u * part, part)
                ogl[u, RANK:, there] = get(12, u * part, part)
                da[u, :, there] = get(6, u * part, part)

    shapes = [
        (3 * RANK, width), (3 * RANK, width + 2 * kv), (RANK, width), (RANK, width), (2 * RANK, width),
        (chunks, 2 * RANK, 4 * part), (chunks, RANK, 4 * part), (RANK, width),
    ]
    return kernel_call(
        body, place, NO_BUNDLE, [], [(v, VM) for v in slots], [(like(sh, BF16), VM) for sh in shapes],
        [pltpu.VMEM((4, *slots[0].shape), BF16)], "unpack_factors",
    )


def fold_cores(place, keep, got, name):
    _, rank, cols = keep.shape

    def body(pr, land_refs, ins, outs, weights, sems, scratch):
        keep_ref, got_ref = ins
        chip = pr[0] // 2
        for out, which in zip(outs, (chip, 1 - chip)):
            out[:, :cols] = (keep_ref[which] + got_ref[which].astype(F32)).astype(BF16)
            out[:, cols:] = jnp.full((rank, LANES), pr[3], jnp.int32).astype(F32).astype(BF16)

    shape = (like((rank, cols + LANES), BF16), VM)
    return kernel_call(
        body, place, NO_BUNDLE, [], [(keep, VM), (got, VM)], [shape, shape], [], name
    )


def spread_sums(place, gathered, pieces, mix, name, ties=()):
    count = sum(v.shape[0] for v in gathered)
    cols = gathered[0].shape[1] - LANES

    def body(pr, land_refs, ins, outs, weights, sems, scratch):
        if len(ins) == 1:
            got = ins[0]
        else:
            (got,) = scratch
            at = 0
            for ref in ins:
                got[at : at + ref.shape[0]] = ref[...]
                at += ref.shape[0]
        tag = got[:, cols:].astype(F32).astype(jnp.int32) * RANK
        spot = tag + lax.broadcasted_iota(jnp.int32, (count, LANES), 0) % RANK
        choose = (spot == lax.broadcasted_iota(jnp.int32, (count, LANES), 1)).astype(F32).astype(BF16)
        choose_t = choose.T
        for out, (is_inner, runs) in zip(outs, pieces):
            at = 0
            for start, n in runs:
                if is_inner:
                    out[at : at + n] = dot_tn(got[:, start : start + n], choose)
                else:
                    out[:, at : at + n] = dot(choose_t, got[:, start : start + n])
                at += n

    outs = []
    for is_inner, runs in pieces:
        n = sum(c for _, c in runs)
        outs.append((like((n, mix) if is_inner else (mix, n), F32), VM))
    scratch = [pltpu.VMEM((count, cols + LANES), BF16)] if len(gathered) > 1 else []
    return kernel_call(
        body, place, NO_BUNDLE, [], [(v, VM) for v in gathered], outs, scratch, name, ties=ties
    )


def local(
    tokens,
    cotangent,
    prefix_len,
    adapter_index,
    gain_attn,
    gain_mlp,
    query_weight,
    key_weight,
    value_weight,
    output_weight,
    gate_weight,
    lift_weight,
    drop_weight,
    *factors,
):
    _, block, width = tokens.shape
    rep, shard = lax.axis_index("rep"), lax.axis_index("shard")
    chip = shard // 2
    rows = 2 * block
    kv_width = KV_HEADS * HEAD_DIM
    where = jnp.stack([shard, rep % 4]).astype(jnp.int32)
    place = jnp.concatenate(
        [where, jnp.stack([prefix_len[chip], adapter_index[chip], adapter_index[1 - chip]])]
    )

    weights = (query_weight, key_weight, value_weight, output_weight, gate_weight, lift_weight, drop_weight)
    inners, outers = factors[0::2], factors[1::2]
    widths = [a.shape[0] for a in inners] + [b.shape[1] for b in outers]
    chunks = 4
    ff = gate_weight.shape[1]
    bundles = make_bundles(width, kv_width, ff, chunks, 4)
    relay = Relay(where, weights, bundles)
    half = block // 2
    relay.step()
    mine, others = pack_factors(place, inners, outers)
    slot_two = to_chip(others)
    (tokens_a,), _ = relay.step([(tokens, 0, half)])
    got = to_core(jnp.concatenate([mine, slot_two], axis=0))
    (tokens_b,), _ = relay.step([(tokens, half, half)], ties=(slot_two, tokens_a))
    relay.step(ties=(tokens_b,))
    inner_qkv, outer_qkv, inner_o, outer_o, inner_gl, outer_gl, drop_a, drop_b = unpack_factors(
        place, (mine, slot_two, got), widths, chunks
    )
    positions = jnp.concatenate(
        [shard * block + jnp.arange(block), (shard ^ 3) * block + jnp.arange(block)]
    )
    cos_table, sine_table = rotary_tables(positions.astype(F32), HEAD_DIM)
    cos_full = jnp.concatenate([cos_table, cos_table], axis=1)
    sin_full = jnp.concatenate([-sine_table, sine_table], axis=1)
    gain_one, gain_two = gain_attn[None], gain_mlp[None]

    def landing(i):
        return landing_operands(bundles[i], weights, relay.here[i], relay.there[i])

    (cot_a,), begun = relay.step([(cotangent, 0, half)], ties=(got,))
    queries, kv_own, hidden_qkv, normed_attn, x = qkv_forward(
        place, bundles[0], landing(0), tokens, (tokens_a, tokens_b), gain_one,
        inner_qkv, outer_qkv, cos_full, sin_full, (begun[0], relay.there[1]),
    )
    (cot_b,), begun = relay.step([(cotangent, half, half)], ties=(x, cot_a))
    kv_own = gate(kv_own, begun[:1])
    kv_near = to_core(kv_own)
    heads_out, lse = attend(place, queries, kv_own, kv_near)
    middle, normed_mlp, attended, output_hidden, cot, hidden_gl, hidden_d = out_forward(
        place, bundles[1], landing(1), heads_out, x, gain_two, inner_o, outer_o,
        cotangent, (cot_a, cot_b), inner_gl, drop_b,
    )
    relay.step(ties=(normed_mlp,))
    sums, packs = None, []
    for u in range(chunks):
        *sums, packed = mlp_chunk(
            place, bundles[2 + u], landing(2 + u), normed_mlp, cot, hidden_gl, hidden_d,
            outer_gl, drop_a, u, sums, f"mlp_{u}",
        )
        packs.append(packed)
        if u < 2:
            relay.step(ties=(packed,))
    mixed_kept, mixed_back, middle_grad, grad_heads, keep, send = out_backward(
        place, bundles[1], landing(1), sums, packs, middle, cot, gain_two, normed_mlp, attended,
        output_hidden, (drop_b, inner_gl, inner_o, outer_o),
    )

    def both_chips(own, other):
        return jnp.concatenate([own, to_chip(other)], axis=0)

    mixed_back = to_diag(mixed_back)
    mixed = complete(place, mixed_kept, mixed_back, (), "complete_mixed")
    folded = fold_cores(place, keep, to_core(send), "fold_late")
    parts, halves = [], 2
    for i in range(halves):
        dq, dkv, dkv_send = attend_back(
            place, queries, kv_own, kv_near, grad_heads, lse, cos_table.T, sine_table.T, i, halves,
            folded if i else (),
        )
        if i:
            late = both_chips(*folded)
            dkv_send = gate(dkv_send, (late, mixed_back))
        parts.append((dq, dkv, to_core(dkv_send)))
    late = lax.all_gather(late, "rep", axis=0, tiled=True)
    g, hgrad, keep, send = qkv_gradients(
        place, parts, cos_full, sin_full, normed_attn, hidden_qkv, outer_qkv
    )
    folded = fold_cores(place, keep, to_core(send), "fold_first")
    both = both_chips(*folded)
    input_kept, input_back = qkv_backward(
        place, bundles[0], landing(0), g, hgrad, x, middle_grad, gain_one, inner_qkv, folded[:1]
    )
    input_back = to_diag(gate(input_back, (both,)))
    pair = jnp.concatenate([both, to_y(both)], axis=0)
    first = [pair]
    for k in range(2, lax.axis_size("rep"), 2):
        first.append(move(pair, lambda r, s, k=k: (r ^ k, s)))

    mix = ADAPTERS * RANK
    w, kw = width // 4, kv_width // 4
    part = ff // 4 // chunks
    runs = lambda j: [(u * 3 * part + j * part, part) for u in range(chunks)]
    base = chunks * 3 * part
    g_out, l_out, d_in, d_out, g_in, l_in, o_in, o_out = spread_sums(
        place, [late],
        [(False, runs(0)), (False, runs(1)), (True, runs(2)), (False, [(base, w)]), (True, [(base + w, w)]),
         (True, [(base + 2 * w, w)]), (True, [(base + 3 * w, w)]), (False, [(base + 4 * w, w)])],
        mix, "spread_late",
    )
    input_grad = complete(place, input_kept, input_back, (), "complete_input_grad")
    q_in, k_in, v_in, q_out, k_out, v_out = spread_sums(
        place, first,
        [(True, [(0, w)]), (True, [(w, w)]), (True, [(2 * w, w)]), (False, [(3 * w, w)]),
         (True, [(4 * w, kw)]), (True, [(4 * w + kw, kw)])],
        mix, "spread_first", (o_out, input_grad),
    )
    k_out, v_out = k_out.T, v_out.T
    return (mixed, input_grad, q_in, q_out, k_in, k_out, v_in, v_out, o_in, o_out,
            g_in, g_out, l_in, l_out, d_in, d_out)


def solution(mesh):
    token_place = P("rep", "shard", None)
    row, col = P("shard", None), P(None, "shard")
    return jax.shard_map(
        local,
        mesh=mesh,
        in_specs=(token_place, token_place, P("rep"), P("rep"), P(), P()) + (row,) * 7 + (row, col) * 7,
        out_specs=(token_place, token_place) + (row, col) * 7,
        check_vma=False,
    )
```

```python
import functools
import math
from typing import NamedTuple

import jax
import jax.numpy as jnp
from jax import lax
from jax.experimental import pallas as pl
from jax.experimental.pallas import tpu as pltpu
from jax.sharding import PartitionSpec as P

HEADS = 16
KV_HEADS = 8
HEAD_DIM = 96
RANK = 16
ADAPTERS = 8
EPSILON = 1e-05
ROPE_BASE = 100000.0
MASKED_SCORE = -1e30
AXES = ("rep", "shard")
F32 = jnp.float32
BF16 = jnp.bfloat16


def move(value, target):
    reps, shards = lax.axis_size("rep"), lax.axis_size("shard")
    pairs = []
    for r in range(reps):
        for s in range(shards):
            r2, s2 = target(r, s)
            pairs.append((r * shards + s, r2 * shards + s2))
    return lax.ppermute(value, AXES, pairs)


def to_core(value):
    return move(value, lambda r, s: (r, s ^ 1))


def to_chip(value):
    return move(value, lambda r, s: (r, s ^ 2))


def to_y(value):
    return move(value, lambda r, s: (r ^ 1, s))


def to_z(value):
    return move(value, lambda r, s: (r ^ 2, s))


PANEL = 512
LANES = 128
EST = 5
PACK_EST = 0.1


class Piece(NamedTuple):
    parts: tuple
    row: int
    rows: int
    target: int
    block: int
    to_row: int
    to_col: int


class Bundle(NamedTuple):
    first: tuple
    second: tuple
    shapes: tuple
    joined: bool = True


def quarter_rows(pieces):
    return sum(p.rows for p in pieces) // 4


def make_bundles(width, kv_width, ff, chunks, shards):
    rows, drop_rows = width // shards, ff // shards // chunks
    panels = width // PANEL
    first = tuple(Piece(((0, c, PANEL),), 0, rows, 0, rows, 0, c) for c in range(0, width, PANEL))
    second = []
    for c in range(0, 2 * kv_width, PANEL):
        parts, at = [], c
        while at < c + PANEL:
            source = 1 if at < kv_width else 2
            base = (source - 1) * kv_width
            stop = min(c + PANEL, base + kv_width)
            parts.append((source, at - base, stop - at))
            at = stop
        second.append(Piece(tuple(parts), 0, rows, 0, rows, 0, width + c))
    found = [Bundle(first, tuple(second), ((width, width + 2 * kv_width),))]

    def halves(source, row, height, target, block):
        return [
            tuple(
                Piece(((source, i * PANEL, PANEL),), row + h * height // 2, height // 2, target, block,
                      h * height // 2, i * PANEL)
                for i in range(panels)
            )
            for h in range(2)
        ]

    top, bottom = halves(3, 0, rows, 0, rows)
    found.append(Bundle(top, bottom, ((width, width),)))
    part = ff // shards // chunks
    for u in range(chunks):
        sides = []
        for j in range(2):
            side = []
            for c in range(0, shards * part, PANEL):
                parts = tuple(
                    (4 + j, t * (ff // shards) + u * part, part)
                    for t in range(c // part, (c + PANEL) // part)
                )
                side.append(Piece(parts, 0, rows, 0, rows, 0, 2 * c + j * PANEL))
            sides.append(tuple(side))
        top, bottom = halves(6, u * drop_rows, drop_rows, 1, drop_rows)
        cols = shards * part
        found.append(
            Bundle(sides[0] + top, sides[1] + bottom, ((width, 2 * cols), (cols, width)), False)
        )
    return found


def work(microseconds):
    return pl.CostEstimate(flops=int(microseconds * 1.1e9), bytes_accessed=2**20, transcendentals=0)


def pack(place, jobs, operands, out_shapes, name):
    n_in, n_out = len(operands), len(out_shapes)

    def kernel(place_ref, *refs):
        ins, refs = refs[:n_in], refs[n_in:]
        outs, held, sems = refs[:n_out], refs[n_out : 2 * n_out], refs[-1]
        arriving, leaving = [], []
        for i, (src, o, *spot) in enumerate(jobs(place_ref, ins)):
            here = held[o].at[tuple(spot)]
            arriving.append(pltpu.make_async_copy(src, here, sems.at[0, i]))
            leaving.append(pltpu.make_async_copy(here, outs[o].at[tuple(spot)], sems.at[1, i]))
        for c in arriving:
            c.start()
        for c, d in zip(arriving, leaving):
            c.wait()
            d.start()
        for d in leaving:
            d.wait()

    class Fake:
        def __init__(self):
            self.at = self

        def __getitem__(self, _):
            return self

    count = len(jobs(None, [Fake()] * n_in))
    hbm = pl.BlockSpec(memory_space=pltpu.HBM)
    return pl.pallas_call(
        kernel,
        out_shape=[jax.ShapeDtypeStruct(sh, BF16) for sh in out_shapes],
        grid_spec=pltpu.PrefetchScalarGridSpec(
            num_scalar_prefetch=1,
            grid=(1,),
            in_specs=[hbm] * n_in,
            out_specs=[hbm] * n_out,
            scratch_shapes=[pltpu.VMEM(sh, BF16) for sh in out_shapes]
            + [pltpu.SemaphoreType.DMA((2, count))],
        ),
        compiler_params=pltpu.CompilerParams(vmem_limit_bytes=64 * 2**20),
        cost_estimate=work(PACK_EST),
        name=name,
    )(place, *operands)


def gate(value, ties):
    return pl.pallas_call(
        lambda *refs: None,
        out_shape=jax.ShapeDtypeStruct(value.shape, value.dtype),
        in_specs=[pl.BlockSpec(memory_space=pltpu.HBM)] * (1 + len(ties)),
        out_specs=pl.BlockSpec(memory_space=pltpu.HBM),
        input_output_aliases={0: 0},
        compiler_params=pltpu.CompilerParams(vmem_limit_bytes=64 * 2**20),
        name="gate",
    )(value, *ties)


def join(*parts, ties=()):
    cols = parts[0].shape[1]

    def kernel(*refs):
        at = 0
        for ref in refs[: len(parts)]:
            refs[-1][at : at + ref.shape[0]] = ref[...]
            at += ref.shape[0]

    return pl.pallas_call(
        kernel,
        out_shape=jax.ShapeDtypeStruct((sum(p.shape[0] for p in parts), cols), parts[0].dtype),
        in_specs=[pl.BlockSpec(memory_space=pltpu.VMEM)] * len(parts)
        + [pl.BlockSpec(memory_space=pltpu.HBM)] * len(ties),
        compiler_params=pltpu.CompilerParams(vmem_limit_bytes=64 * 2**20),
        cost_estimate=work(1),
        name="join",
    )(*parts, *ties)


def quarter_start(place_ref, flip, rows):
    if place_ref is None:
        return 0
    return pl.multiple_of((place_ref[1] ^ flip) * rows, 16)


class Relay:
    def __init__(self, place, weights, bundles):
        self.place, self.weights, self.bundles = place, weights, bundles
        self.direct, self.once, self.twice = {}, {}, {}
        self.here, self.there = {}, {}
        self.tick = 0

    def step(self, extra=(), ties=(), across=True):
        t, bundles = self.tick, self.bundles
        self.tick += 1
        operands, shapes, kinds, sent = [], [], [], []

        def operand(array):
            for i, o in enumerate(operands):
                if o is array:
                    return i
            operands.append(array)
            return len(operands) - 1

        plans = []

        def out(kind, rows, cols=PANEL):
            shapes.append((rows, cols))
            kinds.append(kind)
            return len(shapes) - 1

        if t < len(bundles):
            b = bundles[t]
            base = quarter_rows(b.first + b.second)
            o = out("x", base + sum(n * a.shape[2] // PANEL for a, _, n in extra))
            for array, start, count in extra:
                i = operand(array)
                sent.append((base, count))

                def plan_t(pr, ins, o=o, i=i, start=start, count=count, base=base, cols=array.shape[2]):
                    which = 0 if pr is None else 1 - pr[0] // 2
                    return [
                        (ins[i].at[which, pl.ds(start, count), pl.ds(c, PANEL)], o,
                         pl.ds(base + c // PANEL * count, count), slice(None))
                        for c in range(0, cols, PANEL)
                    ]

                plans.append(plan_t)
                base += count * array.shape[2] // PANEL
            used = [(operand(self.weights[q[0]]), q, p) for p in b.first + b.second for q in p.parts]

            def plan_x(pr, ins, o=o, used=used):
                copies, at, col = [], 0, 0
                for i, (_, c, n), p in used:
                    q = p.rows // 4
                    rows = pl.ds(pl.multiple_of(p.row + quarter_start(pr, 0, q), 16), q)
                    copies.append((ins[i].at[rows, pl.ds(c, n)],
                                   o, pl.ds(at, q), pl.ds(col, n)))
                    col += n
                    if col == PANEL:
                        at, col = at + q, 0
                return copies

            plans.append(plan_x)
        y_parts, z_parts = [], []
        b1, b2, b3 = t - 1, t - 2, t - 3
        if 0 <= b1 < len(bundles):
            qa, qb = quarter_rows(bundles[b1].first), quarter_rows(bundles[b1].second)
            y_parts.append(("first", b1, [(self.direct[b1], 0, qa)]))
            z_parts.append(("first", b1, [(self.direct[b1], qa, qb)]))
        if 0 <= b2 < len(bundles):
            qa, qb = quarter_rows(bundles[b2].first), quarter_rows(bundles[b2].second)
            (ya, yo), (za, zo) = self.once[b2]
            y_parts.append(("second", b2, [(self.direct[b2], qa, qb), (za, zo, qb)]))
            z_parts.append(("second", b2, [(self.direct[b2], 0, qa), (ya, yo, qa)]))
        for kind, parts in (("y", y_parts), ("z", z_parts)):
            if not parts:
                continue
            total = sum(n for _, _, l in parts for _, _, n in l)
            o = out(kind, total)
            flat = [(operand(a), r, n) for _, _, l in parts for a, r, n in l]

            def plan_n(pr, ins, o=o, flat=flat):
                copies, at = [], 0
                for i, r, n in flat:
                    copies.append((ins[i].at[pl.ds(r, n)], o, pl.ds(at, n), slice(None)))
                    at += n
                return copies

            plans.append(plan_n)
        for tie in ties:
            operand(tie)

        def jobs(pr, ins):
            return [c for plan in plans for c in plan(pr, ins)]

        bufs = pack(self.place, jobs, operands, shapes, f"pack_{t}") if shapes else []
        for kind, buf in zip(kinds, bufs):
            if kind == "x":
                self.direct[t] = to_chip(buf)
            else:
                got = (to_y if kind == "y" else to_z)(buf)
                at = 0
                for stage, bi, l in y_parts if kind == "y" else z_parts:
                    store = self.once if stage == "first" else self.twice
                    pair = store.setdefault(bi, [None, None])
                    pair[0 if kind == "y" else 1] = (got, at)
                    at += sum(n for _, _, n in l)
        if 0 <= b3 < len(bundles) and across:
            self.across(b3, bufs[:1] if bufs else ties)
        return [(self.direct[t], *spot) for spot in sent], bufs

    def across(self, b3, ties):
        b = self.bundles[b3]
        operands, shapes = [], []

        def operand(array):
            for i, o in enumerate(operands):
                if o is array:
                    return i
            operands.append(array)
            return len(operands) - 1

        plans = []

        def out(kind, rows, cols=PANEL):
            shapes.append((rows, cols))
            return len(shapes) - 1

        total = 4 * quarter_rows(b.first + b.second)
        o = out("c", (2 if b.joined else 1) * total)
        used = [
            (operand(self.weights[q[0]]), q, p)
            for p in (b.first + b.second if b.joined else ()) for q in p.parts
        ]
        qa = quarter_rows(b.first)
        qb = quarter_rows(b.second)
        (ya, yo), (za, zo) = self.once[b3]
        (ys, yso), (zs, zso) = self.twice[b3]
        d = operand(self.direct[b3])
        sides = [
            (b.first, [(0, d, 0), (1, operand(ya), yo), (2, operand(zs), zso), (3, operand(zs), zso + qa)]),
            (b.second, [(0, d, qa), (2, operand(za), zo), (1, operand(ys), yso), (3, operand(ys), yso + qb)]),
        ]

        def plan_c(pr, ins, o=o, sides=sides, used=used, total=total):
            copies, base, at, col = [], total if b.joined else 0, 0, 0
            for i, (_, c, n), p in used:
                copies.append((ins[i].at[pl.ds(p.row, p.rows), pl.ds(c, n)],
                               o, pl.ds(at, p.rows), pl.ds(col, n)))
                col += n
                if col == PANEL:
                    at, col = at + p.rows, 0
            for pieces, quarters in sides:
                at = 0
                for p in pieces:
                    q = p.rows // 4
                    for flip, i, r in quarters:
                        to = pl.multiple_of(base + quarter_start(pr, flip, q), 16)
                        copies.append((ins[i].at[pl.ds(r + at, q)], o, pl.ds(to, q), slice(None)))
                    at += q
                    base += p.rows
            return copies

        plans.append(plan_c)

        for tie in ties:
            operand(tie)
        jobs = lambda pr, ins: plans[0](pr, ins)
        (buf,) = pack(self.place, jobs, operands, shapes, f"across_{b3}")
        self.here[b3], self.there[b3] = buf, to_core(buf)


def land_copies(place_ref, bundle, own, near, here, there, targets):
    copies = []
    shard = 0 if place_ref is None else place_ref[0]
    pieces = bundle.first + bundle.second
    total = sum(p.rows for p in pieces)
    skip = total if bundle.joined else 0
    for slot, (ref, base) in enumerate(((None, 0), (there, 0), (here, skip), (there, skip))):
        for p in pieces:
            to = (shard ^ slot) * p.block + p.to_row
            to = pl.ds(pl.multiple_of(to, 16), p.rows)
            dst = targets[p.target]
            key = (p.target, p.to_col)
            if slot == 0 or slot == 1 and not bundle.joined:
                col = p.to_col
                for source, c, n in p.parts:
                    copies.append(((near if slot else own)[source].at[pl.ds(p.row, p.rows), pl.ds(c, n)],
                                   dst.at[to, pl.ds(col, n)], key))
                    col += n
            else:
                copies.append((ref.at[pl.ds(base, p.rows)], dst.at[to, pl.ds(p.to_col, PANEL)], key))
            base += p.rows
    return copies


def sources_of(bundle):
    return sorted({q[0] for p in bundle.first + bundle.second for q in p.parts})


def rotary_tables(positions, head_dim):
    half_dim = head_dim // 2
    freq_index = jnp.arange(half_dim).astype(F32)
    frequency = jnp.exp(freq_index * (-2.0 * math.log(ROPE_BASE) / head_dim))
    angles = positions[:, None] * frequency[None, :]
    return jnp.cos(angles), jnp.sin(angles)


def dot(left, right):
    return jnp.dot(left, right, preferred_element_type=F32)


def dot_nt(left, right):
    return lax.dot_general(left, right, (((1,), (1,)), ((), ())), preferred_element_type=F32)


def dot_tn(left, right):
    return lax.dot_general(left, right, (((0,), (0,)), ((), ())), preferred_element_type=F32)


LOG2E = 1.4426950408889634


def last_visible(place_ref, low, lanes, block):
    shard, prefix = place_ref[0], place_ref[2]
    at = shard % 2 if low else 2 + shard % 2
    position = at * block + lax.broadcasted_iota(jnp.int32, (1, lanes), 1) % block
    return jnp.maximum(position + 1, prefix)


def query_start(place_ref, low, block):
    chip = place_ref[0] // 2
    return pl.multiple_of((chip if low else 1 - chip) * block, block)


def natural_rows(place_ref, own, near, into, block):
    shard = place_ref[0]
    for slot, value in (
        (0, own[0, :block]),
        (2, own[0, block:]),
        (1, near[0, :block]),
        (3, near[0, block:]),
    ):
        into[pl.ds(pl.multiple_of((shard ^ slot) * block, block), block)] = value


def hide(scores, limit, first_key):
    keys = first_key + lax.broadcasted_iota(jnp.int32, scores.shape, 0)
    return jnp.where(keys < limit, scores, MASKED_SCORE)


def masked_by_part(low, scores, limit, block):
    if low:
        return hide(scores, limit, 0)
    half = 2 * block
    return jnp.concatenate([scores[:half], hide(scores[half:], limit, half)], axis=0)


def attend_kernel(place, q, k_own, k_near, v_own, v_near, out, lse, keys, values, *, scale):
    block = q.shape[1] // 2
    group = q.shape[0]
    natural_rows(place, k_own, k_near, keys, block)
    natural_rows(place, v_own, v_near, values, block)
    values_t = values[...].T
    for part, low in enumerate((True, False)):
        count = (2 if low else 4) * block
        rows = pl.ds(query_start(place, low, block), block)
        query = jnp.concatenate([q[j, rows] for j in range(group)], axis=0)
        limit = last_visible(place, low, group * block, block)
        scores = masked_by_part(low, dot_nt(keys[:count], query), limit, block)
        top = jnp.max(scores, axis=0, keepdims=True)
        base = scale * LOG2E
        expo = jnp.exp2(scores * base - top * base)
        total = jnp.sum(expo, axis=0, keepdims=True)
        lse[0, part] = (top * base + jnp.log2(total))[0]
        result = dot(values_t[:, :count], expo.astype(BF16)) / total
        result = result.T.astype(BF16)
        for j in range(group):
            out[j, rows] = result[j * block : (j + 1) * block]


def attend(place, queries, kv_own, kv_near):
    heads, rows, dim = queries.shape
    kv_heads = kv_own.shape[0] // 2
    group = heads // kv_heads
    q_spec = pl.BlockSpec((group, rows, dim), lambda g, p: (g, 0, 0))
    kv_spec = pl.BlockSpec((1, rows, dim), lambda g, p: (g, 0, 0))
    v_spec = pl.BlockSpec((1, rows, dim), lambda g, p: (g + kv_heads, 0, 0))
    lse_shape = (kv_heads, 2, group * rows // 2)
    return pl.pallas_call(
        functools.partial(attend_kernel, scale=HEAD_DIM ** (-0.5)),
        out_shape=[
            jax.ShapeDtypeStruct(queries.shape, BF16),
            jax.ShapeDtypeStruct(lse_shape, F32),
        ],
        grid_spec=pltpu.PrefetchScalarGridSpec(
            num_scalar_prefetch=1,
            grid=(kv_heads,),
            in_specs=[q_spec, kv_spec, kv_spec, v_spec, v_spec],
            out_specs=[q_spec, pl.BlockSpec((1, *lse_shape[1:]), lambda g, p: (g, 0, 0))],
            scratch_shapes=[pltpu.VMEM((2 * rows, dim), BF16)] * 2,
        ),
        compiler_params=pltpu.CompilerParams(vmem_limit_bytes=64 * 2**20),
        cost_estimate=work(EST),
        name="attend",
    )(place, queries, kv_own, kv_near, kv_own, kv_near)


def attend_back_kernel(
    place, q, k_own, k_near, v_own, v_near, grad, lse, cos_t, sin_t, *rest, scale
):
    dq, own_out, send_out, keys, values, dk, dv = rest[-7:]
    block = q.shape[1] // 2
    group = q.shape[0]
    half = HEAD_DIM // 2
    natural_rows(place, k_own, k_near, keys, block)
    natural_rows(place, v_own, v_near, values, block)
    keys_t = keys[...].T
    for part, low in ((1, False), (0, True)):
        count = (2 if low else 4) * block
        start = query_start(place, low, block)
        rows = pl.ds(start, block)
        query = jnp.concatenate([q[j, rows] for j in range(group)], axis=0)
        out_grad = jnp.concatenate([grad[j, rows] for j in range(group)], axis=0)
        limit = last_visible(place, low, group * block, block)
        scores = masked_by_part(low, dot_nt(keys[:count], query), limit, block)
        probs = jnp.exp2(scores * (scale * LOG2E) - lse[0, part][None])
        probs_grad = dot_nt(values[:count], out_grad)
        mean = jnp.sum(probs * probs_grad, axis=0, keepdims=True)
        score_grad = (probs * (probs_grad - mean)).astype(BF16)
        v_part = dot(probs.astype(BF16), out_grad)
        k_part = dot(score_grad, query) * scale
        if low:
            dk[:count] += k_part
            dv[:count] += v_part
        else:
            dk[...] = k_part
            dv[...] = v_part
        turned = dot(keys_t[:, :count], score_grad) * scale
        cos = jnp.concatenate([cos_t[:, rows]] * group, axis=1)
        sin = jnp.concatenate([sin_t[:, rows]] * group, axis=1)
        u, w = turned[:half], turned[half : 2 * half]
        pad = jnp.zeros((q.shape[2] - 2 * half, u.shape[1]), F32)
        turned = jnp.concatenate([u * cos + w * sin, w * cos - u * sin, pad], axis=0)
        turned = turned.T.astype(BF16)
        for j in range(group):
            dq[j, rows] = turned[j * block : (j + 1) * block]
    shard = place[0]
    for slot, at, own in ((0, 0, True), (2, 1, True), (1, 0, False), (3, 1, False)):
        rows = pl.ds(pl.multiple_of((shard ^ slot) * block, block), block)
        to = slice(at * block, (at + 1) * block)
        out = own_out if own else send_out
        out[0, 0, to] = dk[rows].astype(out.dtype)
        out[1, 0, to] = dv[rows].astype(out.dtype)


def attend_back(place, queries, kv_own, kv_near, grad, lse, cos_t, sin_t, part, parts, ties):
    heads, rows, dim = queries.shape
    kv_heads = kv_own.shape[0] // 2
    group = heads // kv_heads
    count = kv_heads // parts
    base = part * count
    q_spec = pl.BlockSpec((group, rows, dim), lambda g, p: (g + base, 0, 0))
    kv_spec = pl.BlockSpec((1, rows, dim), lambda g, p: (g + base, 0, 0))
    v_spec = pl.BlockSpec((1, rows, dim), lambda g, p: (g + base + kv_heads, 0, 0))
    whole = pl.BlockSpec(cos_t.shape, lambda g, p: (0, 0))
    return pl.pallas_call(
        functools.partial(attend_back_kernel, scale=HEAD_DIM ** (-0.5)),
        out_shape=[
            jax.ShapeDtypeStruct((heads // parts, rows, dim), BF16),
            jax.ShapeDtypeStruct((2, count, rows, dim), F32),
            jax.ShapeDtypeStruct((2, count, rows, dim), BF16),
        ],
        grid_spec=pltpu.PrefetchScalarGridSpec(
            num_scalar_prefetch=1,
            grid=(count,),
            in_specs=[q_spec, kv_spec, kv_spec, v_spec, v_spec]
            + [q_spec, pl.BlockSpec((1, *lse.shape[1:]), lambda g, p: (g + base, 0, 0)), whole, whole]
            + [pl.BlockSpec(memory_space=pltpu.HBM)] * len(ties),
            out_specs=[pl.BlockSpec((group, rows, dim), lambda g, p: (g, 0, 0))] + [pl.BlockSpec((2, 1, rows, dim), lambda g, p: (0, g, 0, 0))] * 2,
            scratch_shapes=[pltpu.VMEM((2 * rows, dim), BF16)] * 2
            + [pltpu.VMEM((2 * rows, dim), F32)] * 2,
        ),
        compiler_params=pltpu.CompilerParams(vmem_limit_bytes=64 * 2**20),
        cost_estimate=work(1),
        name=f"attend_back_{part}",
    )(place, queries, kv_own, kv_near, kv_own, kv_near, grad, lse, cos_t, sin_t, *ties)


def row_copies(sources, refs, into, sems):
    copies, at = [], into.shape[0] // 2
    for ref, (_, base, count) in zip(refs, sources):
        for c in range(into.shape[1] // PANEL):
            copies.append(
                pltpu.make_async_copy(
                    ref.at[pl.ds(base + c * count, count)],
                    into.at[pl.ds(at, count), pl.ds(c * PANEL, PANEL)],
                    sems.at[len(copies)],
                )
            )
        at += count
    return copies


class Landing:
    def __init__(self, place, bundle, refs, targets, sems):
        used = sources_of(bundle)
        n = len(used)
        own = dict(zip(used, refs[:n]))
        near = {} if bundle.joined else dict(zip(used, refs[n : 2 * n]))
        listed = land_copies(place, bundle, own, near, refs[-2], refs[-1], targets)
        self.copies = [
            (key, pltpu.make_async_copy(src, dst, sems.at[i])) for i, (src, dst, key) in enumerate(listed)
        ]
        self.copies.sort(key=lambda c: c[0])
        for _, c in self.copies:
            c.start()

    def wait(self, wanted=None):
        left = []
        for key, c in self.copies:
            if wanted is None or wanted(key):
                c.wait()
            else:
                left.append((key, c))
        self.copies = left


def landing_operands(bundle, weights, near, here, there):
    used = sources_of(bundle)
    return [weights[i] for i in used] + ([] if bundle.joined else [near[i] for i in used]) + [here, there]


def landing_count(bundle):
    return sum((1 if bundle.joined else 2) * len(p.parts) + 3 for p in bundle.first + bundle.second)


NO_BUNDLE = Bundle((), (), ())


def kernel_call(body, place, bundle, landing, operands, outs, scratch, name, time=0.5, ties=()):
    operands = [*operands, *((t, HB) for t in ties)]
    n_land, n_in, n_out, n_w = len(landing), len(operands), len(outs), len(bundle.shapes)

    def kernel(place_ref, *refs):
        land, refs = refs[:n_land], refs[n_land:]
        ins, refs = refs[: n_in - len(ties)], refs[n_in:]
        out, refs = refs[:n_out], refs[n_out:]
        body(place_ref, land, ins, out, refs[:n_w], refs[n_w], refs[n_w + 1 :])

    def spec(where):
        return where if isinstance(where, pl.BlockSpec) else pl.BlockSpec(memory_space=where)

    return pl.pallas_call(
        kernel,
        out_shape=[o for o, _ in outs],
        grid_spec=pltpu.PrefetchScalarGridSpec(
            num_scalar_prefetch=1,
            grid=(1,),
            in_specs=[spec(pltpu.HBM)] * n_land + [spec(w) for _, w in operands],
            out_specs=[spec(w) for _, w in outs],
            scratch_shapes=[pltpu.VMEM(sh, BF16) for sh in bundle.shapes]
            + [pltpu.SemaphoreType.DMA((max(landing_count(bundle), 1),))]
            + list(scratch),
        ),
        compiler_params=pltpu.CompilerParams(vmem_limit_bytes=64 * 2**20),
        cost_estimate=work(time),
        name=name,
    )(place, *landing, *[a for a, _ in operands])


VM = pltpu.VMEM
HB = pltpu.HBM


def like(shape, dtype):
    return jax.ShapeDtypeStruct(shape, dtype)


def turn(value, cos_full, sin_signed, half):
    swapped = jnp.concatenate([value[:, half:], value[:, :half]], axis=1)
    return value * cos_full + swapped * sin_signed


def padded(value):
    return jnp.concatenate([value, jnp.zeros((value.shape[0], LANES - HEAD_DIM), value.dtype)], axis=1)


def one_of_pair(block, width):
    return pl.BlockSpec((None, block, width), lambda i, p: (p[0] // 2, 0, 0))


def qkv_forward(place, bundle, landing, tokens, tokens_back, gain, inner, outer, cos, sin, ties):
    _, block, width = tokens.shape
    rows = 2 * block
    total = bundle.shapes[0][1]
    kv = (total - width) // 2
    wide = 8 * HEAD_DIM
    half = HEAD_DIM // 2

    def body(pr, land_refs, ins, outs, weights, sems, scratch):
        kept, *backs, gain_ref, inner_ref, outer_ref, cos_ref, sin_ref = ins
        q, kv_ref, hidden_ref, normed_ref, x_ref = outs
        (w,) = weights
        arriving = row_copies(tokens_back, backs, x_ref, scratch[0])
        for c in arriving:
            c.start()
        landing = Landing(pr, bundle, land_refs, weights, sems)
        x_ref[:block] = kept[...]
        for c in arriving:
            c.wait()
        x = x_ref[...].astype(F32)
        scale = lax.rsqrt(jnp.mean(x * x, axis=-1, keepdims=True) + EPSILON)
        normed_ref[...] = (x * scale * gain_ref[...].astype(F32)).astype(BF16)
        hidden_ref[...] = dot_nt(normed_ref[...], inner_ref[...]).astype(BF16)

        def columns(at):
            cols = pl.ds(at, wide)
            return dot(normed_ref[...], w[:, cols]) + dot(hidden_ref[...], outer_ref[:, cols])

        landing.wait(lambda key: key[1] < width)
        for i in range(width // wide):
            acc = columns(i * wide)
            for h in range(8):
                one = acc[:, h * HEAD_DIM : (h + 1) * HEAD_DIM]
                q[8 * i + h] = padded(turn(one, cos_ref[...], sin_ref[...], half)).astype(BF16)
        landing.wait()
        acc = columns(width)
        for h in range(8):
            one = acc[:, h * HEAD_DIM : (h + 1) * HEAD_DIM]
            kv_ref[h] = padded(turn(one, cos_ref[...], sin_ref[...], half)).astype(BF16)
        acc = columns(width + kv)
        for h in range(8):
            kv_ref[8 + h] = padded(acc[:, h * HEAD_DIM : (h + 1) * HEAD_DIM]).astype(BF16)

    heads = width // HEAD_DIM
    return kernel_call(
        body, place, bundle, landing,
        [(tokens, one_of_pair(block, width)), *((t[0], HB) for t in tokens_back), (gain, VM), (inner, VM), (outer, VM), (cos, VM), (sin, VM)],
        [
            (like((heads, rows, LANES), BF16), VM),
            (like((2 * kv // HEAD_DIM, rows, LANES), BF16), VM),
            (like((rows, inner.shape[0]), BF16), VM),
            (like((rows, width), BF16), VM),
            (like((rows, width), BF16), VM),
        ],
        [pltpu.SemaphoreType.DMA((len(tokens_back) * width // PANEL,))], "qkv_forward", time=EST, ties=ties,
    )


def out_forward(place, bundle, landing, heads_out, x, gain, inner, outer, cot, cot_back, inner_gl, drop_b):
    rows, width = x.shape
    heads = heads_out.shape[0]

    def body(pr, land_refs, ins, outs, weights, sems, scratch):
        heads_ref, x_ref, gain_ref, inner_ref, outer_ref, cot_kept, *cot_got, igl, db = ins
        middle, normed, attended, hidden, cot_ref, h_gl, h_d = outs
        arriving = row_copies(cot_back, cot_got, cot_ref, scratch[0])
        for c in arriving:
            c.start()
        landing = Landing(pr, bundle, land_refs, weights, sems)
        for h in range(heads):
            attended[:, h * HEAD_DIM : (h + 1) * HEAD_DIM] = heads_ref[h, :, :HEAD_DIM]
        hidden[...] = dot_nt(attended[...], inner_ref[...]).astype(BF16)
        cot_ref[: rows // 2] = cot_kept[...]
        for c in arriving:
            c.wait()
        h_d[...] = dot_nt(cot_ref[...], db[...]).astype(BF16)
        landing.wait()
        wide = width // 2
        squares = jnp.zeros((rows, 1), F32)
        for i in range(2):
            cols = pl.ds(i * wide, wide)
            branch = dot(attended[...], weights[0][:, cols]) + dot(hidden[...], outer_ref[:, cols])
            value = x_ref[:, cols].astype(F32) + branch
            middle[:, cols] = value
            squares += jnp.sum(value * value, axis=-1, keepdims=True)
        scale = lax.rsqrt(squares / width + EPSILON)
        normed[...] = (middle[...] * scale * gain_ref[...].astype(F32)).astype(BF16)
        h_gl[...] = dot_nt(normed[...], igl[...]).astype(BF16)

    return kernel_call(
        body, place, bundle, landing,
        [(heads_out, VM), (x, VM), (gain, VM), (inner, VM), (outer, VM),
         (cot, one_of_pair(rows // 2, width)), *((c[0], HB) for c in cot_back), (inner_gl, VM), (drop_b, VM)],
        [
            (like((rows, width), F32), VM),
            (like((rows, width), BF16), VM),
            (like((rows, width), BF16), VM),
            (like((rows, RANK), BF16), VM),
            (like((rows, width), BF16), VM),
            (like((rows, 2 * RANK), BF16), VM),
            (like((rows, RANK), BF16), VM),
        ],
        [pltpu.SemaphoreType.DMA((len(cot_back) * width // PANEL,))], "out_forward", time=EST,
    )


def mlp_chunk(place, bundle, landing, normed, cot, hidden_gl, hidden_d, outer_gl, drop_a, chunk, sums, name):
    rows, width = normed.shape
    units = bundle.shapes[1][0]
    steps = units // PANEL
    first = sums is None
    part = units // 4

    def body(pr, land_refs, ins, outs, weights, sems, scratch):
        normed_ref, cot_ref, hgl_ref, hd_ref, ogl, da = ins[:6]
        drop_sum, e_sum, thin, keep, send = outs
        (packed,) = scratch
        w_gl, w_d = weights
        landing = Landing(pr, bundle, land_refs, weights, sems)
        h_d = hd_ref[...]
        h_g, h_l = hgl_ref[:, :RANK], hgl_ref[:, RANK:]
        g_t, l_t, d_t = h_g.T, h_l.T, h_d.T
        for i in range(steps):
            landing.wait(lambda key: key[0] == 1 or key[1] < 2 * (i + 1) * PANEL)
            cols = slice(i * PANEL, (i + 1) * PANEL)
            both = pl.ds(2 * i * PANEL, 2 * PANEL)
            acts = dot(normed_ref[...], w_gl[:, both])
            gate = acts[:, :PANEL] + dot(h_g, ogl[:RANK, cols])
            lift = acts[:, PANEL:] + dot(h_l, ogl[RANK:, cols])
            a_grad = dot_nt(cot_ref[...], w_d[cols]) + dot(h_d, da[:, cols])
            sig = 1.0 / (1.0 + jnp.exp(-gate))
            silu = gate * sig
            active = (silu * lift).astype(BF16)
            gate_grad = (a_grad * lift * sig * (1.0 + gate * (1.0 - sig))).astype(BF16)
            lift_grad = (a_grad * silu).astype(BF16)
            grads = jnp.concatenate([gate_grad, lift_grad], axis=1)
            down = dot(active, w_d[cols])
            back = dot_nt(grads, w_gl[:, both])
            t0 = dot_nt(active, da[:, cols])
            t1 = dot_nt(gate_grad, ogl[:RANK, cols])
            t2 = dot_nt(lift_grad, ogl[RANK:, cols])
            if i == 0 and first:
                drop_sum[...] = down
                e_sum[...] = back
                thin[0], thin[1], thin[2] = t0, t1, t2
            elif i == 0:
                drop_sum[...] = ins[6][...] + down
                e_sum[...] = ins[7][...] + back
                thin[0], thin[1], thin[2] = ins[8][0] + t0, ins[8][1] + t1, ins[8][2] + t2
            else:
                drop_sum[...] += down
                e_sum[...] += back
                thin[0] += t0
                thin[1] += t1
                thin[2] += t2
            per = PANEL // part
            for j, g in enumerate((dot(g_t, gate_grad), dot(l_t, lift_grad), dot(d_t, active))):
                for o in range(per):
                    packed[i * per + o, :, j * part : (j + 1) * part] = g[:, o * part : (o + 1) * part]
        split_by_core(pr, packed, keep, send)

    at_chunk = lambda i, p: (chunk, 0, 0)
    operands = [
        (normed, VM), (cot, VM), (hidden_gl, VM), (hidden_d, VM),
        (outer_gl, pl.BlockSpec((None, *outer_gl.shape[1:]), at_chunk)),
        (drop_a, pl.BlockSpec((None, *drop_a.shape[1:]), at_chunk)),
    ]
    if not first:
        operands += [(s, VM) for s in sums]
    return kernel_call(
        body, place, bundle, landing, operands,
        [
            (like((rows, width), F32), VM),
            (like((rows, width), F32), VM),
            (like((3, rows, RANK), F32), VM),
            (like((2, RANK, 3 * part), F32), VM),
            (like((2, RANK, 3 * part), BF16), VM),
        ],
        [pltpu.VMEM((4, RANK, 3 * part), F32)], name, time=EST,
    )


def split_by_core(place_ref, whole, keep, send):
    core = place_ref[0] % 2
    for j in range(2):
        keep[j] = whole[core + 2 * j]
        send[j] = whole[1 - core + 2 * j].astype(BF16)


def out_backward(place, bundle, landing, sums, middle, cot, gain, normed, attended, hidden, factors, ties):
    rows, width = middle.shape
    heads = width // HEAD_DIM

    def body(pr, land_refs, ins, outs, weights, sems, scratch):
        drop_sum, e_sum, thin, middle_ref, cot_ref, gain_ref, normed_ref, att, hid, drop_b, igl, o_a, o_b = ins
        mixed_kept, mixed_back, mid_grad, out_heads, keep, send = outs
        (w,) = weights
        branch, whole = scratch
        landing = Landing(pr, bundle, land_refs, weights, sems)
        d_hid = thin[0].astype(BF16)
        gl_grad = jnp.concatenate([thin[1].astype(BF16), thin[2].astype(BF16)], axis=1)
        e_in = (e_sum[...] + dot(gl_grad, igl[...])) * gain_ref[...].astype(F32)
        mid = middle_ref[...]
        scale = lax.rsqrt(jnp.mean(mid * mid, axis=-1, keepdims=True) + EPSILON)
        n = mid * scale
        mean = jnp.mean(e_in * n, axis=-1, keepdims=True)
        mid_grad[...] = cot_ref[...].astype(F32) + scale * (e_in - n * mean)
        branch[...] = mid_grad[...].astype(BF16)
        hgrad = dot_nt(branch[...], o_b[...]).astype(BF16)
        landing.wait()
        wide = 8 * HEAD_DIM
        for i in range(heads // 8):
            part = slice(i * wide, (i + 1) * wide)
            grad = dot_nt(branch[...], w[part]) + dot(hgrad, o_a[:, part])
            for h in range(8):
                out_heads[8 * i + h] = padded(grad[:, h * HEAD_DIM : (h + 1) * HEAD_DIM]).astype(BF16)
        mixed = (mid + drop_sum[...] + dot(d_hid, drop_b[...])).astype(BF16)
        mixed_kept[...] = mixed[: rows // 2]
        mixed_back[...] = mixed[rows // 2 :]
        gl = dot(gl_grad.T, normed_ref[...])
        own = (
            dot(d_hid.T, cot_ref[...]), gl[:RANK], gl[RANK:],
            dot(hgrad.T, att[...]), dot(hid[...].T, branch[...]),
        )
        for t in range(4):
            for j, g in enumerate(own):
                at = j * quarter
                whole[t, :, at : at + quarter] = g[:, t * quarter : (t + 1) * quarter]
        split_by_core(pr, whole, keep, send)

    quarter = width // 4
    cols = 5 * quarter
    return kernel_call(
        body, place, bundle, landing,
        [(v, VM) for v in (*sums, middle, cot, gain, normed, attended, hidden, *factors)],
        [
            (like((2, rows // 2, width), BF16), one_of_pair(rows // 2, width)),
            (like((rows // 2, width), BF16), VM),
            (like((rows, width), F32), VM),
            (like((heads, rows, LANES), BF16), VM),
            (like((2, RANK, cols), F32), VM),
            (like((2, RANK, cols), BF16), VM),
        ],
        [pltpu.VMEM((rows, width), BF16), pltpu.VMEM((4, RANK, cols), F32)], "out_backward", time=15, ties=ties,
    )


def qkv_gradients(place, parts, cos, sin, normed, hidden, outer, ties):
    rows, width = normed.shape
    total = outer.shape[1]
    kv = (total - width) // 2
    half = HEAD_DIM // 2
    rank3 = outer.shape[0]
    quarter, kv_quarter = width // 4, kv // 4
    cols = 4 * quarter + 2 * kv_quarter
    q_count, kv_count = parts[0][0].shape[0], parts[0][1].shape[1]

    def body(pr, land_refs, ins, outs, weights, sems, scratch):
        *part_refs, cos_ref, sin_ref, nrm, hid, b = ins
        dq_refs, dkv_refs, got_refs = part_refs[0::3], part_refs[1::3], part_refs[2::3]
        g, hgrad_ref, keep, send = outs
        (whole,) = scratch
        for h in range(width // HEAD_DIM):
            ref, i = dq_refs[h // q_count], h % q_count
            g[:, h * HEAD_DIM : (h + 1) * HEAD_DIM] = ref[i, :, :HEAD_DIM]
        for h in range(kv // HEAD_DIM):
            dkv_ref, got_ref, i = dkv_refs[h // kv_count], got_refs[h // kv_count], h % kv_count
            one = (dkv_ref[0, i] + got_ref[0, i].astype(F32))[:, :HEAD_DIM]
            at = width + h * HEAD_DIM
            g[:, at : at + HEAD_DIM] = turn(one, cos_ref[...], -sin_ref[...], half).astype(BF16)
            at += kv
            g[:, at : at + HEAD_DIM] = (dkv_ref[1, i] + got_ref[1, i].astype(F32))[:, :HEAD_DIM].astype(BF16)
        hgrad_ref[...] = dot_nt(g[...], b[...]).astype(BF16)
        g_in = dot(hgrad_ref[...].T, nrm[...])
        g_out = dot(hid[...].T, g[...])
        for t in range(4):
            for i in range(3):
                whole[t, :, i * quarter : (i + 1) * quarter] = g_in[
                    i * RANK : (i + 1) * RANK, t * quarter : (t + 1) * quarter
                ]
            whole[t, :, 3 * quarter : 4 * quarter] = g_out[:RANK, t * quarter : (t + 1) * quarter]
            for i in range(2):
                at, start = 4 * quarter + i * kv_quarter, width + i * kv + t * kv_quarter
                whole[t, :, at : at + kv_quarter] = g_out[
                    (1 + i) * RANK : (2 + i) * RANK, start : start + kv_quarter
                ]
        split_by_core(pr, whole, keep, send)

    return kernel_call(
        body, place, NO_BUNDLE, [],
        [(v, VM) for v in (*[v for p in parts for v in p], cos, sin, normed, hidden, outer)],
        [
            (like((rows, total), BF16), VM),
            (like((rows, rank3), BF16), VM),
            (like((2, RANK, cols), F32), VM),
            (like((2, RANK, cols), BF16), VM),
        ],
        [pltpu.VMEM((4, RANK, cols), F32)], "qkv_gradients", time=1, ties=ties,
    )


def qkv_backward(place, bundle, landing, g, hgrad, x, mid_grad, gain, inner, ties):
    rows, width = x.shape
    total = bundle.shapes[0][1]
    block = rows // 2

    def body(pr, land_refs, ins, outs, weights, sems, scratch):
        g_ref, hg, x_ref, mg, gain_ref, a = ins
        kept, back = outs
        (w,) = weights
        landing = Landing(pr, bundle, land_refs, weights, sems)
        xf = x_ref[...].astype(F32)
        scale = lax.rsqrt(jnp.mean(xf * xf, axis=-1, keepdims=True) + EPSILON)
        n = xf * scale
        thin = dot(hg[...], a[...])
        landing.wait()
        e_in = (dot_nt(g_ref[...], w[...]) + thin) * gain_ref[...].astype(F32)
        mean = jnp.mean(e_in * n, axis=-1, keepdims=True)
        result = mg[...] + scale * (e_in - n * mean)
        kept[...] = result[:block]
        back[...] = result[block:].astype(BF16)

    return kernel_call(
        body, place, bundle, landing,
        [(v, VM) for v in (g, hgrad, x, mid_grad, gain, inner)],
        [(like((2, block, width), F32), one_of_pair(block, width)), (like((block, width), BF16), VM)],
        [], "qkv_backward", time=0.2, ties=ties,
    )


def complete(place, partial, back, ties, name):
    _, block, width = partial.shape

    def kernel(place_ref, partial_ref, back_ref, *rest):
        rest[-1][...] = back_ref[...].astype(partial.dtype)

    return pl.pallas_call(
        kernel,
        out_shape=jax.ShapeDtypeStruct(partial.shape, partial.dtype),
        grid_spec=pltpu.PrefetchScalarGridSpec(
            num_scalar_prefetch=1,
            grid=(1,),
            in_specs=[pl.BlockSpec(memory_space=pltpu.HBM), pl.BlockSpec(memory_space=pltpu.VMEM)]
            + [pl.BlockSpec(memory_space=pltpu.HBM)] * len(ties),
            out_specs=pl.BlockSpec((None, block, width), lambda i, p: (1 - p[0] // 2, 0, 0)),
        ),
        input_output_aliases={1: 0},
        compiler_params=pltpu.CompilerParams(vmem_limit_bytes=64 * 2**20),
        cost_estimate=work(0.5),
        name=name,
    )(place, partial, back, *ties)


def pack_factors(place, inners, outers):
    widths = [a.shape[0] for a in inners] + [b.shape[1] for b in outers]
    n = len(inners)
    mix = outers[0].shape[0]
    narrow = (n + 1, n + 2)

    def body(pr, land_refs, ins, outs, weights, sems, scratch):
        for which, out in enumerate(outs):
            row = lax.broadcasted_iota(jnp.int32, (RANK, mix), 0) + pr[3 + which] * RANK
            choose = (row == lax.broadcasted_iota(jnp.int32, (RANK, mix), 1)).astype(F32).astype(BF16)
            at = 0
            for i, ref in enumerate(ins):
                part = dot_nt(choose, ref[...]) if i < n or i in narrow else dot(choose, ref[...])
                out[:, at : at + widths[i]] = part.astype(BF16)
                at += widths[i]

    shape = (like((RANK, sum(widths)), BF16), VM)
    return kernel_call(
        body, place, NO_BUNDLE, [], [(v.T if i in narrow else v, VM) for i, v in enumerate((*inners, *outers))],
        [shape, shape], [], "pack_factors",
    )


def unpack_factors(place, slots, widths, chunks):
    inner_w, outer_w = widths[:7], widths[7:]
    width, kv = 4 * outer_w[0], 4 * outer_w[1]
    part = outer_w[4] // chunks
    starts = [sum(widths[:i]) for i in range(len(widths))]

    def body(pr, land_refs, ins, outs, weights, sems, scratch):
        iq, oq, io, oo, igl, ogl, da, db = outs
        (nat,) = scratch
        mine, two, got = ins
        nat[pr[0]] = mine[...]
        nat[pr[0] ^ 2] = two[...]
        nat[pr[0] ^ 1] = got[:RANK]
        nat[pr[0] ^ 3] = got[RANK:]
        oq[...] = jnp.zeros(oq.shape, BF16)
        for t in range(4):
            get = lambda i, a=0, n=None: nat[t, :, starts[i] + a : starts[i] + a + (n or widths[i])]
            w = inner_w[0]
            here = slice(t * w, (t + 1) * w)
            for i in range(3):
                iq[i * RANK : (i + 1) * RANK, here] = get(i)
            io[:, here] = get(3)
            igl[:RANK, here] = get(4)
            igl[RANK:, here] = get(5)
            base = 0
            for i in range(3):
                n = outer_w[i]
                oq[i * RANK : (i + 1) * RANK, base + t * n : base + (t + 1) * n] = get(7 + i)
                base += 4 * n
            oo[:, here] = get(10)
            db[:, here] = get(13)
            for u in range(chunks):
                there = slice(t * part, (t + 1) * part)
                ogl[u, :RANK, there] = get(11, u * part, part)
                ogl[u, RANK:, there] = get(12, u * part, part)
                da[u, :, there] = get(6, u * part, part)

    shapes = [
        (3 * RANK, width), (3 * RANK, width + 2 * kv), (RANK, width), (RANK, width), (2 * RANK, width),
        (chunks, 2 * RANK, 4 * part), (chunks, RANK, 4 * part), (RANK, width),
    ]
    return kernel_call(
        body, place, NO_BUNDLE, [], [(v, VM) for v in slots], [(like(sh, BF16), VM) for sh in shapes],
        [pltpu.VMEM((4, *slots[0].shape), BF16)], "unpack_factors",
    )


def fold_cores(place, sums, name, ties=()):
    n = len(sums)
    cols = sum(k.shape[2] for k, _ in sums)

    def body(pr, land_refs, ins, outs, weights, sems, scratch):
        chip = pr[0] // 2
        for out, which in zip(outs, (chip, 1 - chip)):
            at = 0
            for keep_ref, got_ref in zip(ins[:n], ins[n:]):
                w = keep_ref.shape[2]
                out[:, at : at + w] = (keep_ref[which] + got_ref[which].astype(F32)).astype(BF16)
                at += w
            out[:, cols:] = jnp.full((RANK, LANES), pr[3], jnp.int32).astype(F32).astype(BF16)

    shape = (like((RANK, cols + LANES), BF16), VM)
    return kernel_call(
        body, place, NO_BUNDLE, [], [(k, VM) for k, _ in sums] + [(g, VM) for _, g in sums],
        [shape, shape], [], name, ties=ties,
    )


def spread_sums(place, groups, pieces, mix, name, ties=()):
    count = sum(v.shape[0] for v in groups[0])
    tall = [len(g) > 1 for g in groups]

    def body(pr, land_refs, ins, outs, weights, sems, scratch):
        gots, at, held = [], 0, list(scratch)
        for g in groups:
            refs = ins[at : at + len(g)]
            at += len(g)
            if len(g) == 1:
                gots.append(refs[0])
                continue
            got, row = held.pop(0), 0
            for ref in refs:
                got[row : row + ref.shape[0]] = ref[...]
                row += ref.shape[0]
            gots.append(got)
        tag = gots[0][:, -LANES:].astype(F32).astype(jnp.int32) * RANK
        spot = tag + lax.broadcasted_iota(jnp.int32, (count, LANES), 0) % RANK
        choose = (spot == lax.broadcasted_iota(jnp.int32, (count, LANES), 1)).astype(F32).astype(BF16)
        choose_t = choose.T
        for out, (is_inner, runs) in zip(outs, pieces):
            at = 0
            for g, start, n in runs:
                if is_inner:
                    out[at : at + n] = dot_tn(gots[g][:, start : start + n], choose)
                else:
                    out[:, at : at + n] = dot(choose_t, gots[g][:, start : start + n])
                at += n

    outs = []
    for is_inner, runs in pieces:
        n = sum(c for _, _, c in runs)
        outs.append((like((n, mix) if is_inner else (mix, n), F32), VM))
    scratch = [pltpu.VMEM((count, g[0].shape[1]), BF16) for g, t in zip(groups, tall) if t]
    return kernel_call(
        body, place, NO_BUNDLE, [], [(v, VM) for g in groups for v in g], outs, scratch, name, ties=ties
    )


def local(
    tokens,
    cotangent,
    prefix_len,
    adapter_index,
    gain_attn,
    gain_mlp,
    query_weight,
    key_weight,
    value_weight,
    output_weight,
    gate_weight,
    lift_weight,
    drop_weight,
    *factors,
):
    _, block, width = tokens.shape
    rep, shard = lax.axis_index("rep"), lax.axis_index("shard")
    chip = shard // 2
    rows = 2 * block
    kv_width = KV_HEADS * HEAD_DIM
    where = jnp.stack([shard, rep % 4]).astype(jnp.int32)
    place = jnp.concatenate(
        [where, jnp.stack([prefix_len[chip], adapter_index[chip], adapter_index[1 - chip]])]
    )

    weights = (query_weight, key_weight, value_weight, output_weight, gate_weight, lift_weight, drop_weight)
    inners, outers = factors[0::2], factors[1::2]
    widths = [a.shape[0] for a in inners] + [b.shape[1] for b in outers]
    chunks = 4
    ff = gate_weight.shape[1]
    bundles = make_bundles(width, kv_width, ff, chunks, 4)
    positions = jnp.concatenate(
        [shard * block + jnp.arange(block), (shard ^ 2) * block + jnp.arange(block)]
    )
    cos_table, sine_table = rotary_tables(positions.astype(F32), HEAD_DIM)
    cos_full = jnp.concatenate([cos_table, cos_table], axis=1)
    sin_full = jnp.concatenate([-sine_table, sine_table], axis=1)
    gain_one, gain_two = gain_attn[None], gain_mlp[None]
    cos_t, sin_t = cos_table.T, sine_table.T

    relay = Relay(where, weights, bundles)
    half = block // 2
    near = {i: to_core(weights[i]) for i in (4, 5, 6)}
    relay.step()
    mine, others = pack_factors(place, inners, outers)
    slot_two = to_chip(others)
    (tokens_a,), _ = relay.step([(tokens, 0, half)], ties=(near[4], near[5], sin_full, cos_full, cos_t, sin_t, gain_one, gain_two, place))
    (tokens_b,), _ = relay.step([(tokens, half, half)], ties=(slot_two,))
    joined = join(mine, slot_two)
    got = to_core(joined)
    relay.step(ties=(near[6], got))
    inner_qkv, outer_qkv, inner_o, outer_o, inner_gl, outer_gl, drop_a, drop_b = unpack_factors(
        place, (mine, slot_two, got), widths, chunks
    )

    def landing(i):
        return landing_operands(bundles[i], weights, near, relay.here[i], relay.there[i])

    (cot_a,), begun = relay.step([(cotangent, 0, half)], ties=(inner_qkv,), across=False)
    queries, kv_own, hidden_qkv, normed_attn, x = qkv_forward(
        place, bundles[0], landing(0), tokens, (tokens_a, tokens_b), gain_one,
        inner_qkv, outer_qkv, cos_full, sin_full, begun[:1],
    )
    (cot_b,), begun = relay.step([(cotangent, half, half)], ties=(x,))
    kv_own = gate(kv_own, begun[:1])
    relay.across(1, begun[:1])
    kv_near = to_core(kv_own)
    heads_out, lse = attend(place, queries, kv_own, kv_near)
    middle, normed_mlp, attended, output_hidden, cot, hidden_gl, hidden_d = out_forward(
        place, bundles[1], landing(1), heads_out, x, gain_two, inner_o, outer_o,
        cotangent, (cot_a, cot_b), inner_gl, drop_b,
    )
    relay.step(ties=(normed_mlp,))
    sums, kept_sums = None, []
    for u in range(chunks):
        *sums, keep, send = mlp_chunk(
            place, bundles[2 + u], landing(2 + u), normed_mlp, cot, hidden_gl, hidden_d,
            outer_gl, drop_a, u, sums, f"mlp_{u}",
        )
        kept_sums.append((keep, to_core(send)))
        if u < 2:
            relay.step(ties=(keep,))
    early = fold_cores(place, kept_sums[:-1], "fold_early", (keep,))
    mixed_kept, mixed_back, middle_grad, grad_heads, keep, send = out_backward(
        place, bundles[1], landing(1), sums, middle, cot, gain_two, normed_mlp, attended,
        output_hidden, (drop_b, inner_gl, inner_o, outer_o), early[:1],
    )

    mixed_back = to_chip(mixed_back)
    early = join(early[0], to_chip(early[1]))
    folded = fold_cores(place, [kept_sums[-1], (keep, to_core(send))], "fold_late")
    parts, halves = [], 2
    for i in range(halves):
        dq, dkv, dkv_send = attend_back(
            place, queries, kv_own, kv_near, grad_heads, lse, cos_t, sin_t, i, halves,
            folded if i else (early,),
        )
        if i:
            late = to_chip(folded[1])
            dkv_send = gate(dkv_send, (late, mixed_back))
        parts.append((dq, dkv, to_core(dkv_send)))
    early = lax.all_gather(early, "rep", axis=0, tiled=True)
    late_both = join(folded[0], late)
    late = lax.all_gather(late_both, "rep", axis=0, tiled=True)
    g, hgrad, keep, send = qkv_gradients(
        place, parts, cos_full, sin_full, normed_attn, hidden_qkv, outer_qkv, (late_both,)
    )
    folded = fold_cores(place, [(keep, to_core(send))], "fold_first")
    other = to_chip(folded[1])
    both = join(folded[0], other)
    input_kept, input_back = qkv_backward(
        place, bundles[0], landing(0), g, hgrad, x, middle_grad, gain_one, inner_qkv, (both, early)
    )
    line = [both]
    for k in range(2, lax.axis_size("rep"), 2):
        line.append(move(both, lambda r, s, k=k: (r ^ k, s)))
    line = join(*line, ties=(input_back,))
    input_back = to_chip(gate(input_back, (line,)))
    first = [line, to_y(line)]
    mixed = complete(place, mixed_kept, mixed_back, (), "complete_mixed")

    mix = ADAPTERS * RANK
    w, kw = width // 4, kv_width // 4
    part = ff // 4 // chunks
    wide = 3 * part
    runs = lambda j: [
        (0, u * wide + j * part, part) if u < chunks - 1 else (1, j * part, part) for u in range(chunks)
    ]
    rest = lambda j: [(1, wide + j * w, w)]
    g_out, l_out, d_in, d_out, g_in, l_in, o_in, o_out = spread_sums(
        place, [[early], [late]],
        [(False, runs(0)), (False, runs(1)), (True, runs(2)), (False, rest(0)), (True, rest(1)),
         (True, rest(2)), (True, rest(3)), (False, rest(4))],
        mix, "spread_late",
    )
    q_in, k_in, v_in, q_out, k_out, v_out = spread_sums(
        place, [first],
        [(True, [(0, 0, w)]), (True, [(0, w, w)]), (True, [(0, 2 * w, w)]), (False, [(0, 3 * w, w)]),
         (True, [(0, 4 * w, kw)]), (True, [(0, 4 * w + kw, kw)])],
        mix, "spread_first", (o_out,),
    )
    k_out, v_out = k_out.T, v_out.T
    input_grad = complete(place, input_kept, input_back, (q_in,), "complete_input_grad")
    return (mixed, input_grad, q_in, q_out, k_in, k_out, v_in, v_out, o_in, o_out,
            g_in, g_out, l_in, l_out, d_in, d_out)


def solution(mesh):
    token_place = P("rep", "shard", None)
    row, col = P("shard", None), P(None, "shard")
    return jax.shard_map(
        local,
        mesh=mesh,
        in_specs=(token_place, token_place, P("rep"), P("rep"), P(), P()) + (row,) * 7 + (row, col) * 7,
        out_specs=(token_place, token_place) + (row, col) * 7,
        check_vma=False,
    )
```

```python
import functools
import math
from typing import NamedTuple

import jax
import jax.numpy as jnp
from jax import lax
from jax.experimental import pallas as pl
from jax.experimental.pallas import tpu as pltpu
from jax.sharding import PartitionSpec as P

HEADS = 16
KV_HEADS = 8
HEAD_DIM = 96
RANK = 16
ADAPTERS = 8
EPSILON = 1e-05
ROPE_BASE = 100000.0
MASKED_SCORE = -1e30
AXES = ("rep", "shard")
F32 = jnp.float32
BF16 = jnp.bfloat16


def move(value, target):
    reps, shards = lax.axis_size("rep"), lax.axis_size("shard")
    pairs = []
    for r in range(reps):
        for s in range(shards):
            r2, s2 = target(r, s)
            pairs.append((r * shards + s, r2 * shards + s2))
    return lax.ppermute(value, AXES, pairs)


def to_core(value):
    return move(value, lambda r, s: (r, s ^ 1))


def to_chip(value):
    return move(value, lambda r, s: (r, s ^ 2))


def to_y(value):
    return move(value, lambda r, s: (r ^ 1, s))


def to_z(value):
    return move(value, lambda r, s: (r ^ 2, s))


PANEL = 512
LANES = 128
EST = 5
PACK_EST = 0.1


class Piece(NamedTuple):
    parts: tuple
    row: int
    rows: int
    target: int
    block: int
    to_row: int
    to_col: int


class Bundle(NamedTuple):
    first: tuple
    second: tuple
    shapes: tuple
    joined: bool = True


def quarter_rows(pieces):
    return sum(p.rows for p in pieces) // 4


def make_bundles(width, kv_width, ff, chunks, shards):
    rows, drop_rows = width // shards, ff // shards // chunks
    panels = width // PANEL
    first = tuple(Piece(((0, c, PANEL),), 0, rows, 0, rows, 0, c) for c in range(0, width, PANEL))
    second = []
    for c in range(0, 2 * kv_width, PANEL):
        parts, at = [], c
        while at < c + PANEL:
            source = 1 if at < kv_width else 2
            base = (source - 1) * kv_width
            stop = min(c + PANEL, base + kv_width)
            parts.append((source, at - base, stop - at))
            at = stop
        second.append(Piece(tuple(parts), 0, rows, 0, rows, 0, width + c))
    found = [Bundle(first, tuple(second), ((width, width + 2 * kv_width),))]

    def halves(source, row, height, target, block):
        return [
            tuple(
                Piece(((source, i * PANEL, PANEL),), row + h * height // 2, height // 2, target, block,
                      h * height // 2, i * PANEL)
                for i in range(panels)
            )
            for h in range(2)
        ]

    top, bottom = halves(3, 0, rows, 0, rows)
    found.append(Bundle(top, bottom, ((width, width),)))
    part = ff // shards // chunks
    for u in range(chunks):
        sides = []
        for j in range(2):
            side = []
            for c in range(0, shards * part, PANEL):
                parts = tuple(
                    (4 + j, t * (ff // shards) + u * part, part)
                    for t in range(c // part, (c + PANEL) // part)
                )
                side.append(Piece(parts, 0, rows, 0, rows, 0, 2 * c + j * PANEL))
            sides.append(tuple(side))
        top, bottom = halves(6, u * drop_rows, drop_rows, 1, drop_rows)
        cols = shards * part
        found.append(
            Bundle(sides[0] + top, sides[1] + bottom, ((width, 2 * cols), (cols, width)), False)
        )
    return found


def work(microseconds):
    return pl.CostEstimate(flops=int(microseconds * 1.1e9), bytes_accessed=2**20, transcendentals=0)


def pack(place, jobs, operands, out_shapes, name):
    n_in, n_out = len(operands), len(out_shapes)

    def kernel(place_ref, *refs):
        ins, refs = refs[:n_in], refs[n_in:]
        outs, held, sems = refs[:n_out], refs[n_out : 2 * n_out], refs[-1]
        arriving, leaving = [], []
        for i, (src, o, *spot) in enumerate(jobs(place_ref, ins)):
            here = held[o].at[tuple(spot)]
            arriving.append(pltpu.make_async_copy(src, here, sems.at[0, i]))
            leaving.append(pltpu.make_async_copy(here, outs[o].at[tuple(spot)], sems.at[1, i]))
        for c in arriving:
            c.start()
        for c, d in zip(arriving, leaving):
            c.wait()
            d.start()
        for d in leaving:
            d.wait()

    class Fake:
        def __init__(self):
            self.at = self

        def __getitem__(self, _):
            return self

    count = len(jobs(None, [Fake()] * n_in))
    hbm = pl.BlockSpec(memory_space=pltpu.HBM)
    return pl.pallas_call(
        kernel,
        out_shape=[jax.ShapeDtypeStruct(sh, BF16) for sh in out_shapes],
        grid_spec=pltpu.PrefetchScalarGridSpec(
            num_scalar_prefetch=1,
            grid=(1,),
            in_specs=[hbm] * n_in,
            out_specs=[hbm] * n_out,
            scratch_shapes=[pltpu.VMEM(sh, BF16) for sh in out_shapes]
            + [pltpu.SemaphoreType.DMA((2, count))],
        ),
        compiler_params=pltpu.CompilerParams(vmem_limit_bytes=64 * 2**20),
        cost_estimate=work(PACK_EST),
        name=name,
    )(place, *operands)


def gate(value, ties):
    return pl.pallas_call(
        lambda *refs: None,
        out_shape=jax.ShapeDtypeStruct(value.shape, value.dtype),
        in_specs=[pl.BlockSpec(memory_space=pltpu.HBM)] * (1 + len(ties)),
        out_specs=pl.BlockSpec(memory_space=pltpu.HBM),
        input_output_aliases={0: 0},
        compiler_params=pltpu.CompilerParams(vmem_limit_bytes=64 * 2**20),
        name="gate",
    )(value, *ties)


def join(*parts, ties=()):
    cols = parts[0].shape[1]

    def kernel(*refs):
        at = 0
        for ref in refs[: len(parts)]:
            refs[-1][at : at + ref.shape[0]] = ref[...]
            at += ref.shape[0]

    return pl.pallas_call(
        kernel,
        out_shape=jax.ShapeDtypeStruct((sum(p.shape[0] for p in parts), cols), parts[0].dtype),
        in_specs=[pl.BlockSpec(memory_space=pltpu.VMEM)] * len(parts)
        + [pl.BlockSpec(memory_space=pltpu.HBM)] * len(ties),
        compiler_params=pltpu.CompilerParams(vmem_limit_bytes=64 * 2**20),
        cost_estimate=work(1),
        name="join",
    )(*parts, *ties)


def quarter_start(place_ref, flip, rows):
    if place_ref is None:
        return 0
    return pl.multiple_of((place_ref[1] ^ flip) * rows, 16)


class Relay:
    def __init__(self, place, weights, bundles):
        self.place, self.weights, self.bundles = place, weights, bundles
        self.direct, self.once, self.twice = {}, {}, {}
        self.here, self.there = {}, {}
        self.tick = 0

    def step(self, extra=(), ties=(), across=True):
        t, bundles = self.tick, self.bundles
        self.tick += 1
        operands, shapes, kinds, sent = [], [], [], []

        def operand(array):
            for i, o in enumerate(operands):
                if o is array:
                    return i
            operands.append(array)
            return len(operands) - 1

        plans = []

        def out(kind, rows, cols=PANEL):
            shapes.append((rows, cols))
            kinds.append(kind)
            return len(shapes) - 1

        if t < len(bundles):
            b = bundles[t]
            base = quarter_rows(b.first + b.second)
            o = out("x", base + sum(n * a.shape[2] // PANEL for a, _, n in extra))
            for array, start, count in extra:
                i = operand(array)
                sent.append((base, count))

                def plan_t(pr, ins, o=o, i=i, start=start, count=count, base=base, cols=array.shape[2]):
                    which = 0 if pr is None else 1 - pr[0] // 2
                    return [
                        (ins[i].at[which, pl.ds(start, count), pl.ds(c, PANEL)], o,
                         pl.ds(base + c // PANEL * count, count), slice(None))
                        for c in range(0, cols, PANEL)
                    ]

                plans.append(plan_t)
                base += count * array.shape[2] // PANEL
            used = [(operand(self.weights[q[0]]), q, p) for p in b.first + b.second for q in p.parts]

            def plan_x(pr, ins, o=o, used=used):
                copies, at, col = [], 0, 0
                for i, (_, c, n), p in used:
                    q = p.rows // 4
                    rows = pl.ds(pl.multiple_of(p.row + quarter_start(pr, 0, q), 16), q)
                    copies.append((ins[i].at[rows, pl.ds(c, n)],
                                   o, pl.ds(at, q), pl.ds(col, n)))
                    col += n
                    if col == PANEL:
                        at, col = at + q, 0
                return copies

            plans.append(plan_x)
        y_parts, z_parts = [], []
        b1, b2, b3 = t - 1, t - 2, t - 3
        if 0 <= b1 < len(bundles):
            qa, qb = quarter_rows(bundles[b1].first), quarter_rows(bundles[b1].second)
            y_parts.append(("first", b1, [(self.direct[b1], 0, qa)]))
            z_parts.append(("first", b1, [(self.direct[b1], qa, qb)]))
        if 0 <= b2 < len(bundles):
            qa, qb = quarter_rows(bundles[b2].first), quarter_rows(bundles[b2].second)
            (ya, yo), (za, zo) = self.once[b2]
            y_parts.append(("second", b2, [(self.direct[b2], qa, qb), (za, zo, qb)]))
            z_parts.append(("second", b2, [(self.direct[b2], 0, qa), (ya, yo, qa)]))
        for kind, parts in (("y", y_parts), ("z", z_parts)):
            if not parts:
                continue
            total = sum(n for _, _, l in parts for _, _, n in l)
            o = out(kind, total)
            flat = [(operand(a), r, n) for _, _, l in parts for a, r, n in l]

            def plan_n(pr, ins, o=o, flat=flat):
                copies, at = [], 0
                for i, r, n in flat:
                    copies.append((ins[i].at[pl.ds(r, n)], o, pl.ds(at, n), slice(None)))
                    at += n
                return copies

            plans.append(plan_n)
        for tie in ties:
            operand(tie)

        def jobs(pr, ins):
            return [c for plan in plans for c in plan(pr, ins)]

        bufs = pack(self.place, jobs, operands, shapes, f"pack_{t}") if shapes else []
        for kind, buf in zip(kinds, bufs):
            if kind == "x":
                self.direct[t] = to_chip(buf)
            else:
                got = (to_y if kind == "y" else to_z)(buf)
                at = 0
                for stage, bi, l in y_parts if kind == "y" else z_parts:
                    store = self.once if stage == "first" else self.twice
                    pair = store.setdefault(bi, [None, None])
                    pair[0 if kind == "y" else 1] = (got, at)
                    at += sum(n for _, _, n in l)
        if 0 <= b3 < len(bundles) and across:
            self.across(b3, bufs[:1] if bufs else ties)
        return [(self.direct[t], *spot) for spot in sent], bufs

    def across(self, b3, ties):
        b = self.bundles[b3]
        operands, shapes = [], []

        def operand(array):
            for i, o in enumerate(operands):
                if o is array:
                    return i
            operands.append(array)
            return len(operands) - 1

        plans = []

        def out(kind, rows, cols=PANEL):
            shapes.append((rows, cols))
            return len(shapes) - 1

        total = 4 * quarter_rows(b.first + b.second)
        o = out("c", (2 if b.joined else 1) * total)
        used = [
            (operand(self.weights[q[0]]), q, p)
            for p in (b.first + b.second if b.joined else ()) for q in p.parts
        ]
        qa = quarter_rows(b.first)
        qb = quarter_rows(b.second)
        (ya, yo), (za, zo) = self.once[b3]
        (ys, yso), (zs, zso) = self.twice[b3]
        d = operand(self.direct[b3])
        sides = [
            (b.first, [(0, d, 0), (1, operand(ya), yo), (2, operand(zs), zso), (3, operand(zs), zso + qa)]),
            (b.second, [(0, d, qa), (2, operand(za), zo), (1, operand(ys), yso), (3, operand(ys), yso + qb)]),
        ]

        def plan_c(pr, ins, o=o, sides=sides, used=used, total=total):
            copies, base, at, col = [], total if b.joined else 0, 0, 0
            for i, (_, c, n), p in used:
                copies.append((ins[i].at[pl.ds(p.row, p.rows), pl.ds(c, n)],
                               o, pl.ds(at, p.rows), pl.ds(col, n)))
                col += n
                if col == PANEL:
                    at, col = at + p.rows, 0
            for pieces, quarters in sides:
                at = 0
                for p in pieces:
                    q = p.rows // 4
                    for flip, i, r in quarters:
                        to = pl.multiple_of(base + quarter_start(pr, flip, q), 16)
                        copies.append((ins[i].at[pl.ds(r + at, q)], o, pl.ds(to, q), slice(None)))
                    at += q
                    base += p.rows
            return copies

        plans.append(plan_c)

        for tie in ties:
            operand(tie)
        jobs = lambda pr, ins: plans[0](pr, ins)
        (buf,) = pack(self.place, jobs, operands, shapes, f"across_{b3}")
        self.here[b3], self.there[b3] = buf, to_core(buf)


def land_copies(place_ref, bundle, own, near, here, there, targets):
    copies = []
    shard = 0 if place_ref is None else place_ref[0]
    pieces = bundle.first + bundle.second
    total = sum(p.rows for p in pieces)
    skip = total if bundle.joined else 0
    for slot, (ref, base) in enumerate(((None, 0), (there, 0), (here, skip), (there, skip))):
        for p in pieces:
            to = (shard ^ slot) * p.block + p.to_row
            to = pl.ds(pl.multiple_of(to, 16), p.rows)
            dst = targets[p.target]
            key = (p.target, p.to_col)
            if slot == 0 or slot == 1 and not bundle.joined:
                col = p.to_col
                for source, c, n in p.parts:
                    copies.append(((near if slot else own)[source].at[pl.ds(p.row, p.rows), pl.ds(c, n)],
                                   dst.at[to, pl.ds(col, n)], key))
                    col += n
            else:
                copies.append((ref.at[pl.ds(base, p.rows)], dst.at[to, pl.ds(p.to_col, PANEL)], key))
            base += p.rows
    return copies


def sources_of(bundle):
    return sorted({q[0] for p in bundle.first + bundle.second for q in p.parts})


def rotary_tables(positions, head_dim):
    half_dim = head_dim // 2
    freq_index = jnp.arange(half_dim).astype(F32)
    frequency = jnp.exp(freq_index * (-2.0 * math.log(ROPE_BASE) / head_dim))
    angles = positions[:, None] * frequency[None, :]
    return jnp.cos(angles), jnp.sin(angles)


def dot(left, right):
    return jnp.dot(left, right, preferred_element_type=F32)


def dot_nt(left, right):
    return lax.dot_general(left, right, (((1,), (1,)), ((), ())), preferred_element_type=F32)


def dot_tn(left, right):
    return lax.dot_general(left, right, (((0,), (0,)), ((), ())), preferred_element_type=F32)


LOG2E = 1.4426950408889634


def last_visible(place_ref, low, lanes, block):
    shard, prefix = place_ref[0], place_ref[2]
    at = shard % 2 if low else 2 + shard % 2
    position = at * block + lax.broadcasted_iota(jnp.int32, (1, lanes), 1) % block
    return jnp.maximum(position + 1, prefix)


def query_start(place_ref, low, block):
    chip = place_ref[0] // 2
    return pl.multiple_of((chip if low else 1 - chip) * block, block)


def natural_rows(place_ref, own, near, into, block):
    shard = place_ref[0]
    for slot, value in (
        (0, own[0, :block]),
        (2, own[0, block:]),
        (1, near[0, :block]),
        (3, near[0, block:]),
    ):
        into[pl.ds(pl.multiple_of((shard ^ slot) * block, block), block)] = value


def hide(scores, limit, first_key):
    keys = first_key + lax.broadcasted_iota(jnp.int32, scores.shape, 0)
    return jnp.where(keys < limit, scores, MASKED_SCORE)


def masked_by_part(low, scores, limit, block):
    if low:
        return hide(scores, limit, 0)
    half = 2 * block
    return jnp.concatenate([scores[:half], hide(scores[half:], limit, half)], axis=0)


def attend_kernel(place, q, k_own, k_near, v_own, v_near, out, lse, keys, values, *, scale):
    block = q.shape[1] // 2
    group = q.shape[0]
    natural_rows(place, k_own, k_near, keys, block)
    natural_rows(place, v_own, v_near, values, block)
    values_t = values[...].T
    for part, low in enumerate((True, False)):
        count = (2 if low else 4) * block
        rows = pl.ds(query_start(place, low, block), block)
        query = jnp.concatenate([q[j, rows] for j in range(group)], axis=0)
        limit = last_visible(place, low, group * block, block)
        scores = masked_by_part(low, dot_nt(keys[:count], query), limit, block)
        top = jnp.max(scores, axis=0, keepdims=True)
        base = scale * LOG2E
        expo = jnp.exp2(scores * base - top * base)
        total = jnp.sum(expo, axis=0, keepdims=True)
        lse[0, part] = (top * base + jnp.log2(total))[0]
        result = dot(values_t[:, :count], expo.astype(BF16)) / total
        result = result.T.astype(BF16)
        for j in range(group):
            out[j, rows] = result[j * block : (j + 1) * block]


def attend(place, queries, kv_own, kv_near):
    heads, rows, dim = queries.shape
    kv_heads = kv_own.shape[0] // 2
    group = heads // kv_heads
    q_spec = pl.BlockSpec((group, rows, dim), lambda g, p: (g, 0, 0))
    kv_spec = pl.BlockSpec((1, rows, dim), lambda g, p: (g, 0, 0))
    v_spec = pl.BlockSpec((1, rows, dim), lambda g, p: (g + kv_heads, 0, 0))
    lse_shape = (kv_heads, 2, group * rows // 2)
    return pl.pallas_call(
        functools.partial(attend_kernel, scale=HEAD_DIM ** (-0.5)),
        out_shape=[
            jax.ShapeDtypeStruct(queries.shape, BF16),
            jax.ShapeDtypeStruct(lse_shape, F32),
        ],
        grid_spec=pltpu.PrefetchScalarGridSpec(
            num_scalar_prefetch=1,
            grid=(kv_heads,),
            in_specs=[q_spec, kv_spec, kv_spec, v_spec, v_spec],
            out_specs=[q_spec, pl.BlockSpec((1, *lse_shape[1:]), lambda g, p: (g, 0, 0))],
            scratch_shapes=[pltpu.VMEM((2 * rows, dim), BF16)] * 2,
        ),
        compiler_params=pltpu.CompilerParams(vmem_limit_bytes=64 * 2**20),
        cost_estimate=work(EST),
        name="attend",
    )(place, queries, kv_own, kv_near, kv_own, kv_near)


def attend_back_kernel(
    place, q, k_own, k_near, v_own, v_near, grad, lse, cos_t, sin_t, *rest, scale
):
    dq, own_out, send_out, keys, values, dk, dv = rest[-7:]
    block = q.shape[1] // 2
    group = q.shape[0]
    half = HEAD_DIM // 2
    natural_rows(place, k_own, k_near, keys, block)
    natural_rows(place, v_own, v_near, values, block)
    keys_t = keys[...].T
    for part, low in ((1, False), (0, True)):
        count = (2 if low else 4) * block
        start = query_start(place, low, block)
        rows = pl.ds(start, block)
        query = jnp.concatenate([q[j, rows] for j in range(group)], axis=0)
        out_grad = jnp.concatenate([grad[j, rows] for j in range(group)], axis=0)
        limit = last_visible(place, low, group * block, block)
        scores = masked_by_part(low, dot_nt(keys[:count], query), limit, block)
        probs = jnp.exp2(scores * (scale * LOG2E) - lse[0, part][None])
        probs_grad = dot_nt(values[:count], out_grad)
        mean = jnp.sum(probs * probs_grad, axis=0, keepdims=True)
        score_grad = (probs * (probs_grad - mean)).astype(BF16)
        v_part = dot(probs.astype(BF16), out_grad)
        k_part = dot(score_grad, query) * scale
        if low:
            dk[:count] += k_part
            dv[:count] += v_part
        else:
            dk[...] = k_part
            dv[...] = v_part
        turned = dot(keys_t[:, :count], score_grad) * scale
        cos = jnp.concatenate([cos_t[:, rows]] * group, axis=1)
        sin = jnp.concatenate([sin_t[:, rows]] * group, axis=1)
        u, w = turned[:half], turned[half : 2 * half]
        pad = jnp.zeros((q.shape[2] - 2 * half, u.shape[1]), F32)
        turned = jnp.concatenate([u * cos + w * sin, w * cos - u * sin, pad], axis=0)
        turned = turned.T.astype(BF16)
        for j in range(group):
            dq[j, rows] = turned[j * block : (j + 1) * block]
    shard = place[0]
    for slot, at, own in ((0, 0, True), (2, 1, True), (1, 0, False), (3, 1, False)):
        rows = pl.ds(pl.multiple_of((shard ^ slot) * block, block), block)
        to = slice(at * block, (at + 1) * block)
        out = own_out if own else send_out
        out[0, 0, to] = dk[rows].astype(out.dtype)
        out[1, 0, to] = dv[rows].astype(out.dtype)


def attend_back(place, queries, kv_own, kv_near, grad, lse, cos_t, sin_t, part, parts, ties):
    heads, rows, dim = queries.shape
    kv_heads = kv_own.shape[0] // 2
    group = heads // kv_heads
    count = kv_heads // parts
    base = part * count
    q_spec = pl.BlockSpec((group, rows, dim), lambda g, p: (g + base, 0, 0))
    kv_spec = pl.BlockSpec((1, rows, dim), lambda g, p: (g + base, 0, 0))
    v_spec = pl.BlockSpec((1, rows, dim), lambda g, p: (g + base + kv_heads, 0, 0))
    whole = pl.BlockSpec(cos_t.shape, lambda g, p: (0, 0))
    return pl.pallas_call(
        functools.partial(attend_back_kernel, scale=HEAD_DIM ** (-0.5)),
        out_shape=[
            jax.ShapeDtypeStruct((heads // parts, rows, dim), BF16),
            jax.ShapeDtypeStruct((2, count, rows, dim), F32),
            jax.ShapeDtypeStruct((2, count, rows, dim), BF16),
        ],
        grid_spec=pltpu.PrefetchScalarGridSpec(
            num_scalar_prefetch=1,
            grid=(count,),
            in_specs=[q_spec, kv_spec, kv_spec, v_spec, v_spec]
            + [q_spec, pl.BlockSpec((1, *lse.shape[1:]), lambda g, p: (g + base, 0, 0)), whole, whole]
            + [pl.BlockSpec(memory_space=pltpu.HBM)] * len(ties),
            out_specs=[pl.BlockSpec((group, rows, dim), lambda g, p: (g, 0, 0))] + [pl.BlockSpec((2, 1, rows, dim), lambda g, p: (0, g, 0, 0))] * 2,
            scratch_shapes=[pltpu.VMEM((2 * rows, dim), BF16)] * 2
            + [pltpu.VMEM((2 * rows, dim), F32)] * 2,
        ),
        compiler_params=pltpu.CompilerParams(vmem_limit_bytes=64 * 2**20),
        cost_estimate=work(1),
        name=f"attend_back_{part}",
    )(place, queries, kv_own, kv_near, kv_own, kv_near, grad, lse, cos_t, sin_t, *ties)


def row_copies(sources, refs, into, sems):
    copies, at = [], into.shape[0] // 2
    for ref, (_, base, count) in zip(refs, sources):
        for c in range(into.shape[1] // PANEL):
            copies.append(
                pltpu.make_async_copy(
                    ref.at[pl.ds(base + c * count, count)],
                    into.at[pl.ds(at, count), pl.ds(c * PANEL, PANEL)],
                    sems.at[len(copies)],
                )
            )
        at += count
    return copies


class Landing:
    def __init__(self, place, bundle, refs, targets, sems):
        used = sources_of(bundle)
        n = len(used)
        own = dict(zip(used, refs[:n]))
        near = {} if bundle.joined else dict(zip(used, refs[n : 2 * n]))
        listed = land_copies(place, bundle, own, near, refs[-2], refs[-1], targets)
        self.copies = [
            (key, pltpu.make_async_copy(src, dst, sems.at[i])) for i, (src, dst, key) in enumerate(listed)
        ]
        self.copies.sort(key=lambda c: c[0])
        for _, c in self.copies:
            c.start()

    def wait(self, wanted=None):
        left = []
        for key, c in self.copies:
            if wanted is None or wanted(key):
                c.wait()
            else:
                left.append((key, c))
        self.copies = left


def landing_operands(bundle, weights, near, here, there):
    used = sources_of(bundle)
    return [weights[i] for i in used] + ([] if bundle.joined else [near[i] for i in used]) + [here, there]


def landing_count(bundle):
    return sum((1 if bundle.joined else 2) * len(p.parts) + 3 for p in bundle.first + bundle.second)


NO_BUNDLE = Bundle((), (), ())


def kernel_call(body, place, bundle, landing, operands, outs, scratch, name, time=0.5, ties=()):
    operands = [*operands, *((t, HB) for t in ties)]
    n_land, n_in, n_out, n_w = len(landing), len(operands), len(outs), len(bundle.shapes)

    def kernel(place_ref, *refs):
        land, refs = refs[:n_land], refs[n_land:]
        ins, refs = refs[: n_in - len(ties)], refs[n_in:]
        out, refs = refs[:n_out], refs[n_out:]
        body(place_ref, land, ins, out, refs[:n_w], refs[n_w], refs[n_w + 1 :])

    def spec(where):
        return where if isinstance(where, pl.BlockSpec) else pl.BlockSpec(memory_space=where)

    return pl.pallas_call(
        kernel,
        out_shape=[o for o, _ in outs],
        grid_spec=pltpu.PrefetchScalarGridSpec(
            num_scalar_prefetch=1,
            grid=(1,),
            in_specs=[spec(pltpu.HBM)] * n_land + [spec(w) for _, w in operands],
            out_specs=[spec(w) for _, w in outs],
            scratch_shapes=[pltpu.VMEM(sh, BF16) for sh in bundle.shapes]
            + [pltpu.SemaphoreType.DMA((max(landing_count(bundle), 1),))]
            + list(scratch),
        ),
        compiler_params=pltpu.CompilerParams(vmem_limit_bytes=64 * 2**20),
        cost_estimate=work(time),
        name=name,
    )(place, *landing, *[a for a, _ in operands])


VM = pltpu.VMEM
HB = pltpu.HBM


def like(shape, dtype):
    return jax.ShapeDtypeStruct(shape, dtype)


def turn(value, cos_full, sin_signed, half):
    swapped = jnp.concatenate([value[:, half:], value[:, :half]], axis=1)
    return value * cos_full + swapped * sin_signed


def padded(value):
    return jnp.concatenate([value, jnp.zeros((value.shape[0], LANES - HEAD_DIM), value.dtype)], axis=1)


def one_of_pair(block, width):
    return pl.BlockSpec((None, block, width), lambda i, p: (p[0] // 2, 0, 0))


def qkv_forward(place, bundle, landing, tokens, tokens_back, gain, inner, outer, cos, sin, ties):
    _, block, width = tokens.shape
    rows = 2 * block
    total = bundle.shapes[0][1]
    kv = (total - width) // 2
    wide = 8 * HEAD_DIM
    half = HEAD_DIM // 2

    def body(pr, land_refs, ins, outs, weights, sems, scratch):
        kept, *backs, gain_ref, inner_ref, outer_ref, cos_ref, sin_ref = ins
        q, kv_ref, hidden_ref, normed_ref, x_ref = outs
        (w,) = weights
        arriving = row_copies(tokens_back, backs, x_ref, scratch[0])
        for c in arriving:
            c.start()
        landing = Landing(pr, bundle, land_refs, weights, sems)
        x_ref[:block] = kept[...]
        for c in arriving:
            c.wait()
        x = x_ref[...].astype(F32)
        scale = lax.rsqrt(jnp.mean(x * x, axis=-1, keepdims=True) + EPSILON)
        normed_ref[...] = (x * scale * gain_ref[...].astype(F32)).astype(BF16)
        hidden_ref[...] = dot_nt(normed_ref[...], inner_ref[...]).astype(BF16)

        def columns(at):
            cols = pl.ds(at, wide)
            return dot(normed_ref[...], w[:, cols]) + dot(hidden_ref[...], outer_ref[:, cols])

        landing.wait(lambda key: key[1] < width)
        for i in range(width // wide):
            acc = columns(i * wide)
            for h in range(8):
                one = acc[:, h * HEAD_DIM : (h + 1) * HEAD_DIM]
                q[8 * i + h] = padded(turn(one, cos_ref[...], sin_ref[...], half)).astype(BF16)
        landing.wait()
        acc = columns(width)
        for h in range(8):
            one = acc[:, h * HEAD_DIM : (h + 1) * HEAD_DIM]
            kv_ref[h] = padded(turn(one, cos_ref[...], sin_ref[...], half)).astype(BF16)
        acc = columns(width + kv)
        for h in range(8):
            kv_ref[8 + h] = padded(acc[:, h * HEAD_DIM : (h + 1) * HEAD_DIM]).astype(BF16)

    heads = width // HEAD_DIM
    return kernel_call(
        body, place, bundle, landing,
        [(tokens, one_of_pair(block, width)), *((t[0], HB) for t in tokens_back), (gain, VM), (inner, VM), (outer, VM), (cos, VM), (sin, VM)],
        [
            (like((heads, rows, LANES), BF16), VM),
            (like((2 * kv // HEAD_DIM, rows, LANES), BF16), VM),
            (like((rows, inner.shape[0]), BF16), VM),
            (like((rows, width), BF16), VM),
            (like((rows, width), BF16), VM),
        ],
        [pltpu.SemaphoreType.DMA((len(tokens_back) * width // PANEL,))], "qkv_forward", time=EST, ties=ties,
    )


def out_forward(place, bundle, landing, heads_out, x, gain, inner, outer, cot, cot_back, inner_gl, drop_b):
    rows, width = x.shape
    heads = heads_out.shape[0]

    def body(pr, land_refs, ins, outs, weights, sems, scratch):
        heads_ref, x_ref, gain_ref, inner_ref, outer_ref, cot_kept, *cot_got, igl, db = ins
        middle, normed, attended, hidden, cot_ref, h_gl, h_d = outs
        arriving = row_copies(cot_back, cot_got, cot_ref, scratch[0])
        for c in arriving:
            c.start()
        landing = Landing(pr, bundle, land_refs, weights, sems)
        for h in range(heads):
            attended[:, h * HEAD_DIM : (h + 1) * HEAD_DIM] = heads_ref[h, :, :HEAD_DIM]
        hidden[...] = dot_nt(attended[...], inner_ref[...]).astype(BF16)
        cot_ref[: rows // 2] = cot_kept[...]
        for c in arriving:
            c.wait()
        h_d[...] = dot_nt(cot_ref[...], db[...]).astype(BF16)
        landing.wait()
        wide = width // 2
        squares = jnp.zeros((rows, 1), F32)
        for i in range(2):
            cols = pl.ds(i * wide, wide)
            branch = dot(attended[...], weights[0][:, cols]) + dot(hidden[...], outer_ref[:, cols])
            value = x_ref[:, cols].astype(F32) + branch
            middle[:, cols] = value
            squares += jnp.sum(value * value, axis=-1, keepdims=True)
        scale = lax.rsqrt(squares / width + EPSILON)
        normed[...] = (middle[...] * scale * gain_ref[...].astype(F32)).astype(BF16)
        h_gl[...] = dot_nt(normed[...], igl[...]).astype(BF16)

    return kernel_call(
        body, place, bundle, landing,
        [(heads_out, VM), (x, VM), (gain, VM), (inner, VM), (outer, VM),
         (cot, one_of_pair(rows // 2, width)), *((c[0], HB) for c in cot_back), (inner_gl, VM), (drop_b, VM)],
        [
            (like((rows, width), F32), VM),
            (like((rows, width), BF16), VM),
            (like((rows, width), BF16), VM),
            (like((rows, RANK), BF16), VM),
            (like((rows, width), BF16), VM),
            (like((rows, 2 * RANK), BF16), VM),
            (like((rows, RANK), BF16), VM),
        ],
        [pltpu.SemaphoreType.DMA((len(cot_back) * width // PANEL,))], "out_forward", time=EST,
    )


def mlp_chunk(place, bundle, landing, normed, cot, hidden_gl, hidden_d, outer_gl, drop_a, chunk, sums, name):
    rows, width = normed.shape
    units = bundle.shapes[1][0]
    steps = units // PANEL
    first = sums is None
    part = units // 4

    def body(pr, land_refs, ins, outs, weights, sems, scratch):
        normed_ref, cot_ref, hgl_ref, hd_ref, ogl, da = ins[:6]
        drop_sum, e_sum, thin, keep, send = outs
        (packed,) = scratch
        w_gl, w_d = weights
        landing = Landing(pr, bundle, land_refs, weights, sems)
        h_d = hd_ref[...]
        h_g, h_l = hgl_ref[:, :RANK], hgl_ref[:, RANK:]
        g_t, l_t, d_t = h_g.T, h_l.T, h_d.T
        for i in range(steps):
            landing.wait(lambda key: key[0] == 1 or key[1] < 2 * (i + 1) * PANEL)
            cols = slice(i * PANEL, (i + 1) * PANEL)
            both = pl.ds(2 * i * PANEL, 2 * PANEL)
            acts = dot(normed_ref[...], w_gl[:, both])
            gate = acts[:, :PANEL] + dot(h_g, ogl[:RANK, cols])
            lift = acts[:, PANEL:] + dot(h_l, ogl[RANK:, cols])
            a_grad = dot_nt(cot_ref[...], w_d[cols]) + dot(h_d, da[:, cols])
            sig = 1.0 / (1.0 + jnp.exp(-gate))
            silu = gate * sig
            active = (silu * lift).astype(BF16)
            gate_grad = (a_grad * lift * sig * (1.0 + gate * (1.0 - sig))).astype(BF16)
            lift_grad = (a_grad * silu).astype(BF16)
            grads = jnp.concatenate([gate_grad, lift_grad], axis=1)
            down = dot(active, w_d[cols])
            back = dot_nt(grads, w_gl[:, both])
            t0 = dot_nt(active, da[:, cols])
            t1 = dot_nt(gate_grad, ogl[:RANK, cols])
            t2 = dot_nt(lift_grad, ogl[RANK:, cols])
            if i == 0 and first:
                drop_sum[...] = down
                e_sum[...] = back
                thin[0], thin[1], thin[2] = t0, t1, t2
            elif i == 0:
                drop_sum[...] = ins[6][...] + down
                e_sum[...] = ins[7][...] + back
                thin[0], thin[1], thin[2] = ins[8][0] + t0, ins[8][1] + t1, ins[8][2] + t2
            else:
                drop_sum[...] += down
                e_sum[...] += back
                thin[0] += t0
                thin[1] += t1
                thin[2] += t2
            per = PANEL // part
            for j, g in enumerate((dot(g_t, gate_grad), dot(l_t, lift_grad), dot(d_t, active))):
                for o in range(per):
                    packed[i * per + o, :, j * part : (j + 1) * part] = g[:, o * part : (o + 1) * part]
        split_by_core(pr, packed, keep, send)

    at_chunk = lambda i, p: (chunk, 0, 0)
    operands = [
        (normed, VM), (cot, VM), (hidden_gl, VM), (hidden_d, VM),
        (outer_gl, pl.BlockSpec((None, *outer_gl.shape[1:]), at_chunk)),
        (drop_a, pl.BlockSpec((None, *drop_a.shape[1:]), at_chunk)),
    ]
    if not first:
        operands += [(s, VM) for s in sums]
    return kernel_call(
        body, place, bundle, landing, operands,
        [
            (like((rows, width), F32), VM),
            (like((rows, width), F32), VM),
            (like((3, rows, RANK), F32), VM),
            (like((2, RANK, 3 * part), F32), VM),
            (like((2, RANK, 3 * part), BF16), VM),
        ],
        [pltpu.VMEM((4, RANK, 3 * part), F32)], name, time=EST,
    )


def split_by_core(place_ref, whole, keep, send):
    core = place_ref[0] % 2
    for j in range(2):
        keep[j] = whole[core + 2 * j]
        send[j] = whole[1 - core + 2 * j].astype(BF16)


def out_backward(place, bundle, landing, sums, middle, cot, gain, normed, attended, hidden, factors, ties):
    rows, width = middle.shape
    heads = width // HEAD_DIM

    def body(pr, land_refs, ins, outs, weights, sems, scratch):
        drop_sum, e_sum, thin, middle_ref, cot_ref, gain_ref, normed_ref, att, hid, drop_b, igl, o_a, o_b = ins
        mixed_kept, mixed_back, mid_grad, out_heads, keep, send = outs
        (w,) = weights
        branch, whole = scratch
        landing = Landing(pr, bundle, land_refs, weights, sems)
        d_hid = thin[0].astype(BF16)
        gl_grad = jnp.concatenate([thin[1].astype(BF16), thin[2].astype(BF16)], axis=1)
        e_in = (e_sum[...] + dot(gl_grad, igl[...])) * gain_ref[...].astype(F32)
        mid = middle_ref[...]
        scale = lax.rsqrt(jnp.mean(mid * mid, axis=-1, keepdims=True) + EPSILON)
        n = mid * scale
        mean = jnp.mean(e_in * n, axis=-1, keepdims=True)
        mid_grad[...] = cot_ref[...].astype(F32) + scale * (e_in - n * mean)
        branch[...] = mid_grad[...].astype(BF16)
        hgrad = dot_nt(branch[...], o_b[...]).astype(BF16)
        landing.wait()
        wide = 8 * HEAD_DIM
        for i in range(heads // 8):
            part = slice(i * wide, (i + 1) * wide)
            grad = dot_nt(branch[...], w[part]) + dot(hgrad, o_a[:, part])
            for h in range(8):
                out_heads[8 * i + h] = padded(grad[:, h * HEAD_DIM : (h + 1) * HEAD_DIM]).astype(BF16)
        mixed = (mid + drop_sum[...] + dot(d_hid, drop_b[...])).astype(BF16)
        mixed_kept[...] = mixed[: rows // 2]
        mixed_back[...] = mixed[rows // 2 :]
        gl = dot(gl_grad.T, normed_ref[...])
        own = (
            dot(d_hid.T, cot_ref[...]), gl[:RANK], gl[RANK:],
            dot(hgrad.T, att[...]), dot(hid[...].T, branch[...]),
        )
        for t in range(4):
            for j, g in enumerate(own):
                at = j * quarter
                whole[t, :, at : at + quarter] = g[:, t * quarter : (t + 1) * quarter]
        split_by_core(pr, whole, keep, send)

    quarter = width // 4
    cols = 5 * quarter
    return kernel_call(
        body, place, bundle, landing,
        [(v, VM) for v in (*sums, middle, cot, gain, normed, attended, hidden, *factors)],
        [
            (like((2, rows // 2, width), BF16), one_of_pair(rows // 2, width)),
            (like((rows // 2, width), BF16), VM),
            (like((rows, width), F32), VM),
            (like((heads, rows, LANES), BF16), VM),
            (like((2, RANK, cols), F32), VM),
            (like((2, RANK, cols), BF16), VM),
        ],
        [pltpu.VMEM((rows, width), BF16), pltpu.VMEM((4, RANK, cols), F32)], "out_backward", time=15, ties=ties,
    )


def qkv_gradients(place, parts, cos, sin, normed, hidden, outer, ties):
    rows, width = normed.shape
    total = outer.shape[1]
    kv = (total - width) // 2
    half = HEAD_DIM // 2
    rank3 = outer.shape[0]
    quarter, kv_quarter = width // 4, kv // 4
    cols = 4 * quarter + 2 * kv_quarter
    q_count, kv_count = parts[0][0].shape[0], parts[0][1].shape[1]

    def body(pr, land_refs, ins, outs, weights, sems, scratch):
        *part_refs, cos_ref, sin_ref, nrm, hid, b = ins
        dq_refs, dkv_refs, got_refs = part_refs[0::3], part_refs[1::3], part_refs[2::3]
        g, hgrad_ref, keep, send = outs
        (whole,) = scratch
        for h in range(width // HEAD_DIM):
            ref, i = dq_refs[h // q_count], h % q_count
            g[:, h * HEAD_DIM : (h + 1) * HEAD_DIM] = ref[i, :, :HEAD_DIM]
        for h in range(kv // HEAD_DIM):
            dkv_ref, got_ref, i = dkv_refs[h // kv_count], got_refs[h // kv_count], h % kv_count
            one = (dkv_ref[0, i] + got_ref[0, i].astype(F32))[:, :HEAD_DIM]
            at = width + h * HEAD_DIM
            g[:, at : at + HEAD_DIM] = turn(one, cos_ref[...], -sin_ref[...], half).astype(BF16)
            at += kv
            g[:, at : at + HEAD_DIM] = (dkv_ref[1, i] + got_ref[1, i].astype(F32))[:, :HEAD_DIM].astype(BF16)
        hgrad_ref[...] = dot_nt(g[...], b[...]).astype(BF16)
        g_in = dot(hgrad_ref[...].T, nrm[...])
        g_out = dot(hid[...].T, g[...])
        for t in range(4):
            for i in range(3):
                whole[t, :, i * quarter : (i + 1) * quarter] = g_in[
                    i * RANK : (i + 1) * RANK, t * quarter : (t + 1) * quarter
                ]
            whole[t, :, 3 * quarter : 4 * quarter] = g_out[:RANK, t * quarter : (t + 1) * quarter]
            for i in range(2):
                at, start = 4 * quarter + i * kv_quarter, width + i * kv + t * kv_quarter
                whole[t, :, at : at + kv_quarter] = g_out[
                    (1 + i) * RANK : (2 + i) * RANK, start : start + kv_quarter
                ]
        split_by_core(pr, whole, keep, send)

    return kernel_call(
        body, place, NO_BUNDLE, [],
        [(v, VM) for v in (*[v for p in parts for v in p], cos, sin, normed, hidden, outer)],
        [
            (like((rows, total), BF16), VM),
            (like((rows, rank3), BF16), VM),
            (like((2, RANK, cols), F32), VM),
            (like((2, RANK, cols), BF16), VM),
        ],
        [pltpu.VMEM((4, RANK, cols), F32)], "qkv_gradients", time=1, ties=ties,
    )


def qkv_backward(place, bundle, landing, g, hgrad, x, mid_grad, gain, inner, ties):
    rows, width = x.shape
    total = bundle.shapes[0][1]
    block = rows // 2

    def body(pr, land_refs, ins, outs, weights, sems, scratch):
        g_ref, hg, x_ref, mg, gain_ref, a = ins
        kept, back = outs
        (w,) = weights
        landing = Landing(pr, bundle, land_refs, weights, sems)
        xf = x_ref[...].astype(F32)
        scale = lax.rsqrt(jnp.mean(xf * xf, axis=-1, keepdims=True) + EPSILON)
        n = xf * scale
        thin = dot(hg[...], a[...])
        landing.wait()
        e_in = (dot_nt(g_ref[...], w[...]) + thin) * gain_ref[...].astype(F32)
        mean = jnp.mean(e_in * n, axis=-1, keepdims=True)
        result = mg[...] + scale * (e_in - n * mean)
        kept[...] = result[:block]
        back[...] = result[block:].astype(BF16)

    return kernel_call(
        body, place, bundle, landing,
        [(v, VM) for v in (g, hgrad, x, mid_grad, gain, inner)],
        [(like((2, block, width), F32), one_of_pair(block, width)), (like((block, width), BF16), VM)],
        [], "qkv_backward", time=0.2, ties=ties,
    )


def complete(place, partial, back, ties, name):
    _, block, width = partial.shape

    def kernel(place_ref, partial_ref, back_ref, *rest):
        rest[-1][...] = back_ref[...].astype(partial.dtype)

    return pl.pallas_call(
        kernel,
        out_shape=jax.ShapeDtypeStruct(partial.shape, partial.dtype),
        grid_spec=pltpu.PrefetchScalarGridSpec(
            num_scalar_prefetch=1,
            grid=(1,),
            in_specs=[pl.BlockSpec(memory_space=pltpu.HBM), pl.BlockSpec(memory_space=pltpu.VMEM)]
            + [pl.BlockSpec(memory_space=pltpu.HBM)] * len(ties),
            out_specs=pl.BlockSpec((None, block, width), lambda i, p: (1 - p[0] // 2, 0, 0)),
        ),
        input_output_aliases={1: 0},
        compiler_params=pltpu.CompilerParams(vmem_limit_bytes=64 * 2**20),
        cost_estimate=work(0.5),
        name=name,
    )(place, partial, back, *ties)


def pack_factors(place, inners, outers):
    widths = [a.shape[0] for a in inners] + [b.shape[1] for b in outers]
    n = len(inners)
    mix = outers[0].shape[0]
    narrow = (n + 1, n + 2)

    def body(pr, land_refs, ins, outs, weights, sems, scratch):
        for which, out in enumerate(outs):
            row = lax.broadcasted_iota(jnp.int32, (RANK, mix), 0) + pr[3 + which] * RANK
            choose = (row == lax.broadcasted_iota(jnp.int32, (RANK, mix), 1)).astype(F32).astype(BF16)
            at = 0
            for i, ref in enumerate(ins):
                part = dot_nt(choose, ref[...]) if i < n or i in narrow else dot(choose, ref[...])
                out[:, at : at + widths[i]] = part.astype(BF16)
                at += widths[i]

    shape = (like((RANK, sum(widths)), BF16), VM)
    return kernel_call(
        body, place, NO_BUNDLE, [], [(v.T if i in narrow else v, VM) for i, v in enumerate((*inners, *outers))],
        [shape, shape], [], "pack_factors",
    )


def unpack_factors(place, slots, widths, chunks):
    inner_w, outer_w = widths[:7], widths[7:]
    width, kv = 4 * outer_w[0], 4 * outer_w[1]
    part = outer_w[4] // chunks
    starts = [sum(widths[:i]) for i in range(len(widths))]

    def body(pr, land_refs, ins, outs, weights, sems, scratch):
        iq, oq, io, oo, igl, ogl, da, db = outs
        (nat,) = scratch
        mine, two, got = ins
        nat[pr[0]] = mine[...]
        nat[pr[0] ^ 2] = two[...]
        nat[pr[0] ^ 1] = got[:RANK]
        nat[pr[0] ^ 3] = got[RANK:]
        oq[...] = jnp.zeros(oq.shape, BF16)
        for t in range(4):
            get = lambda i, a=0, n=None: nat[t, :, starts[i] + a : starts[i] + a + (n or widths[i])]
            w = inner_w[0]
            here = slice(t * w, (t + 1) * w)
            for i in range(3):
                iq[i * RANK : (i + 1) * RANK, here] = get(i)
            io[:, here] = get(3)
            igl[:RANK, here] = get(4)
            igl[RANK:, here] = get(5)
            base = 0
            for i in range(3):
                n = outer_w[i]
                oq[i * RANK : (i + 1) * RANK, base + t * n : base + (t + 1) * n] = get(7 + i)
                base += 4 * n
            oo[:, here] = get(10)
            db[:, here] = get(13)
            for u in range(chunks):
                there = slice(t * part, (t + 1) * part)
                ogl[u, :RANK, there] = get(11, u * part, part)
                ogl[u, RANK:, there] = get(12, u * part, part)
                da[u, :, there] = get(6, u * part, part)

    shapes = [
        (3 * RANK, width), (3 * RANK, width + 2 * kv), (RANK, width), (RANK, width), (2 * RANK, width),
        (chunks, 2 * RANK, 4 * part), (chunks, RANK, 4 * part), (RANK, width),
    ]
    return kernel_call(
        body, place, NO_BUNDLE, [], [(v, VM) for v in slots], [(like(sh, BF16), VM) for sh in shapes],
        [pltpu.VMEM((4, *slots[0].shape), BF16)], "unpack_factors",
    )


def fold_cores(place, sums, name, ties=()):
    n = len(sums)
    cols = sum(k.shape[2] for k, _ in sums)

    def body(pr, land_refs, ins, outs, weights, sems, scratch):
        chip = pr[0] // 2
        for out, which in zip(outs, (chip, 1 - chip)):
            at = 0
            for keep_ref, got_ref in zip(ins[:n], ins[n:]):
                w = keep_ref.shape[2]
                out[:, at : at + w] = (keep_ref[which] + got_ref[which].astype(F32)).astype(BF16)
                at += w
            out[:, cols:] = jnp.full((RANK, LANES), pr[3], jnp.int32).astype(F32).astype(BF16)

    shape = (like((RANK, cols + LANES), BF16), VM)
    return kernel_call(
        body, place, NO_BUNDLE, [], [(k, VM) for k, _ in sums] + [(g, VM) for _, g in sums],
        [shape, shape], [], name, ties=ties,
    )


def spread_sums(place, groups, pieces, mix, name, ties=()):
    count = sum(v.shape[0] for v in groups[0])
    tall = [len(g) > 1 for g in groups]

    def body(pr, land_refs, ins, outs, weights, sems, scratch):
        gots, at, held = [], 0, list(scratch)
        for g in groups:
            refs = ins[at : at + len(g)]
            at += len(g)
            if len(g) == 1:
                gots.append(refs[0])
                continue
            got, row = held.pop(0), 0
            for ref in refs:
                got[row : row + ref.shape[0]] = ref[...]
                row += ref.shape[0]
            gots.append(got)
        tag = gots[0][:, -LANES:].astype(F32).astype(jnp.int32) * RANK
        spot = tag + lax.broadcasted_iota(jnp.int32, (count, LANES), 0) % RANK
        choose = (spot == lax.broadcasted_iota(jnp.int32, (count, LANES), 1)).astype(F32).astype(BF16)
        choose_t = choose.T
        for out, (is_inner, runs) in zip(outs, pieces):
            at = 0
            for g, start, n in runs:
                if is_inner:
                    out[at : at + n] = dot_tn(gots[g][:, start : start + n], choose)
                else:
                    out[:, at : at + n] = dot(choose_t, gots[g][:, start : start + n])
                at += n

    outs = []
    for is_inner, runs in pieces:
        n = sum(c for _, _, c in runs)
        outs.append((like((n, mix) if is_inner else (mix, n), F32), VM))
    scratch = [pltpu.VMEM((count, g[0].shape[1]), BF16) for g, t in zip(groups, tall) if t]
    return kernel_call(
        body, place, NO_BUNDLE, [], [(v, VM) for g in groups for v in g], outs, scratch, name, ties=ties
    )


def local(
    tokens,
    cotangent,
    prefix_len,
    adapter_index,
    gain_attn,
    gain_mlp,
    query_weight,
    key_weight,
    value_weight,
    output_weight,
    gate_weight,
    lift_weight,
    drop_weight,
    *factors,
):
    _, block, width = tokens.shape
    rep, shard = lax.axis_index("rep"), lax.axis_index("shard")
    chip = shard // 2
    rows = 2 * block
    kv_width = KV_HEADS * HEAD_DIM
    where = jnp.stack([shard, rep % 4]).astype(jnp.int32)
    place = jnp.concatenate(
        [where, jnp.stack([prefix_len[chip], adapter_index[chip], adapter_index[1 - chip]])]
    )

    weights = (query_weight, key_weight, value_weight, output_weight, gate_weight, lift_weight, drop_weight)
    inners, outers = factors[0::2], factors[1::2]
    widths = [a.shape[0] for a in inners] + [b.shape[1] for b in outers]
    chunks = 4
    ff = gate_weight.shape[1]
    bundles = make_bundles(width, kv_width, ff, chunks, 4)
    positions = jnp.concatenate(
        [shard * block + jnp.arange(block), (shard ^ 2) * block + jnp.arange(block)]
    )
    cos_table, sine_table = rotary_tables(positions.astype(F32), HEAD_DIM)
    cos_full = jnp.concatenate([cos_table, cos_table], axis=1)
    sin_full = jnp.concatenate([-sine_table, sine_table], axis=1)
    gain_one, gain_two = gain_attn[None], gain_mlp[None]
    cos_t, sin_t = cos_table.T, sine_table.T

    relay = Relay(where, weights, bundles)
    half = block // 2
    near = {i: to_core(weights[i]) for i in (4, 5, 6)}
    relay.step()
    mine, others = pack_factors(place, inners, outers)
    slot_two = to_chip(others)
    (tokens_a,), _ = relay.step([(tokens, 0, half)], ties=(near[4], near[5], sin_full, cos_full, cos_t, sin_t, gain_one, gain_two, place))
    (tokens_b,), _ = relay.step([(tokens, half, half)], ties=(slot_two,))
    joined = join(mine, slot_two)
    got = to_core(joined)
    relay.step(ties=(near[6], got))
    inner_qkv, outer_qkv, inner_o, outer_o, inner_gl, outer_gl, drop_a, drop_b = unpack_factors(
        place, (mine, slot_two, got), widths, chunks
    )

    def landing(i):
        return landing_operands(bundles[i], weights, near, relay.here[i], relay.there[i])

    (cot_a,), begun = relay.step([(cotangent, 0, half)], ties=(inner_qkv,), across=False)
    queries, kv_own, hidden_qkv, normed_attn, x = qkv_forward(
        place, bundles[0], landing(0), tokens, (tokens_a, tokens_b), gain_one,
        inner_qkv, outer_qkv, cos_full, sin_full, begun[:1],
    )
    (cot_b,), begun = relay.step([(cotangent, half, half)], ties=(x,))
    kv_own = gate(kv_own, begun[:1])
    relay.across(1, begun[:1])
    kv_near = to_core(kv_own)
    heads_out, lse = attend(place, queries, kv_own, kv_near)
    middle, normed_mlp, attended, output_hidden, cot, hidden_gl, hidden_d = out_forward(
        place, bundles[1], landing(1), heads_out, x, gain_two, inner_o, outer_o,
        cotangent, (cot_a, cot_b), inner_gl, drop_b,
    )
    relay.step(ties=(normed_mlp,))
    sums, kept_sums = None, []
    for u in range(chunks):
        *sums, keep, send = mlp_chunk(
            place, bundles[2 + u], landing(2 + u), normed_mlp, cot, hidden_gl, hidden_d,
            outer_gl, drop_a, u, sums, f"mlp_{u}",
        )
        kept_sums.append((keep, to_core(send)))
        if u < 2:
            relay.step(ties=(keep,))
    early = fold_cores(place, kept_sums[:-1], "fold_early", (keep,))
    mixed_kept, mixed_back, middle_grad, grad_heads, keep, send = out_backward(
        place, bundles[1], landing(1), sums, middle, cot, gain_two, normed_mlp, attended,
        output_hidden, (drop_b, inner_gl, inner_o, outer_o), early[:1],
    )

    mixed_back = to_chip(mixed_back)
    early = join(early[0], to_chip(early[1]))
    folded = fold_cores(place, [kept_sums[-1], (keep, to_core(send))], "fold_late")
    parts, halves = [], 2
    for i in range(halves):
        dq, dkv, dkv_send = attend_back(
            place, queries, kv_own, kv_near, grad_heads, lse, cos_t, sin_t, i, halves,
            folded if i else (early,),
        )
        if i:
            late = to_chip(folded[1])
            dkv_send = gate(dkv_send, (late, mixed_back))
        parts.append((dq, dkv, to_core(dkv_send)))
    early = lax.all_gather(early, "rep", axis=0, tiled=True)
    late_both = join(folded[0], late, ties=parts[0][:1])
    late = lax.all_gather(late_both, "rep", axis=0, tiled=True)
    g, hgrad, keep, send = qkv_gradients(
        place, parts, cos_full, sin_full, normed_attn, hidden_qkv, outer_qkv, (late_both,)
    )
    folded = fold_cores(place, [(keep, to_core(send))], "fold_first")
    other = to_chip(folded[1])
    both = join(folded[0], other)
    input_kept, input_back = qkv_backward(
        place, bundles[0], landing(0), g, hgrad, x, middle_grad, gain_one, inner_qkv, (both, early)
    )
    line = [both]
    for k in range(2, lax.axis_size("rep"), 2):
        line.append(move(both, lambda r, s, k=k: (r ^ k, s)))
    line = join(*line, ties=(input_back,))
    input_back = to_chip(gate(input_back, (line,)))
    first = [line, to_y(line)]
    mixed = complete(place, mixed_kept, mixed_back, (), "complete_mixed")

    mix = ADAPTERS * RANK
    w, kw = width // 4, kv_width // 4
    part = ff // 4 // chunks
    wide = 3 * part
    runs = lambda j: [
        (0, u * wide + j * part, part) if u < chunks - 1 else (1, j * part, part) for u in range(chunks)
    ]
    rest = lambda j: [(1, wide + j * w, w)]
    g_out, l_out, d_in, d_out, g_in, l_in, o_in, o_out = spread_sums(
        place, [[early], [late]],
        [(False, runs(0)), (False, runs(1)), (True, runs(2)), (False, rest(0)), (True, rest(1)),
         (True, rest(2)), (True, rest(3)), (False, rest(4))],
        mix, "spread_late",
    )
    q_in, k_in, v_in, q_out, k_out, v_out = spread_sums(
        place, [first],
        [(True, [(0, 0, w)]), (True, [(0, w, w)]), (True, [(0, 2 * w, w)]), (False, [(0, 3 * w, w)]),
         (True, [(0, 4 * w, kw)]), (True, [(0, 4 * w + kw, kw)])],
        mix, "spread_first", (o_out,),
    )
    k_out, v_out = k_out.T, v_out.T
    input_grad = complete(place, input_kept, input_back, (q_in,), "complete_input_grad")
    return (mixed, input_grad, q_in, q_out, k_in, k_out, v_in, v_out, o_in, o_out,
            g_in, g_out, l_in, l_out, d_in, d_out)


def solution(mesh):
    token_place = P("rep", "shard", None)
    row, col = P("shard", None), P(None, "shard")
    return jax.shard_map(
        local,
        mesh=mesh,
        in_specs=(token_place, token_place, P("rep"), P("rep"), P(), P()) + (row,) * 7 + (row, col) * 7,
        out_specs=(token_place, token_place) + (row, col) * 7,
        check_vma=False,
    )
```

```python
import functools
import math
from typing import NamedTuple

import jax
import jax.numpy as jnp
from jax import lax
from jax.experimental import pallas as pl
from jax.experimental.pallas import tpu as pltpu
from jax.sharding import PartitionSpec as P

HEADS = 16
KV_HEADS = 8
HEAD_DIM = 96
RANK = 16
ADAPTERS = 8
EPSILON = 1e-05
ROPE_BASE = 100000.0
MASKED_SCORE = -1e30
AXES = ("rep", "shard")
F32 = jnp.float32
BF16 = jnp.bfloat16


def move(value, target):
    reps, shards = lax.axis_size("rep"), lax.axis_size("shard")
    pairs = []
    for r in range(reps):
        for s in range(shards):
            r2, s2 = target(r, s)
            pairs.append((r * shards + s, r2 * shards + s2))
    return lax.ppermute(value, AXES, pairs)


def to_core(value):
    return move(value, lambda r, s: (r, s ^ 1))


def to_chip(value):
    return move(value, lambda r, s: (r, s ^ 2))


def to_y(value):
    return move(value, lambda r, s: (r ^ 1, s))


def to_z(value):
    return move(value, lambda r, s: (r ^ 2, s))


PANEL = 512
LANES = 128
PER_STEP = 2
EST = 5
PACK_EST = 0.1


class Piece(NamedTuple):
    parts: tuple
    row: int
    rows: int
    target: int
    block: int
    to_row: int
    to_col: int


class Bundle(NamedTuple):
    first: tuple
    second: tuple
    shapes: tuple
    joined: bool = True


def quarter_rows(pieces):
    return sum(p.rows for p in pieces) // 4


def make_bundles(width, kv_width, ff, chunks, shards):
    rows, drop_rows = width // shards, ff // shards // chunks
    panels = width // PANEL
    first = tuple(Piece(((0, c, PANEL),), 0, rows, 0, rows, 0, c) for c in range(0, width, PANEL))
    second = []
    for c in range(0, 2 * kv_width, PANEL):
        parts, at = [], c
        while at < c + PANEL:
            source = 1 if at < kv_width else 2
            base = (source - 1) * kv_width
            stop = min(c + PANEL, base + kv_width)
            parts.append((source, at - base, stop - at))
            at = stop
        second.append(Piece(tuple(parts), 0, rows, 0, rows, 0, width + c))
    found = [Bundle(first, tuple(second), ((width, width + 2 * kv_width),))]

    def halves(source, row, height, target, block):
        return [
            tuple(
                Piece(((source, i * PANEL, PANEL),), row + h * height // 2, height // 2, target, block,
                      h * height // 2, i * PANEL)
                for i in range(panels)
            )
            for h in range(2)
        ]

    top, bottom = halves(3, 0, rows, 0, rows)
    found.append(Bundle(top, bottom, ((width, width),)))
    part = ff // shards // chunks
    for u in range(chunks):
        sides = []
        for j in range(2):
            side = []
            for c in range(0, shards * part, PANEL):
                parts = tuple(
                    (4 + j, t * (ff // shards) + u * part, part)
                    for t in range(c // part, (c + PANEL) // part)
                )
                side.append(Piece(parts, 0, rows, 0, rows, 0, 2 * c + j * PANEL))
            sides.append(tuple(side))
        top, bottom = halves(6, u * drop_rows, drop_rows, 1, drop_rows)
        cols = shards * part
        found.append(
            Bundle(sides[0] + top, sides[1] + bottom, ((width, 2 * cols), (cols, width)), False)
        )
    return found


def work(microseconds):
    return pl.CostEstimate(flops=int(microseconds * 1.1e9), bytes_accessed=2**20, transcendentals=0)


def pack(place, jobs, operands, out_shapes, name):
    n_in, n_out = len(operands), len(out_shapes)

    def kernel(place_ref, *refs):
        ins, refs = refs[:n_in], refs[n_in:]
        outs, held, sems = refs[:n_out], refs[n_out : 2 * n_out], refs[-1]
        arriving, leaving = [], []
        for i, (src, o, *spot) in enumerate(jobs(place_ref, ins)):
            here = held[o].at[tuple(spot)]
            arriving.append(pltpu.make_async_copy(src, here, sems.at[0, i]))
            leaving.append(pltpu.make_async_copy(here, outs[o].at[tuple(spot)], sems.at[1, i]))
        for c in arriving:
            c.start()
        for c, d in zip(arriving, leaving):
            c.wait()
            d.start()
        for d in leaving:
            d.wait()

    class Fake:
        def __init__(self):
            self.at = self

        def __getitem__(self, _):
            return self

    count = len(jobs(None, [Fake()] * n_in))
    hbm = pl.BlockSpec(memory_space=pltpu.HBM)
    return pl.pallas_call(
        kernel,
        out_shape=[jax.ShapeDtypeStruct(sh, BF16) for sh in out_shapes],
        grid_spec=pltpu.PrefetchScalarGridSpec(
            num_scalar_prefetch=1,
            grid=(1,),
            in_specs=[hbm] * n_in,
            out_specs=[hbm] * n_out,
            scratch_shapes=[pltpu.VMEM(sh, BF16) for sh in out_shapes]
            + [pltpu.SemaphoreType.DMA((2, count))],
        ),
        compiler_params=pltpu.CompilerParams(vmem_limit_bytes=64 * 2**20),
        cost_estimate=work(PACK_EST),
        name=name,
    )(place, *operands)


def gate(value, ties):
    return pl.pallas_call(
        lambda *refs: None,
        out_shape=jax.ShapeDtypeStruct(value.shape, value.dtype),
        in_specs=[pl.BlockSpec(memory_space=pltpu.HBM)] * (1 + len(ties)),
        out_specs=pl.BlockSpec(memory_space=pltpu.HBM),
        input_output_aliases={0: 0},
        compiler_params=pltpu.CompilerParams(vmem_limit_bytes=64 * 2**20),
        name="gate",
    )(value, *ties)


def join(*parts, ties=()):
    cols = parts[0].shape[1]

    def kernel(*refs):
        at = 0
        for ref in refs[: len(parts)]:
            refs[-1][at : at + ref.shape[0]] = ref[...]
            at += ref.shape[0]

    return pl.pallas_call(
        kernel,
        out_shape=jax.ShapeDtypeStruct((sum(p.shape[0] for p in parts), cols), parts[0].dtype),
        in_specs=[pl.BlockSpec(memory_space=pltpu.VMEM)] * len(parts)
        + [pl.BlockSpec(memory_space=pltpu.HBM)] * len(ties),
        compiler_params=pltpu.CompilerParams(vmem_limit_bytes=64 * 2**20),
        cost_estimate=work(1),
        name="join",
    )(*parts, *ties)


def quarter_start(place_ref, flip, rows):
    if place_ref is None:
        return 0
    return pl.multiple_of((place_ref[1] ^ flip) * rows, 16)


class Relay:
    def __init__(self, place, weights, bundles):
        self.place, self.weights, self.bundles = place, weights, bundles
        self.direct, self.once, self.twice = {}, {}, {}
        self.here, self.there = {}, {}
        self.tick = 0

    def step(self, extra=(), ties=(), across=True):
        t, bundles = self.tick, self.bundles
        self.tick += 1
        operands, shapes, kinds, sent = [], [], [], []

        def operand(array):
            for i, o in enumerate(operands):
                if o is array:
                    return i
            operands.append(array)
            return len(operands) - 1

        plans = []

        def out(kind, rows, cols=PANEL):
            shapes.append((rows, cols))
            kinds.append(kind)
            return len(shapes) - 1

        if t < len(bundles):
            b = bundles[t]
            base = quarter_rows(b.first + b.second)
            o = out("x", base + sum(n * a.shape[2] // PANEL for a, _, n in extra))
            for array, start, count in extra:
                i = operand(array)
                sent.append((base, count))

                def plan_t(pr, ins, o=o, i=i, start=start, count=count, base=base, cols=array.shape[2]):
                    which = 0 if pr is None else 1 - pr[0] // 2
                    return [
                        (ins[i].at[which, pl.ds(start, count), pl.ds(c, PANEL)], o,
                         pl.ds(base + c // PANEL * count, count), slice(None))
                        for c in range(0, cols, PANEL)
                    ]

                plans.append(plan_t)
                base += count * array.shape[2] // PANEL
            used = [(operand(self.weights[q[0]]), q, p) for p in b.first + b.second for q in p.parts]

            def plan_x(pr, ins, o=o, used=used):
                copies, at, col = [], 0, 0
                for i, (_, c, n), p in used:
                    q = p.rows // 4
                    rows = pl.ds(pl.multiple_of(p.row + quarter_start(pr, 0, q), 16), q)
                    copies.append((ins[i].at[rows, pl.ds(c, n)],
                                   o, pl.ds(at, q), pl.ds(col, n)))
                    col += n
                    if col == PANEL:
                        at, col = at + q, 0
                return copies

            plans.append(plan_x)
        y_parts, z_parts = [], []
        b1, b2, b3 = t - 1, t - 2, t - 3
        if 0 <= b1 < len(bundles):
            qa, qb = quarter_rows(bundles[b1].first), quarter_rows(bundles[b1].second)
            y_parts.append(("first", b1, [(self.direct[b1], 0, qa)]))
            z_parts.append(("first", b1, [(self.direct[b1], qa, qb)]))
        if 0 <= b2 < len(bundles):
            qa, qb = quarter_rows(bundles[b2].first), quarter_rows(bundles[b2].second)
            (ya, yo), (za, zo) = self.once[b2]
            y_parts.append(("second", b2, [(self.direct[b2], qa, qb), (za, zo, qb)]))
            z_parts.append(("second", b2, [(self.direct[b2], 0, qa), (ya, yo, qa)]))
        for kind, parts in (("y", y_parts), ("z", z_parts)):
            if not parts:
                continue
            total = sum(n for _, _, l in parts for _, _, n in l)
            o = out(kind, total)
            flat = [(operand(a), r, n) for _, _, l in parts for a, r, n in l]

            def plan_n(pr, ins, o=o, flat=flat):
                copies, at = [], 0
                for i, r, n in flat:
                    copies.append((ins[i].at[pl.ds(r, n)], o, pl.ds(at, n), slice(None)))
                    at += n
                return copies

            plans.append(plan_n)
        for tie in ties:
            operand(tie)

        def jobs(pr, ins):
            return [c for plan in plans for c in plan(pr, ins)]

        bufs = pack(self.place, jobs, operands, shapes, f"pack_{t}") if shapes else []
        for kind, buf in zip(kinds, bufs):
            if kind == "x":
                self.direct[t] = to_chip(buf)
            else:
                got = (to_y if kind == "y" else to_z)(buf)
                at = 0
                for stage, bi, l in y_parts if kind == "y" else z_parts:
                    store = self.once if stage == "first" else self.twice
                    pair = store.setdefault(bi, [None, None])
                    pair[0 if kind == "y" else 1] = (got, at)
                    at += sum(n for _, _, n in l)
        if 0 <= b3 < len(bundles) and across:
            self.across(b3, bufs[:1] if bufs else ties)
        return [(self.direct[t], *spot) for spot in sent], bufs

    def across(self, b3, ties):
        b = self.bundles[b3]
        operands, shapes = [], []

        def operand(array):
            for i, o in enumerate(operands):
                if o is array:
                    return i
            operands.append(array)
            return len(operands) - 1

        plans = []

        def out(kind, rows, cols=PANEL):
            shapes.append((rows, cols))
            return len(shapes) - 1

        total = 4 * quarter_rows(b.first + b.second)
        o = out("c", (2 if b.joined else 1) * total)
        used = [
            (operand(self.weights[q[0]]), q, p)
            for p in (b.first + b.second if b.joined else ()) for q in p.parts
        ]
        qa = quarter_rows(b.first)
        qb = quarter_rows(b.second)
        (ya, yo), (za, zo) = self.once[b3]
        (ys, yso), (zs, zso) = self.twice[b3]
        d = operand(self.direct[b3])
        sides = [
            (b.first, [(0, d, 0), (1, operand(ya), yo), (2, operand(zs), zso), (3, operand(zs), zso + qa)]),
            (b.second, [(0, d, qa), (2, operand(za), zo), (1, operand(ys), yso), (3, operand(ys), yso + qb)]),
        ]

        def plan_c(pr, ins, o=o, sides=sides, used=used, total=total):
            copies, base, at, col = [], total if b.joined else 0, 0, 0
            for i, (_, c, n), p in used:
                copies.append((ins[i].at[pl.ds(p.row, p.rows), pl.ds(c, n)],
                               o, pl.ds(at, p.rows), pl.ds(col, n)))
                col += n
                if col == PANEL:
                    at, col = at + p.rows, 0
            for pieces, quarters in sides:
                at = 0
                for p in pieces:
                    q = p.rows // 4
                    for flip, i, r in quarters:
                        to = pl.multiple_of(base + quarter_start(pr, flip, q), 16)
                        copies.append((ins[i].at[pl.ds(r + at, q)], o, pl.ds(to, q), slice(None)))
                    at += q
                    base += p.rows
            return copies

        plans.append(plan_c)

        for tie in ties:
            operand(tie)
        jobs = lambda pr, ins: plans[0](pr, ins)
        (buf,) = pack(self.place, jobs, operands, shapes, f"across_{b3}")
        self.here[b3], self.there[b3] = buf, to_core(buf)


def land_copies(place_ref, bundle, own, near, here, there, targets):
    copies = []
    shard = 0 if place_ref is None else place_ref[0]
    pieces = bundle.first + bundle.second
    total = sum(p.rows for p in pieces)
    skip = total if bundle.joined else 0
    for slot, (ref, base) in enumerate(((None, 0), (there, 0), (here, skip), (there, skip))):
        for p in pieces:
            to = (shard ^ slot) * p.block + p.to_row
            to = pl.ds(pl.multiple_of(to, 16), p.rows)
            dst = targets[p.target]
            key = (p.target, p.to_col)
            if slot == 0 or slot == 1 and not bundle.joined:
                col = p.to_col
                for source, c, n in p.parts:
                    copies.append(((near if slot else own)[source].at[pl.ds(p.row, p.rows), pl.ds(c, n)],
                                   dst.at[to, pl.ds(col, n)], key))
                    col += n
            else:
                copies.append((ref.at[pl.ds(base, p.rows)], dst.at[to, pl.ds(p.to_col, PANEL)], key))
            base += p.rows
    return copies


def sources_of(bundle):
    return sorted({q[0] for p in bundle.first + bundle.second for q in p.parts})


def rotary_tables(positions, head_dim):
    half_dim = head_dim // 2
    freq_index = jnp.arange(half_dim).astype(F32)
    frequency = jnp.exp(freq_index * (-2.0 * math.log(ROPE_BASE) / head_dim))
    angles = positions[:, None] * frequency[None, :]
    return jnp.cos(angles), jnp.sin(angles)


def dot(left, right):
    return jnp.dot(left, right, preferred_element_type=F32)


def dot_nt(left, right):
    return lax.dot_general(left, right, (((1,), (1,)), ((), ())), preferred_element_type=F32)


def dot_tn(left, right):
    return lax.dot_general(left, right, (((0,), (0,)), ((), ())), preferred_element_type=F32)


LOG2E = 1.4426950408889634


def last_visible(place_ref, low, lanes, block):
    shard, prefix = place_ref[0], place_ref[2]
    at = shard % 2 if low else 2 + shard % 2
    position = at * block + lax.broadcasted_iota(jnp.int32, (1, lanes), 1) % block
    return jnp.maximum(position + 1, prefix)


def query_start(place_ref, low, block):
    chip = place_ref[0] // 2
    return pl.multiple_of((chip if low else 1 - chip) * block, block)


def natural_rows(place_ref, own, near, into, block, n):
    shard = place_ref[0]
    for slot, value in (
        (0, own[n, :block]),
        (2, own[n, block:]),
        (1, near[n, :block]),
        (3, near[n, block:]),
    ):
        into[n, pl.ds(pl.multiple_of((shard ^ slot) * block, block), block)] = value


def hide(scores, limit, first_key):
    keys = first_key + lax.broadcasted_iota(jnp.int32, scores.shape, 0)
    return jnp.where(keys < limit, scores, MASKED_SCORE)


def masked_by_part(low, scores, limit, block):
    if low:
        return hide(scores, limit, 0)
    half = 2 * block
    return jnp.concatenate([scores[:half], hide(scores[half:], limit, half)], axis=0)


def attend_kernel(place, q, k_own, k_near, v_own, v_near, out, lse, keys, values, *, scale):
    block = q.shape[1] // 2
    count_kv = k_own.shape[0]
    group = q.shape[0] // count_kv
    for n in range(count_kv):
        natural_rows(place, k_own, k_near, keys, block, n)
        natural_rows(place, v_own, v_near, values, block, n)
    for n in range(count_kv):
        values_t = values[n].T
        for part, low in enumerate((True, False)):
            count = (2 if low else 4) * block
            rows = pl.ds(query_start(place, low, block), block)
            query = jnp.concatenate([q[n * group + j, rows] for j in range(group)], axis=0)
            limit = last_visible(place, low, group * block, block)
            scores = masked_by_part(low, dot_nt(keys[n, :count], query), limit, block)
            top = jnp.max(scores, axis=0, keepdims=True)
            base = scale * LOG2E
            expo = jnp.exp2(scores * base - top * base)
            total = jnp.sum(expo, axis=0, keepdims=True)
            lse[n, part] = (top * base + jnp.log2(total))[0]
            result = dot(values_t[:, :count], expo.astype(BF16)) / total
            result = result.T.astype(BF16)
            for j in range(group):
                out[n * group + j, rows] = result[j * block : (j + 1) * block]


def attend(place, queries, kv_own, kv_near):
    heads, rows, dim = queries.shape
    kv_heads = kv_own.shape[0] // 2
    group = heads // kv_heads
    per = PER_STEP
    q_spec = pl.BlockSpec((per * group, rows, dim), lambda g, p: (g, 0, 0))
    kv_spec = pl.BlockSpec((per, rows, dim), lambda g, p: (g, 0, 0))
    v_spec = pl.BlockSpec((per, rows, dim), lambda g, p: (g + kv_heads // per, 0, 0))
    lse_shape = (kv_heads, 2, group * rows // 2)
    return pl.pallas_call(
        functools.partial(attend_kernel, scale=HEAD_DIM ** (-0.5)),
        out_shape=[
            jax.ShapeDtypeStruct(queries.shape, BF16),
            jax.ShapeDtypeStruct(lse_shape, F32),
        ],
        grid_spec=pltpu.PrefetchScalarGridSpec(
            num_scalar_prefetch=1,
            grid=(kv_heads // per,),
            in_specs=[q_spec, kv_spec, kv_spec, v_spec, v_spec],
            out_specs=[q_spec, pl.BlockSpec((per, *lse_shape[1:]), lambda g, p: (g, 0, 0))],
            scratch_shapes=[pltpu.VMEM((per, 2 * rows, dim), BF16)] * 2,
        ),
        compiler_params=pltpu.CompilerParams(vmem_limit_bytes=64 * 2**20),
        cost_estimate=work(EST),
        name="attend",
    )(place, queries, kv_own, kv_near, kv_own, kv_near)


def attend_back_kernel(
    place, q, k_own, k_near, v_own, v_near, grad, lse, cos_t, sin_t, *rest, scale
):
    dq, own_out, send_out, keys, values, dk, dv = rest[-7:]
    block = q.shape[1] // 2
    count_kv = k_own.shape[0]
    group = q.shape[0] // count_kv
    half = HEAD_DIM // 2
    for n in range(count_kv):
        natural_rows(place, k_own, k_near, keys, block, n)
        natural_rows(place, v_own, v_near, values, block, n)
    for n in range(count_kv):
        keys_t = keys[n].T
        for part, low in ((1, False), (0, True)):
            count = (2 if low else 4) * block
            start = query_start(place, low, block)
            rows = pl.ds(start, block)
            query = jnp.concatenate([q[n * group + j, rows] for j in range(group)], axis=0)
            out_grad = jnp.concatenate([grad[n * group + j, rows] for j in range(group)], axis=0)
            limit = last_visible(place, low, group * block, block)
            scores = masked_by_part(low, dot_nt(keys[n, :count], query), limit, block)
            probs = jnp.exp2(scores * (scale * LOG2E) - lse[n, part][None])
            probs_grad = dot_nt(values[n, :count], out_grad)
            mean = jnp.sum(probs * probs_grad, axis=0, keepdims=True)
            score_grad = (probs * (probs_grad - mean)).astype(BF16)
            v_part = dot(probs.astype(BF16), out_grad)
            k_part = dot(score_grad, query) * scale
            if low:
                dk[n, :count] += k_part
                dv[n, :count] += v_part
            else:
                dk[n] = k_part
                dv[n] = v_part
            turned = dot(keys_t[:, :count], score_grad) * scale
            cos = jnp.concatenate([cos_t[:, rows]] * group, axis=1)
            sin = jnp.concatenate([sin_t[:, rows]] * group, axis=1)
            u, w = turned[:half], turned[half : 2 * half]
            pad = jnp.zeros((q.shape[2] - 2 * half, u.shape[1]), F32)
            turned = jnp.concatenate([u * cos + w * sin, w * cos - u * sin, pad], axis=0)
            turned = turned.T.astype(BF16)
            for j in range(group):
                dq[n * group + j, rows] = turned[j * block : (j + 1) * block]
        shard = place[0]
        for slot, at, own in ((0, 0, True), (2, 1, True), (1, 0, False), (3, 1, False)):
            rows = pl.ds(pl.multiple_of((shard ^ slot) * block, block), block)
            to = slice(at * block, (at + 1) * block)
            out = own_out if own else send_out
            out[0, n, to] = dk[n, rows].astype(out.dtype)
            out[1, n, to] = dv[n, rows].astype(out.dtype)


def attend_back(place, queries, kv_own, kv_near, grad, lse, cos_t, sin_t, part, parts, ties):
    heads, rows, dim = queries.shape
    kv_heads = kv_own.shape[0] // 2
    group = heads // kv_heads
    count = kv_heads // parts
    per = PER_STEP
    base = part * count // per
    q_spec = pl.BlockSpec((per * group, rows, dim), lambda g, p: (g + base, 0, 0))
    kv_spec = pl.BlockSpec((per, rows, dim), lambda g, p: (g + base, 0, 0))
    v_spec = pl.BlockSpec((per, rows, dim), lambda g, p: (g + base + kv_heads // per, 0, 0))
    whole = pl.BlockSpec(cos_t.shape, lambda g, p: (0, 0))
    return pl.pallas_call(
        functools.partial(attend_back_kernel, scale=HEAD_DIM ** (-0.5)),
        out_shape=[
            jax.ShapeDtypeStruct((heads // parts, rows, dim), BF16),
            jax.ShapeDtypeStruct((2, count, rows, dim), F32),
            jax.ShapeDtypeStruct((2, count, rows, dim), BF16),
        ],
        grid_spec=pltpu.PrefetchScalarGridSpec(
            num_scalar_prefetch=1,
            grid=(count // per,),
            in_specs=[q_spec, kv_spec, kv_spec, v_spec, v_spec]
            + [q_spec, pl.BlockSpec((per, *lse.shape[1:]), lambda g, p: (g + base, 0, 0)), whole, whole]
            + [pl.BlockSpec(memory_space=pltpu.HBM)] * len(ties),
            out_specs=[pl.BlockSpec((per * group, rows, dim), lambda g, p: (g, 0, 0))] + [pl.BlockSpec((2, per, rows, dim), lambda g, p: (0, g, 0, 0))] * 2,
            scratch_shapes=[pltpu.VMEM((per, 2 * rows, dim), BF16)] * 2
            + [pltpu.VMEM((per, 2 * rows, dim), F32)] * 2,
        ),
        compiler_params=pltpu.CompilerParams(vmem_limit_bytes=64 * 2**20),
        cost_estimate=work(1),
        name=f"attend_back_{part}",
    )(place, queries, kv_own, kv_near, kv_own, kv_near, grad, lse, cos_t, sin_t, *ties)


def row_copies(sources, refs, into, sems):
    copies, at = [], into.shape[0] // 2
    for ref, (_, base, count) in zip(refs, sources):
        for c in range(into.shape[1] // PANEL):
            copies.append(
                pltpu.make_async_copy(
                    ref.at[pl.ds(base + c * count, count)],
                    into.at[pl.ds(at, count), pl.ds(c * PANEL, PANEL)],
                    sems.at[len(copies)],
                )
            )
        at += count
    return copies


class Landing:
    def __init__(self, place, bundle, refs, targets, sems):
        used = sources_of(bundle)
        n = len(used)
        own = dict(zip(used, refs[:n]))
        near = {} if bundle.joined else dict(zip(used, refs[n : 2 * n]))
        listed = land_copies(place, bundle, own, near, refs[-2], refs[-1], targets)
        self.copies = [
            (key, pltpu.make_async_copy(src, dst, sems.at[i])) for i, (src, dst, key) in enumerate(listed)
        ]
        self.copies.sort(key=lambda c: c[0])
        for _, c in self.copies:
            c.start()

    def wait(self, wanted=None):
        left = []
        for key, c in self.copies:
            if wanted is None or wanted(key):
                c.wait()
            else:
                left.append((key, c))
        self.copies = left


def landing_operands(bundle, weights, near, here, there):
    used = sources_of(bundle)
    return [weights[i] for i in used] + ([] if bundle.joined else [near[i] for i in used]) + [here, there]


def landing_count(bundle):
    return sum((1 if bundle.joined else 2) * len(p.parts) + 3 for p in bundle.first + bundle.second)


NO_BUNDLE = Bundle((), (), ())


def kernel_call(body, place, bundle, landing, operands, outs, scratch, name, time=0.5, ties=()):
    operands = [*operands, *((t, HB) for t in ties)]
    n_land, n_in, n_out, n_w = len(landing), len(operands), len(outs), len(bundle.shapes)

    def kernel(place_ref, *refs):
        land, refs = refs[:n_land], refs[n_land:]
        ins, refs = refs[: n_in - len(ties)], refs[n_in:]
        out, refs = refs[:n_out], refs[n_out:]
        body(place_ref, land, ins, out, refs[:n_w], refs[n_w], refs[n_w + 1 :])

    def spec(where):
        return where if isinstance(where, pl.BlockSpec) else pl.BlockSpec(memory_space=where)

    return pl.pallas_call(
        kernel,
        out_shape=[o for o, _ in outs],
        grid_spec=pltpu.PrefetchScalarGridSpec(
            num_scalar_prefetch=1,
            grid=(1,),
            in_specs=[spec(pltpu.HBM)] * n_land + [spec(w) for _, w in operands],
            out_specs=[spec(w) for _, w in outs],
            scratch_shapes=[pltpu.VMEM(sh, BF16) for sh in bundle.shapes]
            + [pltpu.SemaphoreType.DMA((max(landing_count(bundle), 1),))]
            + list(scratch),
        ),
        compiler_params=pltpu.CompilerParams(vmem_limit_bytes=64 * 2**20),
        cost_estimate=work(time),
        name=name,
    )(place, *landing, *[a for a, _ in operands])


VM = pltpu.VMEM
HB = pltpu.HBM


def like(shape, dtype):
    return jax.ShapeDtypeStruct(shape, dtype)


def turn(value, cos_full, sin_signed, half):
    swapped = jnp.concatenate([value[:, half:], value[:, :half]], axis=1)
    return value * cos_full + swapped * sin_signed


def padded(value):
    return jnp.concatenate([value, jnp.zeros((value.shape[0], LANES - HEAD_DIM), value.dtype)], axis=1)


def one_of_pair(block, width):
    return pl.BlockSpec((None, block, width), lambda i, p: (p[0] // 2, 0, 0))


def qkv_forward(place, bundle, landing, tokens, tokens_back, gain, inner, outer, cos, sin, ties):
    _, block, width = tokens.shape
    rows = 2 * block
    total = bundle.shapes[0][1]
    kv = (total - width) // 2
    wide = 8 * HEAD_DIM
    half = HEAD_DIM // 2

    def body(pr, land_refs, ins, outs, weights, sems, scratch):
        kept, *backs, gain_ref, inner_ref, outer_ref, cos_ref, sin_ref = ins
        q, kv_ref, hidden_ref, normed_ref, x_ref = outs
        (w,) = weights
        arriving = row_copies(tokens_back, backs, x_ref, scratch[0])
        for c in arriving:
            c.start()
        landing = Landing(pr, bundle, land_refs, weights, sems)
        x_ref[:block] = kept[...]
        for c in arriving:
            c.wait()
        x = x_ref[...].astype(F32)
        scale = lax.rsqrt(jnp.mean(x * x, axis=-1, keepdims=True) + EPSILON)
        normed_ref[...] = (x * scale * gain_ref[...].astype(F32)).astype(BF16)
        hidden_ref[...] = dot_nt(normed_ref[...], inner_ref[...]).astype(BF16)

        def columns(at):
            cols = pl.ds(at, wide)
            return dot(normed_ref[...], w[:, cols]) + dot(hidden_ref[...], outer_ref[:, cols])

        landing.wait(lambda key: key[1] < width)
        for i in range(width // wide):
            acc = columns(i * wide)
            for h in range(8):
                one = acc[:, h * HEAD_DIM : (h + 1) * HEAD_DIM]
                q[8 * i + h] = padded(turn(one, cos_ref[...], sin_ref[...], half)).astype(BF16)
        landing.wait()
        acc = columns(width)
        for h in range(8):
            one = acc[:, h * HEAD_DIM : (h + 1) * HEAD_DIM]
            kv_ref[h] = padded(turn(one, cos_ref[...], sin_ref[...], half)).astype(BF16)
        acc = columns(width + kv)
        for h in range(8):
            kv_ref[8 + h] = padded(acc[:, h * HEAD_DIM : (h + 1) * HEAD_DIM]).astype(BF16)

    heads = width // HEAD_DIM
    return kernel_call(
        body, place, bundle, landing,
        [(tokens, one_of_pair(block, width)), *((t[0], HB) for t in tokens_back), (gain, VM), (inner, VM), (outer, VM), (cos, VM), (sin, VM)],
        [
            (like((heads, rows, LANES), BF16), VM),
            (like((2 * kv // HEAD_DIM, rows, LANES), BF16), VM),
            (like((rows, inner.shape[0]), BF16), VM),
            (like((rows, width), BF16), VM),
            (like((rows, width), BF16), VM),
        ],
        [pltpu.SemaphoreType.DMA((len(tokens_back) * width // PANEL,))], "qkv_forward", time=EST, ties=ties,
    )


def out_forward(place, bundle, landing, heads_out, x, gain, inner, outer, cot, cot_back, inner_gl, drop_b):
    rows, width = x.shape
    heads = heads_out.shape[0]

    def body(pr, land_refs, ins, outs, weights, sems, scratch):
        heads_ref, x_ref, gain_ref, inner_ref, outer_ref, cot_kept, *cot_got, igl, db = ins
        middle, normed, attended, hidden, cot_ref, h_gl, h_d = outs
        arriving = row_copies(cot_back, cot_got, cot_ref, scratch[0])
        for c in arriving:
            c.start()
        landing = Landing(pr, bundle, land_refs, weights, sems)
        for h in range(heads):
            attended[:, h * HEAD_DIM : (h + 1) * HEAD_DIM] = heads_ref[h, :, :HEAD_DIM]
        hidden[...] = dot_nt(attended[...], inner_ref[...]).astype(BF16)
        cot_ref[: rows // 2] = cot_kept[...]
        for c in arriving:
            c.wait()
        h_d[...] = dot_nt(cot_ref[...], db[...]).astype(BF16)
        landing.wait()
        wide = width // 2
        squares = jnp.zeros((rows, 1), F32)
        for i in range(2):
            cols = pl.ds(i * wide, wide)
            branch = dot(attended[...], weights[0][:, cols]) + dot(hidden[...], outer_ref[:, cols])
            value = x_ref[:, cols].astype(F32) + branch
            middle[:, cols] = value
            squares += jnp.sum(value * value, axis=-1, keepdims=True)
        scale = lax.rsqrt(squares / width + EPSILON)
        normed[...] = (middle[...] * scale * gain_ref[...].astype(F32)).astype(BF16)
        h_gl[...] = dot_nt(normed[...], igl[...]).astype(BF16)

    return kernel_call(
        body, place, bundle, landing,
        [(heads_out, VM), (x, VM), (gain, VM), (inner, VM), (outer, VM),
         (cot, one_of_pair(rows // 2, width)), *((c[0], HB) for c in cot_back), (inner_gl, VM), (drop_b, VM)],
        [
            (like((rows, width), F32), VM),
            (like((rows, width), BF16), VM),
            (like((rows, width), BF16), VM),
            (like((rows, RANK), BF16), VM),
            (like((rows, width), BF16), VM),
            (like((rows, 2 * RANK), BF16), VM),
            (like((rows, RANK), BF16), VM),
        ],
        [pltpu.SemaphoreType.DMA((len(cot_back) * width // PANEL,))], "out_forward", time=EST,
    )


def mlp_chunk(place, bundle, landing, normed, cot, hidden_gl, hidden_d, outer_gl, drop_a, chunk, sums, name):
    rows, width = normed.shape
    units = bundle.shapes[1][0]
    steps = units // PANEL
    first = sums is None
    part = units // 4

    def body(pr, land_refs, ins, outs, weights, sems, scratch):
        normed_ref, cot_ref, hgl_ref, hd_ref, ogl, da = ins[:6]
        drop_sum, e_sum, thin, keep, send = outs
        (packed,) = scratch
        w_gl, w_d = weights
        landing = Landing(pr, bundle, land_refs, weights, sems)
        h_d = hd_ref[...]
        h_g, h_l = hgl_ref[:, :RANK], hgl_ref[:, RANK:]
        g_t, l_t, d_t = h_g.T, h_l.T, h_d.T
        for i in range(steps):
            landing.wait(lambda key: key[0] == 1 or key[1] < 2 * (i + 1) * PANEL)
            cols = slice(i * PANEL, (i + 1) * PANEL)
            both = pl.ds(2 * i * PANEL, 2 * PANEL)
            acts = dot(normed_ref[...], w_gl[:, both])
            gate = acts[:, :PANEL] + dot(h_g, ogl[:RANK, cols])
            lift = acts[:, PANEL:] + dot(h_l, ogl[RANK:, cols])
            a_grad = dot_nt(cot_ref[...], w_d[cols]) + dot(h_d, da[:, cols])
            sig = 1.0 / (1.0 + jnp.exp(-gate))
            silu = gate * sig
            active = (silu * lift).astype(BF16)
            gate_grad = (a_grad * lift * sig * (1.0 + gate * (1.0 - sig))).astype(BF16)
            lift_grad = (a_grad * silu).astype(BF16)
            grads = jnp.concatenate([gate_grad, lift_grad], axis=1)
            down = dot(active, w_d[cols])
            back = dot_nt(grads, w_gl[:, both])
            t0 = dot_nt(active, da[:, cols])
            t1 = dot_nt(gate_grad, ogl[:RANK, cols])
            t2 = dot_nt(lift_grad, ogl[RANK:, cols])
            if i == 0 and first:
                drop_sum[...] = down
                e_sum[...] = back
                thin[0], thin[1], thin[2] = t0, t1, t2
            elif i == 0:
                drop_sum[...] = ins[6][...] + down
                e_sum[...] = ins[7][...] + back
                thin[0], thin[1], thin[2] = ins[8][0] + t0, ins[8][1] + t1, ins[8][2] + t2
            else:
                drop_sum[...] += down
                e_sum[...] += back
                thin[0] += t0
                thin[1] += t1
                thin[2] += t2
            per = PANEL // part
            for j, g in enumerate((dot(g_t, gate_grad), dot(l_t, lift_grad), dot(d_t, active))):
                for o in range(per):
                    packed[i * per + o, :, j * part : (j + 1) * part] = g[:, o * part : (o + 1) * part]
        split_by_core(pr, packed, keep, send)

    at_chunk = lambda i, p: (chunk, 0, 0)
    operands = [
        (normed, VM), (cot, VM), (hidden_gl, VM), (hidden_d, VM),
        (outer_gl, pl.BlockSpec((None, *outer_gl.shape[1:]), at_chunk)),
        (drop_a, pl.BlockSpec((None, *drop_a.shape[1:]), at_chunk)),
    ]
    if not first:
        operands += [(s, VM) for s in sums]
    return kernel_call(
        body, place, bundle, landing, operands,
        [
            (like((rows, width), F32), VM),
            (like((rows, width), F32), VM),
            (like((3, rows, RANK), F32), VM),
            (like((2, RANK, 3 * part), F32), VM),
            (like((2, RANK, 3 * part), BF16), VM),
        ],
        [pltpu.VMEM((4, RANK, 3 * part), F32)], name, time=EST,
    )


def split_by_core(place_ref, whole, keep, send):
    core = place_ref[0] % 2
    for j in range(2):
        keep[j] = whole[core + 2 * j]
        send[j] = whole[1 - core + 2 * j].astype(BF16)


def out_backward(place, bundle, landing, sums, middle, cot, gain, normed, attended, hidden, factors, ties):
    rows, width = middle.shape
    heads = width // HEAD_DIM

    def body(pr, land_refs, ins, outs, weights, sems, scratch):
        drop_sum, e_sum, thin, middle_ref, cot_ref, gain_ref, normed_ref, att, hid, drop_b, igl, o_a, o_b = ins
        mixed_kept, mixed_back, mid_grad, out_heads, keep, send = outs
        (w,) = weights
        branch, whole = scratch
        landing = Landing(pr, bundle, land_refs, weights, sems)
        d_hid = thin[0].astype(BF16)
        gl_grad = jnp.concatenate([thin[1].astype(BF16), thin[2].astype(BF16)], axis=1)
        e_in = (e_sum[...] + dot(gl_grad, igl[...])) * gain_ref[...].astype(F32)
        mid = middle_ref[...]
        scale = lax.rsqrt(jnp.mean(mid * mid, axis=-1, keepdims=True) + EPSILON)
        n = mid * scale
        mean = jnp.mean(e_in * n, axis=-1, keepdims=True)
        mid_grad[...] = cot_ref[...].astype(F32) + scale * (e_in - n * mean)
        branch[...] = mid_grad[...].astype(BF16)
        hgrad = dot_nt(branch[...], o_b[...]).astype(BF16)
        landing.wait()
        wide = 8 * HEAD_DIM
        for i in range(heads // 8):
            part = slice(i * wide, (i + 1) * wide)
            grad = dot_nt(branch[...], w[part]) + dot(hgrad, o_a[:, part])
            for h in range(8):
                out_heads[8 * i + h] = padded(grad[:, h * HEAD_DIM : (h + 1) * HEAD_DIM]).astype(BF16)
        mixed = (mid + drop_sum[...] + dot(d_hid, drop_b[...])).astype(BF16)
        mixed_kept[...] = mixed[: rows // 2]
        mixed_back[...] = mixed[rows // 2 :]
        gl = dot(gl_grad.T, normed_ref[...])
        own = (
            dot(d_hid.T, cot_ref[...]), gl[:RANK], gl[RANK:],
            dot(hgrad.T, att[...]), dot(hid[...].T, branch[...]),
        )
        for t in range(4):
            for j, g in enumerate(own):
                at = j * quarter
                whole[t, :, at : at + quarter] = g[:, t * quarter : (t + 1) * quarter]
        split_by_core(pr, whole, keep, send)

    quarter = width // 4
    cols = 5 * quarter
    return kernel_call(
        body, place, bundle, landing,
        [(v, VM) for v in (*sums, middle, cot, gain, normed, attended, hidden, *factors)],
        [
            (like((2, rows // 2, width), BF16), one_of_pair(rows // 2, width)),
            (like((rows // 2, width), BF16), VM),
            (like((rows, width), F32), VM),
            (like((heads, rows, LANES), BF16), VM),
            (like((2, RANK, cols), F32), VM),
            (like((2, RANK, cols), BF16), VM),
        ],
        [pltpu.VMEM((rows, width), BF16), pltpu.VMEM((4, RANK, cols), F32)], "out_backward", time=15, ties=ties,
    )


def qkv_gradients(place, parts, cos, sin, normed, hidden, outer, ties):
    rows, width = normed.shape
    total = outer.shape[1]
    kv = (total - width) // 2
    half = HEAD_DIM // 2
    rank3 = outer.shape[0]
    quarter, kv_quarter = width // 4, kv // 4
    cols = 4 * quarter + 2 * kv_quarter
    q_count, kv_count = parts[0][0].shape[0], parts[0][1].shape[1]

    def body(pr, land_refs, ins, outs, weights, sems, scratch):
        *part_refs, cos_ref, sin_ref, nrm, hid, b = ins
        dq_refs, dkv_refs, got_refs = part_refs[0::3], part_refs[1::3], part_refs[2::3]
        g, hgrad_ref, keep, send = outs
        (whole,) = scratch
        for h in range(width // HEAD_DIM):
            ref, i = dq_refs[h // q_count], h % q_count
            g[:, h * HEAD_DIM : (h + 1) * HEAD_DIM] = ref[i, :, :HEAD_DIM]
        for h in range(kv // HEAD_DIM):
            dkv_ref, got_ref, i = dkv_refs[h // kv_count], got_refs[h // kv_count], h % kv_count
            one = (dkv_ref[0, i] + got_ref[0, i].astype(F32))[:, :HEAD_DIM]
            at = width + h * HEAD_DIM
            g[:, at : at + HEAD_DIM] = turn(one, cos_ref[...], -sin_ref[...], half).astype(BF16)
            at += kv
            g[:, at : at + HEAD_DIM] = (dkv_ref[1, i] + got_ref[1, i].astype(F32))[:, :HEAD_DIM].astype(BF16)
        hgrad_ref[...] = dot_nt(g[...], b[...]).astype(BF16)
        g_in = dot(hgrad_ref[...].T, nrm[...])
        g_out = dot(hid[...].T, g[...])
        for t in range(4):
            for i in range(3):
                whole[t, :, i * quarter : (i + 1) * quarter] = g_in[
                    i * RANK : (i + 1) * RANK, t * quarter : (t + 1) * quarter
                ]
            whole[t, :, 3 * quarter : 4 * quarter] = g_out[:RANK, t * quarter : (t + 1) * quarter]
            for i in range(2):
                at, start = 4 * quarter + i * kv_quarter, width + i * kv + t * kv_quarter
                whole[t, :, at : at + kv_quarter] = g_out[
                    (1 + i) * RANK : (2 + i) * RANK, start : start + kv_quarter
                ]
        split_by_core(pr, whole, keep, send)

    return kernel_call(
        body, place, NO_BUNDLE, [],
        [(v, VM) for v in (*[v for p in parts for v in p], cos, sin, normed, hidden, outer)],
        [
            (like((rows, total), BF16), VM),
            (like((rows, rank3), BF16), VM),
            (like((2, RANK, cols), F32), VM),
            (like((2, RANK, cols), BF16), VM),
        ],
        [pltpu.VMEM((4, RANK, cols), F32)], "qkv_gradients", time=1, ties=ties,
    )


def qkv_backward(place, bundle, landing, g, hgrad, x, mid_grad, gain, inner, ties):
    rows, width = x.shape
    total = bundle.shapes[0][1]
    block = rows // 2

    def body(pr, land_refs, ins, outs, weights, sems, scratch):
        g_ref, hg, x_ref, mg, gain_ref, a = ins
        kept, back = outs
        (w,) = weights
        landing = Landing(pr, bundle, land_refs, weights, sems)
        xf = x_ref[...].astype(F32)
        scale = lax.rsqrt(jnp.mean(xf * xf, axis=-1, keepdims=True) + EPSILON)
        n = xf * scale
        thin = dot(hg[...], a[...])
        landing.wait()
        e_in = (dot_nt(g_ref[...], w[...]) + thin) * gain_ref[...].astype(F32)
        mean = jnp.mean(e_in * n, axis=-1, keepdims=True)
        result = mg[...] + scale * (e_in - n * mean)
        kept[...] = result[:block]
        back[...] = result[block:].astype(BF16)

    return kernel_call(
        body, place, bundle, landing,
        [(v, VM) for v in (g, hgrad, x, mid_grad, gain, inner)],
        [(like((2, block, width), F32), one_of_pair(block, width)), (like((block, width), BF16), VM)],
        [], "qkv_backward", time=0.2, ties=ties,
    )


def complete(place, partial, back, ties, name):
    _, block, width = partial.shape

    def kernel(place_ref, partial_ref, back_ref, *rest):
        rest[-1][...] = back_ref[...].astype(partial.dtype)

    return pl.pallas_call(
        kernel,
        out_shape=jax.ShapeDtypeStruct(partial.shape, partial.dtype),
        grid_spec=pltpu.PrefetchScalarGridSpec(
            num_scalar_prefetch=1,
            grid=(1,),
            in_specs=[pl.BlockSpec(memory_space=pltpu.HBM), pl.BlockSpec(memory_space=pltpu.VMEM)]
            + [pl.BlockSpec(memory_space=pltpu.HBM)] * len(ties),
            out_specs=pl.BlockSpec((None, block, width), lambda i, p: (1 - p[0] // 2, 0, 0)),
        ),
        input_output_aliases={1: 0},
        compiler_params=pltpu.CompilerParams(vmem_limit_bytes=64 * 2**20),
        cost_estimate=work(0.5),
        name=name,
    )(place, partial, back, *ties)


def pack_factors(place, inners, outers):
    widths = [a.shape[0] for a in inners] + [b.shape[1] for b in outers]
    n = len(inners)
    mix = outers[0].shape[0]
    narrow = (n + 1, n + 2)

    def body(pr, land_refs, ins, outs, weights, sems, scratch):
        for which, out in enumerate(outs):
            row = lax.broadcasted_iota(jnp.int32, (RANK, mix), 0) + pr[3 + which] * RANK
            choose = (row == lax.broadcasted_iota(jnp.int32, (RANK, mix), 1)).astype(F32).astype(BF16)
            at = 0
            for i, ref in enumerate(ins):
                part = dot_nt(choose, ref[...]) if i < n or i in narrow else dot(choose, ref[...])
                out[:, at : at + widths[i]] = part.astype(BF16)
                at += widths[i]

    shape = (like((RANK, sum(widths)), BF16), VM)
    return kernel_call(
        body, place, NO_BUNDLE, [], [(v.T if i in narrow else v, VM) for i, v in enumerate((*inners, *outers))],
        [shape, shape], [], "pack_factors",
    )


def unpack_factors(place, slots, widths, chunks):
    inner_w, outer_w = widths[:7], widths[7:]
    width, kv = 4 * outer_w[0], 4 * outer_w[1]
    part = outer_w[4] // chunks
    starts = [sum(widths[:i]) for i in range(len(widths))]

    def body(pr, land_refs, ins, outs, weights, sems, scratch):
        iq, oq, io, oo, igl, ogl, da, db = outs
        (nat,) = scratch
        mine, two, got = ins
        nat[pr[0]] = mine[...]
        nat[pr[0] ^ 2] = two[...]
        nat[pr[0] ^ 1] = got[:RANK]
        nat[pr[0] ^ 3] = got[RANK:]
        oq[...] = jnp.zeros(oq.shape, BF16)
        for t in range(4):
            get = lambda i, a=0, n=None: nat[t, :, starts[i] + a : starts[i] + a + (n or widths[i])]
            w = inner_w[0]
            here = slice(t * w, (t + 1) * w)
            for i in range(3):
                iq[i * RANK : (i + 1) * RANK, here] = get(i)
            io[:, here] = get(3)
            igl[:RANK, here] = get(4)
            igl[RANK:, here] = get(5)
            base = 0
            for i in range(3):
                n = outer_w[i]
                oq[i * RANK : (i + 1) * RANK, base + t * n : base + (t + 1) * n] = get(7 + i)
                base += 4 * n
            oo[:, here] = get(10)
            db[:, here] = get(13)
            for u in range(chunks):
                there = slice(t * part, (t + 1) * part)
                ogl[u, :RANK, there] = get(11, u * part, part)
                ogl[u, RANK:, there] = get(12, u * part, part)
                da[u, :, there] = get(6, u * part, part)

    shapes = [
        (3 * RANK, width), (3 * RANK, width + 2 * kv), (RANK, width), (RANK, width), (2 * RANK, width),
        (chunks, 2 * RANK, 4 * part), (chunks, RANK, 4 * part), (RANK, width),
    ]
    return kernel_call(
        body, place, NO_BUNDLE, [], [(v, VM) for v in slots], [(like(sh, BF16), VM) for sh in shapes],
        [pltpu.VMEM((4, *slots[0].shape), BF16)], "unpack_factors",
    )


def fold_cores(place, sums, name, ties=()):
    n = len(sums)
    cols = sum(k.shape[2] for k, _ in sums)

    def body(pr, land_refs, ins, outs, weights, sems, scratch):
        chip = pr[0] // 2
        for out, which in zip(outs, (chip, 1 - chip)):
            at = 0
            for keep_ref, got_ref in zip(ins[:n], ins[n:]):
                w = keep_ref.shape[2]
                out[:, at : at + w] = (keep_ref[which] + got_ref[which].astype(F32)).astype(BF16)
                at += w
            out[:, cols:] = jnp.full((RANK, LANES), pr[3], jnp.int32).astype(F32).astype(BF16)

    shape = (like((RANK, cols + LANES), BF16), VM)
    return kernel_call(
        body, place, NO_BUNDLE, [], [(k, VM) for k, _ in sums] + [(g, VM) for _, g in sums],
        [shape, shape], [], name, ties=ties,
    )


def spread_sums(place, groups, pieces, mix, name, ties=()):
    count = sum(v.shape[0] for v in groups[0])
    tall = [len(g) > 1 for g in groups]

    def body(pr, land_refs, ins, outs, weights, sems, scratch):
        gots, at, held = [], 0, list(scratch)
        for g in groups:
            refs = ins[at : at + len(g)]
            at += len(g)
            if len(g) == 1:
                gots.append(refs[0])
                continue
            got, row = held.pop(0), 0
            for ref in refs:
                got[row : row + ref.shape[0]] = ref[...]
                row += ref.shape[0]
            gots.append(got)
        tag = gots[0][:, -LANES:].astype(F32).astype(jnp.int32) * RANK
        spot = tag + lax.broadcasted_iota(jnp.int32, (count, LANES), 0) % RANK
        choose = (spot == lax.broadcasted_iota(jnp.int32, (count, LANES), 1)).astype(F32).astype(BF16)
        choose_t = choose.T
        for out, (is_inner, runs) in zip(outs, pieces):
            at = 0
            for g, start, n in runs:
                if is_inner:
                    out[at : at + n] = dot_tn(gots[g][:, start : start + n], choose)
                else:
                    out[:, at : at + n] = dot(choose_t, gots[g][:, start : start + n])
                at += n

    outs = []
    for is_inner, runs in pieces:
        n = sum(c for _, _, c in runs)
        outs.append((like((n, mix) if is_inner else (mix, n), F32), VM))
    scratch = [pltpu.VMEM((count, g[0].shape[1]), BF16) for g, t in zip(groups, tall) if t]
    return kernel_call(
        body, place, NO_BUNDLE, [], [(v, VM) for g in groups for v in g], outs, scratch, name, ties=ties
    )


def local(
    tokens,
    cotangent,
    prefix_len,
    adapter_index,
    gain_attn,
    gain_mlp,
    query_weight,
    key_weight,
    value_weight,
    output_weight,
    gate_weight,
    lift_weight,
    drop_weight,
    *factors,
):
    _, block, width = tokens.shape
    rep, shard = lax.axis_index("rep"), lax.axis_index("shard")
    chip = shard // 2
    rows = 2 * block
    kv_width = KV_HEADS * HEAD_DIM
    where = jnp.stack([shard, rep % 4]).astype(jnp.int32)
    place = jnp.concatenate(
        [where, jnp.stack([prefix_len[chip], adapter_index[chip], adapter_index[1 - chip]])]
    )

    weights = (query_weight, key_weight, value_weight, output_weight, gate_weight, lift_weight, drop_weight)
    inners, outers = factors[0::2], factors[1::2]
    widths = [a.shape[0] for a in inners] + [b.shape[1] for b in outers]
    chunks = 4
    ff = gate_weight.shape[1]
    bundles = make_bundles(width, kv_width, ff, chunks, 4)
    positions = jnp.concatenate(
        [shard * block + jnp.arange(block), (shard ^ 2) * block + jnp.arange(block)]
    )
    cos_table, sine_table = rotary_tables(positions.astype(F32), HEAD_DIM)
    cos_full = jnp.concatenate([cos_table, cos_table], axis=1)
    sin_full = jnp.concatenate([-sine_table, sine_table], axis=1)
    gain_one, gain_two = gain_attn[None], gain_mlp[None]
    cos_t, sin_t = cos_table.T, sine_table.T

    relay = Relay(where, weights, bundles)
    half = block // 2
    near = {i: to_core(weights[i]) for i in (4, 5, 6)}
    relay.step()
    mine, others = pack_factors(place, inners, outers)
    slot_two = to_chip(others)
    (tokens_a,), _ = relay.step([(tokens, 0, half)], ties=(near[4], near[5], sin_full, cos_full, cos_t, sin_t, gain_one, gain_two, place))
    (tokens_b,), _ = relay.step([(tokens, half, half)], ties=(slot_two,))
    joined = join(mine, slot_two)
    got = to_core(joined)
    relay.step(ties=(near[6], got))
    inner_qkv, outer_qkv, inner_o, outer_o, inner_gl, outer_gl, drop_a, drop_b = unpack_factors(
        place, (mine, slot_two, got), widths, chunks
    )

    def landing(i):
        return landing_operands(bundles[i], weights, near, relay.here[i], relay.there[i])

    (cot_a,), begun = relay.step([(cotangent, 0, half)], ties=(inner_qkv,), across=False)
    queries, kv_own, hidden_qkv, normed_attn, x = qkv_forward(
        place, bundles[0], landing(0), tokens, (tokens_a, tokens_b), gain_one,
        inner_qkv, outer_qkv, cos_full, sin_full, begun[:1],
    )
    (cot_b,), begun = relay.step([(cotangent, half, half)], ties=(x,))
    kv_own = gate(kv_own, begun[:1])
    relay.across(1, begun[:1])
    kv_near = to_core(kv_own)
    heads_out, lse = attend(place, queries, kv_own, kv_near)
    middle, normed_mlp, attended, output_hidden, cot, hidden_gl, hidden_d = out_forward(
        place, bundles[1], landing(1), heads_out, x, gain_two, inner_o, outer_o,
        cotangent, (cot_a, cot_b), inner_gl, drop_b,
    )
    relay.step(ties=(normed_mlp,))
    sums, kept_sums = None, []
    for u in range(chunks):
        *sums, keep, send = mlp_chunk(
            place, bundles[2 + u], landing(2 + u), normed_mlp, cot, hidden_gl, hidden_d,
            outer_gl, drop_a, u, sums, f"mlp_{u}",
        )
        kept_sums.append((keep, to_core(send)))
        if u < 2:
            relay.step(ties=(keep,))
    early = fold_cores(place, kept_sums[:-1], "fold_early", (keep,))
    mixed_kept, mixed_back, middle_grad, grad_heads, keep, send = out_backward(
        place, bundles[1], landing(1), sums, middle, cot, gain_two, normed_mlp, attended,
        output_hidden, (drop_b, inner_gl, inner_o, outer_o), early[:1],
    )

    mixed_back = to_chip(mixed_back)
    early = join(early[0], to_chip(early[1]))
    folded = fold_cores(place, [kept_sums[-1], (keep, to_core(send))], "fold_late")
    parts, halves = [], 2
    for i in range(halves):
        dq, dkv, dkv_send = attend_back(
            place, queries, kv_own, kv_near, grad_heads, lse, cos_t, sin_t, i, halves,
            folded if i else (early,),
        )
        if i:
            late = to_chip(folded[1])
            dkv_send = gate(dkv_send, (late, mixed_back))
        parts.append((dq, dkv, to_core(dkv_send)))
    early = lax.all_gather(early, "rep", axis=0, tiled=True)
    late_both = join(folded[0], late, ties=parts[0][:1])
    late = lax.all_gather(late_both, "rep", axis=0, tiled=True)
    g, hgrad, keep, send = qkv_gradients(
        place, parts, cos_full, sin_full, normed_attn, hidden_qkv, outer_qkv, (late_both,)
    )
    folded = fold_cores(place, [(keep, to_core(send))], "fold_first")
    other = to_chip(folded[1])
    both = join(folded[0], other)
    input_kept, input_back = qkv_backward(
        place, bundles[0], landing(0), g, hgrad, x, middle_grad, gain_one, inner_qkv, (both, early)
    )
    line = [both]
    for k in range(2, lax.axis_size("rep"), 2):
        line.append(move(both, lambda r, s, k=k: (r ^ k, s)))
    line = join(*line, ties=(input_back,))
    input_back = to_chip(gate(input_back, (line,)))
    first = [line, to_y(line)]
    mixed = complete(place, mixed_kept, mixed_back, (), "complete_mixed")

    mix = ADAPTERS * RANK
    w, kw = width // 4, kv_width // 4
    part = ff // 4 // chunks
    wide = 3 * part
    runs = lambda j: [
        (0, u * wide + j * part, part) if u < chunks - 1 else (1, j * part, part) for u in range(chunks)
    ]
    rest = lambda j: [(1, wide + j * w, w)]
    g_out, l_out, d_in, d_out, g_in, l_in, o_in, o_out = spread_sums(
        place, [[early], [late]],
        [(False, runs(0)), (False, runs(1)), (True, runs(2)), (False, rest(0)), (True, rest(1)),
         (True, rest(2)), (True, rest(3)), (False, rest(4))],
        mix, "spread_late",
    )
    q_in, k_in, v_in, q_out, k_out, v_out = spread_sums(
        place, [first],
        [(True, [(0, 0, w)]), (True, [(0, w, w)]), (True, [(0, 2 * w, w)]), (False, [(0, 3 * w, w)]),
         (True, [(0, 4 * w, kw)]), (True, [(0, 4 * w + kw, kw)])],
        mix, "spread_first", (o_out,),
    )
    k_out, v_out = k_out.T, v_out.T
    input_grad = complete(place, input_kept, input_back, (q_in,), "complete_input_grad")
    return (mixed, input_grad, q_in, q_out, k_in, k_out, v_in, v_out, o_in, o_out,
            g_in, g_out, l_in, l_out, d_in, d_out)


def solution(mesh):
    token_place = P("rep", "shard", None)
    row, col = P("shard", None), P(None, "shard")
    return jax.shard_map(
        local,
        mesh=mesh,
        in_specs=(token_place, token_place, P("rep"), P("rep"), P(), P()) + (row,) * 7 + (row, col) * 7,
        out_specs=(token_place, token_place) + (row, col) * 7,
        check_vma=False,
    )
```

```python
import functools
import math
from typing import NamedTuple

import jax
import jax.numpy as jnp
from jax import lax
from jax.experimental import pallas as pl
from jax.experimental.pallas import tpu as pltpu
from jax.sharding import PartitionSpec as P

HEADS = 16
KV_HEADS = 8
HEAD_DIM = 96
RANK = 16
ADAPTERS = 8
EPSILON = 1e-05
ROPE_BASE = 100000.0
MASKED_SCORE = -1e30
AXES = ("rep", "shard")
F32 = jnp.float32
BF16 = jnp.bfloat16


def move(value, target):
    reps, shards = lax.axis_size("rep"), lax.axis_size("shard")
    pairs = []
    for r in range(reps):
        for s in range(shards):
            r2, s2 = target(r, s)
            pairs.append((r * shards + s, r2 * shards + s2))
    return lax.ppermute(value, AXES, pairs)


def to_core(value):
    return move(value, lambda r, s: (r, s ^ 1))


def to_chip(value):
    return move(value, lambda r, s: (r, s ^ 2))


def to_y(value):
    return move(value, lambda r, s: (r ^ 1, s))


def to_z(value):
    return move(value, lambda r, s: (r ^ 2, s))


PANEL = 512
LANES = 128
PER_STEP = 2
EST = 5
PACK_EST = 0.1


class Piece(NamedTuple):
    parts: tuple
    row: int
    rows: int
    target: int
    block: int
    to_row: int
    to_col: int


class Bundle(NamedTuple):
    first: tuple
    second: tuple
    shapes: tuple
    joined: bool = True


def quarter_rows(pieces):
    return sum(p.rows for p in pieces) // 4


def make_bundles(width, kv_width, ff, chunks, shards):
    rows, drop_rows = width // shards, ff // shards // chunks
    panels = width // PANEL
    first = tuple(Piece(((0, c, PANEL),), 0, rows, 0, rows, 0, c) for c in range(0, width, PANEL))
    second = []
    for c in range(0, 2 * kv_width, PANEL):
        parts, at = [], c
        while at < c + PANEL:
            source = 1 if at < kv_width else 2
            base = (source - 1) * kv_width
            stop = min(c + PANEL, base + kv_width)
            parts.append((source, at - base, stop - at))
            at = stop
        second.append(Piece(tuple(parts), 0, rows, 0, rows, 0, width + c))
    found = [Bundle(first, tuple(second), ((width, width + 2 * kv_width),))]

    def halves(source, row, height, target, block):
        return [
            tuple(
                Piece(((source, i * PANEL, PANEL),), row + h * height // 2, height // 2, target, block,
                      h * height // 2, i * PANEL)
                for i in range(panels)
            )
            for h in range(2)
        ]

    top, bottom = halves(3, 0, rows, 0, rows)
    found.append(Bundle(top, bottom, ((width, width),)))
    part = ff // shards // chunks
    for u in range(chunks):
        sides = []
        for j in range(2):
            side = []
            for c in range(0, shards * part, PANEL):
                parts = tuple(
                    (4 + j, t * (ff // shards) + u * part, part)
                    for t in range(c // part, (c + PANEL) // part)
                )
                side.append(Piece(parts, 0, rows, 0, rows, 0, 2 * c + j * PANEL))
            sides.append(tuple(side))
        top, bottom = halves(6, u * drop_rows, drop_rows, 1, drop_rows)
        cols = shards * part
        found.append(
            Bundle(sides[0] + top, sides[1] + bottom, ((width, 2 * cols), (cols, width)), False)
        )
    return found


def work(microseconds):
    return pl.CostEstimate(flops=int(microseconds * 1.1e9), bytes_accessed=2**20, transcendentals=0)


def pack(place, jobs, operands, out_shapes, name):
    n_in, n_out = len(operands), len(out_shapes)

    def kernel(place_ref, *refs):
        ins, refs = refs[:n_in], refs[n_in:]
        outs, held, sems = refs[:n_out], refs[n_out : 2 * n_out], refs[-1]
        arriving, leaving = [], []
        for i, (src, o, *spot) in enumerate(jobs(place_ref, ins)):
            here = held[o].at[tuple(spot)]
            arriving.append(pltpu.make_async_copy(src, here, sems.at[0, i]))
            leaving.append(pltpu.make_async_copy(here, outs[o].at[tuple(spot)], sems.at[1, i]))
        for c in arriving:
            c.start()
        for c, d in zip(arriving, leaving):
            c.wait()
            d.start()
        for d in leaving:
            d.wait()

    class Fake:
        def __init__(self):
            self.at = self

        def __getitem__(self, _):
            return self

    count = len(jobs(None, [Fake()] * n_in))
    hbm = pl.BlockSpec(memory_space=pltpu.HBM)
    return pl.pallas_call(
        kernel,
        out_shape=[jax.ShapeDtypeStruct(sh, BF16) for sh in out_shapes],
        grid_spec=pltpu.PrefetchScalarGridSpec(
            num_scalar_prefetch=1,
            grid=(1,),
            in_specs=[hbm] * n_in,
            out_specs=[hbm] * n_out,
            scratch_shapes=[pltpu.VMEM(sh, BF16) for sh in out_shapes]
            + [pltpu.SemaphoreType.DMA((2, count))],
        ),
        compiler_params=pltpu.CompilerParams(vmem_limit_bytes=64 * 2**20),
        cost_estimate=work(PACK_EST),
        name=name,
    )(place, *operands)


def gate(value, ties):
    return pl.pallas_call(
        lambda *refs: None,
        out_shape=jax.ShapeDtypeStruct(value.shape, value.dtype),
        in_specs=[pl.BlockSpec(memory_space=pltpu.HBM)] * (1 + len(ties)),
        out_specs=pl.BlockSpec(memory_space=pltpu.HBM),
        input_output_aliases={0: 0},
        compiler_params=pltpu.CompilerParams(vmem_limit_bytes=64 * 2**20),
        name="gate",
    )(value, *ties)


def join(*parts, ties=()):
    cols = parts[0].shape[1]

    def kernel(*refs):
        at = 0
        for ref in refs[: len(parts)]:
            refs[-1][at : at + ref.shape[0]] = ref[...]
            at += ref.shape[0]

    return pl.pallas_call(
        kernel,
        out_shape=jax.ShapeDtypeStruct((sum(p.shape[0] for p in parts), cols), parts[0].dtype),
        in_specs=[pl.BlockSpec(memory_space=pltpu.VMEM)] * len(parts)
        + [pl.BlockSpec(memory_space=pltpu.HBM)] * len(ties),
        compiler_params=pltpu.CompilerParams(vmem_limit_bytes=64 * 2**20),
        cost_estimate=work(1),
        name="join",
    )(*parts, *ties)


def quarter_start(place_ref, flip, rows):
    if place_ref is None:
        return 0
    return pl.multiple_of((place_ref[1] ^ flip) * rows, 16)


class Relay:
    def __init__(self, place, weights, bundles):
        self.place, self.weights, self.bundles = place, weights, bundles
        self.direct, self.once, self.twice = {}, {}, {}
        self.here, self.there = {}, {}
        self.tick = 0

    def step(self, extra=(), ties=(), across=True):
        t, bundles = self.tick, self.bundles
        self.tick += 1
        operands, shapes, kinds, sent = [], [], [], []

        def operand(array):
            for i, o in enumerate(operands):
                if o is array:
                    return i
            operands.append(array)
            return len(operands) - 1

        plans = []

        def out(kind, rows, cols=PANEL):
            shapes.append((rows, cols))
            kinds.append(kind)
            return len(shapes) - 1

        if t < len(bundles):
            b = bundles[t]
            base = quarter_rows(b.first + b.second)
            o = out("x", base + sum(n * a.shape[2] // PANEL for a, _, n in extra))
            for array, start, count in extra:
                i = operand(array)
                sent.append((base, count))

                def plan_t(pr, ins, o=o, i=i, start=start, count=count, base=base, cols=array.shape[2]):
                    which = 0 if pr is None else 1 - pr[0] // 2
                    return [
                        (ins[i].at[which, pl.ds(start, count), pl.ds(c, PANEL)], o,
                         pl.ds(base + c // PANEL * count, count), slice(None))
                        for c in range(0, cols, PANEL)
                    ]

                plans.append(plan_t)
                base += count * array.shape[2] // PANEL
            used = [(operand(self.weights[q[0]]), q, p) for p in b.first + b.second for q in p.parts]

            def plan_x(pr, ins, o=o, used=used):
                copies, at, col = [], 0, 0
                for i, (_, c, n), p in used:
                    q = p.rows // 4
                    rows = pl.ds(pl.multiple_of(p.row + quarter_start(pr, 0, q), 16), q)
                    copies.append((ins[i].at[rows, pl.ds(c, n)],
                                   o, pl.ds(at, q), pl.ds(col, n)))
                    col += n
                    if col == PANEL:
                        at, col = at + q, 0
                return copies

            plans.append(plan_x)
        y_parts, z_parts = [], []
        b1, b2, b3 = t - 1, t - 2, t - 3
        if 0 <= b1 < len(bundles):
            qa, qb = quarter_rows(bundles[b1].first), quarter_rows(bundles[b1].second)
            y_parts.append(("first", b1, [(self.direct[b1], 0, qa)]))
            z_parts.append(("first", b1, [(self.direct[b1], qa, qb)]))
        if 0 <= b2 < len(bundles):
            qa, qb = quarter_rows(bundles[b2].first), quarter_rows(bundles[b2].second)
            (ya, yo), (za, zo) = self.once[b2]
            y_parts.append(("second", b2, [(self.direct[b2], qa, qb), (za, zo, qb)]))
            z_parts.append(("second", b2, [(self.direct[b2], 0, qa), (ya, yo, qa)]))
        for kind, parts in (("y", y_parts), ("z", z_parts)):
            if not parts:
                continue
            total = sum(n for _, _, l in parts for _, _, n in l)
            o = out(kind, total)
            flat = [(operand(a), r, n) for _, _, l in parts for a, r, n in l]

            def plan_n(pr, ins, o=o, flat=flat):
                copies, at = [], 0
                for i, r, n in flat:
                    copies.append((ins[i].at[pl.ds(r, n)], o, pl.ds(at, n), slice(None)))
                    at += n
                return copies

            plans.append(plan_n)
        for tie in ties:
            operand(tie)

        def jobs(pr, ins):
            return [c for plan in plans for c in plan(pr, ins)]

        bufs = pack(self.place, jobs, operands, shapes, f"pack_{t}") if shapes else []
        for kind, buf in zip(kinds, bufs):
            if kind == "x":
                self.direct[t] = to_chip(buf)
            else:
                got = (to_y if kind == "y" else to_z)(buf)
                at = 0
                for stage, bi, l in y_parts if kind == "y" else z_parts:
                    store = self.once if stage == "first" else self.twice
                    pair = store.setdefault(bi, [None, None])
                    pair[0 if kind == "y" else 1] = (got, at)
                    at += sum(n for _, _, n in l)
        if 0 <= b3 < len(bundles) and across:
            self.across(b3, bufs[:1] if bufs else ties)
        return [(self.direct[t], *spot) for spot in sent], bufs

    def across(self, b3, ties):
        b = self.bundles[b3]
        operands, shapes = [], []

        def operand(array):
            for i, o in enumerate(operands):
                if o is array:
                    return i
            operands.append(array)
            return len(operands) - 1

        plans = []

        def out(kind, rows, cols=PANEL):
            shapes.append((rows, cols))
            return len(shapes) - 1

        total = 4 * quarter_rows(b.first + b.second)
        o = out("c", (2 if b.joined else 1) * total)
        used = [
            (operand(self.weights[q[0]]), q, p)
            for p in (b.first + b.second if b.joined else ()) for q in p.parts
        ]
        qa = quarter_rows(b.first)
        qb = quarter_rows(b.second)
        (ya, yo), (za, zo) = self.once[b3]
        (ys, yso), (zs, zso) = self.twice[b3]
        d = operand(self.direct[b3])
        sides = [
            (b.first, [(0, d, 0), (1, operand(ya), yo), (2, operand(zs), zso), (3, operand(zs), zso + qa)]),
            (b.second, [(0, d, qa), (2, operand(za), zo), (1, operand(ys), yso), (3, operand(ys), yso + qb)]),
        ]

        def plan_c(pr, ins, o=o, sides=sides, used=used, total=total):
            copies, base, at, col = [], total if b.joined else 0, 0, 0
            for i, (_, c, n), p in used:
                copies.append((ins[i].at[pl.ds(p.row, p.rows), pl.ds(c, n)],
                               o, pl.ds(at, p.rows), pl.ds(col, n)))
                col += n
                if col == PANEL:
                    at, col = at + p.rows, 0
            for pieces, quarters in sides:
                at = 0
                for p in pieces:
                    q = p.rows // 4
                    for flip, i, r in quarters:
                        to = pl.multiple_of(base + quarter_start(pr, flip, q), 16)
                        copies.append((ins[i].at[pl.ds(r + at, q)], o, pl.ds(to, q), slice(None)))
                    at += q
                    base += p.rows
            return copies

        plans.append(plan_c)

        for tie in ties:
            operand(tie)
        jobs = lambda pr, ins: plans[0](pr, ins)
        (buf,) = pack(self.place, jobs, operands, shapes, f"across_{b3}")
        self.here[b3], self.there[b3] = buf, to_core(buf)


def land_copies(place_ref, bundle, own, near, here, there, targets):
    copies = []
    shard = 0 if place_ref is None else place_ref[0]
    pieces = bundle.first + bundle.second
    total = sum(p.rows for p in pieces)
    skip = total if bundle.joined else 0
    for slot, (ref, base) in enumerate(((None, 0), (there, 0), (here, skip), (there, skip))):
        for p in pieces:
            to = (shard ^ slot) * p.block + p.to_row
            to = pl.ds(pl.multiple_of(to, 16), p.rows)
            dst = targets[p.target]
            key = (p.target, p.to_col)
            if slot == 0 or slot == 1 and not bundle.joined:
                col = p.to_col
                for source, c, n in p.parts:
                    copies.append(((near if slot else own)[source].at[pl.ds(p.row, p.rows), pl.ds(c, n)],
                                   dst.at[to, pl.ds(col, n)], key))
                    col += n
            else:
                copies.append((ref.at[pl.ds(base, p.rows)], dst.at[to, pl.ds(p.to_col, PANEL)], key))
            base += p.rows
    return copies


def sources_of(bundle):
    return sorted({q[0] for p in bundle.first + bundle.second for q in p.parts})


def rotary_tables(positions, head_dim):
    half_dim = head_dim // 2
    freq_index = jnp.arange(half_dim).astype(F32)
    frequency = jnp.exp(freq_index * (-2.0 * math.log(ROPE_BASE) / head_dim))
    angles = positions[:, None] * frequency[None, :]
    return jnp.cos(angles), jnp.sin(angles)


def dot(left, right):
    return jnp.dot(left, right, preferred_element_type=F32)


def dot_nt(left, right):
    return lax.dot_general(left, right, (((1,), (1,)), ((), ())), preferred_element_type=F32)


def dot_tn(left, right):
    return lax.dot_general(left, right, (((0,), (0,)), ((), ())), preferred_element_type=F32)


LOG2E = 1.4426950408889634


def last_visible(place_ref, low, lanes, block):
    shard, prefix = place_ref[0], place_ref[2]
    at = shard % 2 if low else 2 + shard % 2
    position = at * block + lax.broadcasted_iota(jnp.int32, (1, lanes), 1) % block
    return jnp.maximum(position + 1, prefix)


def query_start(place_ref, low, block):
    chip = place_ref[0] // 2
    return pl.multiple_of((chip if low else 1 - chip) * block, block)


def natural_rows(place_ref, own, near, into, block, n):
    shard = place_ref[0]
    for slot, value in (
        (0, own[n, :block]),
        (2, own[n, block:]),
        (1, near[n, :block]),
        (3, near[n, block:]),
    ):
        into[n, pl.ds(pl.multiple_of((shard ^ slot) * block, block), block)] = value


def hide(scores, limit, first_key):
    keys = first_key + lax.broadcasted_iota(jnp.int32, scores.shape, 0)
    return jnp.where(keys < limit, scores, MASKED_SCORE)


def masked_by_part(low, scores, limit, block):
    if low:
        return hide(scores, limit, 0)
    half = 2 * block
    return jnp.concatenate([scores[:half], hide(scores[half:], limit, half)], axis=0)


def attend_kernel(place, q, k_own, k_near, v_own, v_near, out, lse, keys, values, *, scale):
    block = q.shape[1] // 2
    count_kv = k_own.shape[0]
    group = q.shape[0] // count_kv
    for n in range(count_kv):
        natural_rows(place, k_own, k_near, keys, block, n)
        natural_rows(place, v_own, v_near, values, block, n)
    for n in range(count_kv):
        values_t = values[n].T
        for part, low in enumerate((True, False)):
            count = (2 if low else 4) * block
            rows = pl.ds(query_start(place, low, block), block)
            query = jnp.concatenate([q[n * group + j, rows] for j in range(group)], axis=0)
            limit = last_visible(place, low, group * block, block)
            scores = masked_by_part(low, dot_nt(keys[n, :count], query), limit, block)
            top = jnp.max(scores, axis=0, keepdims=True)
            base = scale * LOG2E
            expo = jnp.exp2(scores * base - top * base)
            total = jnp.sum(expo, axis=0, keepdims=True)
            lse[n, part] = (top * base + jnp.log2(total))[0]
            result = dot(values_t[:, :count], expo.astype(BF16)) / total
            result = result.T.astype(BF16)
            for j in range(group):
                out[n * group + j, rows] = result[j * block : (j + 1) * block]


def attend(place, queries, kv_own, kv_near):
    heads, rows, dim = queries.shape
    kv_heads = kv_own.shape[0] // 2
    group = heads // kv_heads
    per = PER_STEP
    q_spec = pl.BlockSpec((per * group, rows, dim), lambda g, p: (g, 0, 0))
    kv_spec = pl.BlockSpec((per, rows, dim), lambda g, p: (g, 0, 0))
    v_spec = pl.BlockSpec((per, rows, dim), lambda g, p: (g + kv_heads // per, 0, 0))
    lse_shape = (kv_heads, 2, group * rows // 2)
    return pl.pallas_call(
        functools.partial(attend_kernel, scale=HEAD_DIM ** (-0.5)),
        out_shape=[
            jax.ShapeDtypeStruct(queries.shape, BF16),
            jax.ShapeDtypeStruct(lse_shape, F32),
        ],
        grid_spec=pltpu.PrefetchScalarGridSpec(
            num_scalar_prefetch=1,
            grid=(kv_heads // per,),
            in_specs=[q_spec, kv_spec, kv_spec, v_spec, v_spec],
            out_specs=[q_spec, pl.BlockSpec((per, *lse_shape[1:]), lambda g, p: (g, 0, 0))],
            scratch_shapes=[pltpu.VMEM((per, 2 * rows, dim), BF16)] * 2,
        ),
        compiler_params=pltpu.CompilerParams(vmem_limit_bytes=64 * 2**20),
        cost_estimate=work(EST),
        name="attend",
    )(place, queries, kv_own, kv_near, kv_own, kv_near)


def attend_back_kernel(
    place, q, k_own, k_near, v_own, v_near, grad, lse, cos_t, sin_t, *rest, scale
):
    dq, own_out, send_out, keys, values, dk, dv = rest[-7:]
    block = q.shape[1] // 2
    count_kv = k_own.shape[0]
    group = q.shape[0] // count_kv
    half = HEAD_DIM // 2
    for n in range(count_kv):
        natural_rows(place, k_own, k_near, keys, block, n)
        natural_rows(place, v_own, v_near, values, block, n)
    for n in range(count_kv):
        keys_t = keys[n].T
        for part, low in ((1, False), (0, True)):
            count = (2 if low else 4) * block
            start = query_start(place, low, block)
            rows = pl.ds(start, block)
            query = jnp.concatenate([q[n * group + j, rows] for j in range(group)], axis=0)
            out_grad = jnp.concatenate([grad[n * group + j, rows] for j in range(group)], axis=0)
            limit = last_visible(place, low, group * block, block)
            scores = masked_by_part(low, dot_nt(keys[n, :count], query), limit, block)
            probs = jnp.exp2(scores * (scale * LOG2E) - lse[n, part][None])
            probs_grad = dot_nt(values[n, :count], out_grad)
            mean = jnp.sum(probs * probs_grad, axis=0, keepdims=True)
            score_grad = (probs * (probs_grad - mean)).astype(BF16)
            v_part = dot(probs.astype(BF16), out_grad)
            k_part = dot(score_grad, query) * scale
            if low:
                dk[n, :count] += k_part
                dv[n, :count] += v_part
            else:
                dk[n] = k_part
                dv[n] = v_part
            turned = dot(keys_t[:, :count], score_grad) * scale
            cos = jnp.concatenate([cos_t[:, rows]] * group, axis=1)
            sin = jnp.concatenate([sin_t[:, rows]] * group, axis=1)
            u, w = turned[:half], turned[half : 2 * half]
            pad = jnp.zeros((q.shape[2] - 2 * half, u.shape[1]), F32)
            turned = jnp.concatenate([u * cos + w * sin, w * cos - u * sin, pad], axis=0)
            turned = turned.T.astype(BF16)
            for j in range(group):
                dq[n * group + j, rows] = turned[j * block : (j + 1) * block]
        shard = place[0]
        for slot, at, own in ((0, 0, True), (2, 1, True), (1, 0, False), (3, 1, False)):
            rows = pl.ds(pl.multiple_of((shard ^ slot) * block, block), block)
            to = slice(at * block, (at + 1) * block)
            out = own_out if own else send_out
            out[0, n, to] = dk[n, rows].astype(out.dtype)
            out[1, n, to] = dv[n, rows].astype(out.dtype)


def attend_back(place, queries, kv_own, kv_near, grad, lse, cos_t, sin_t, part, parts, ties):
    heads, rows, dim = queries.shape
    kv_heads = kv_own.shape[0] // 2
    group = heads // kv_heads
    count = kv_heads // parts
    per = PER_STEP
    base = part * count // per
    q_spec = pl.BlockSpec((per * group, rows, dim), lambda g, p: (g + base, 0, 0))
    kv_spec = pl.BlockSpec((per, rows, dim), lambda g, p: (g + base, 0, 0))
    v_spec = pl.BlockSpec((per, rows, dim), lambda g, p: (g + base + kv_heads // per, 0, 0))
    whole = pl.BlockSpec(cos_t.shape, lambda g, p: (0, 0))
    return pl.pallas_call(
        functools.partial(attend_back_kernel, scale=HEAD_DIM ** (-0.5)),
        out_shape=[
            jax.ShapeDtypeStruct((heads // parts, rows, dim), BF16),
            jax.ShapeDtypeStruct((2, count, rows, dim), F32),
            jax.ShapeDtypeStruct((2, count, rows, dim), BF16),
        ],
        grid_spec=pltpu.PrefetchScalarGridSpec(
            num_scalar_prefetch=1,
            grid=(count // per,),
            in_specs=[q_spec, kv_spec, kv_spec, v_spec, v_spec]
            + [q_spec, pl.BlockSpec((per, *lse.shape[1:]), lambda g, p: (g + base, 0, 0)), whole, whole]
            + [pl.BlockSpec(memory_space=pltpu.HBM)] * len(ties),
            out_specs=[pl.BlockSpec((per * group, rows, dim), lambda g, p: (g, 0, 0))] + [pl.BlockSpec((2, per, rows, dim), lambda g, p: (0, g, 0, 0))] * 2,
            scratch_shapes=[pltpu.VMEM((per, 2 * rows, dim), BF16)] * 2
            + [pltpu.VMEM((per, 2 * rows, dim), F32)] * 2,
        ),
        compiler_params=pltpu.CompilerParams(vmem_limit_bytes=64 * 2**20),
        cost_estimate=work(1),
        name=f"attend_back_{part}",
    )(place, queries, kv_own, kv_near, kv_own, kv_near, grad, lse, cos_t, sin_t, *ties)


def row_copies(sources, refs, into, sems):
    copies, at = [], into.shape[0] // 2
    for ref, (_, base, count) in zip(refs, sources):
        for c in range(into.shape[1] // PANEL):
            copies.append(
                pltpu.make_async_copy(
                    ref.at[pl.ds(base + c * count, count)],
                    into.at[pl.ds(at, count), pl.ds(c * PANEL, PANEL)],
                    sems.at[len(copies)],
                )
            )
        at += count
    return copies


class Landing:
    def __init__(self, place, bundle, refs, targets, sems):
        used = sources_of(bundle)
        n = len(used)
        own = dict(zip(used, refs[:n]))
        near = {} if bundle.joined else dict(zip(used, refs[n : 2 * n]))
        listed = land_copies(place, bundle, own, near, refs[-2], refs[-1], targets)
        self.copies = [
            (key, pltpu.make_async_copy(src, dst, sems.at[i])) for i, (src, dst, key) in enumerate(listed)
        ]
        self.copies.sort(key=lambda c: c[0])
        for _, c in self.copies:
            c.start()

    def wait(self, wanted=None):
        left = []
        for key, c in self.copies:
            if wanted is None or wanted(key):
                c.wait()
            else:
                left.append((key, c))
        self.copies = left


def landing_operands(bundle, weights, near, here, there):
    used = sources_of(bundle)
    return [weights[i] for i in used] + ([] if bundle.joined else [near[i] for i in used]) + [here, there]


def landing_count(bundle):
    return sum((1 if bundle.joined else 2) * len(p.parts) + 3 for p in bundle.first + bundle.second)


NO_BUNDLE = Bundle((), (), ())


def kernel_call(body, place, bundle, landing, operands, outs, scratch, name, time=0.5, ties=()):
    operands = [*operands, *((t, HB) for t in ties)]
    n_land, n_in, n_out, n_w = len(landing), len(operands), len(outs), len(bundle.shapes)

    def kernel(place_ref, *refs):
        land, refs = refs[:n_land], refs[n_land:]
        ins, refs = refs[: n_in - len(ties)], refs[n_in:]
        out, refs = refs[:n_out], refs[n_out:]
        body(place_ref, land, ins, out, refs[:n_w], refs[n_w], refs[n_w + 1 :])

    def spec(where):
        return where if isinstance(where, pl.BlockSpec) else pl.BlockSpec(memory_space=where)

    return pl.pallas_call(
        kernel,
        out_shape=[o for o, _ in outs],
        grid_spec=pltpu.PrefetchScalarGridSpec(
            num_scalar_prefetch=1,
            grid=(1,),
            in_specs=[spec(pltpu.HBM)] * n_land + [spec(w) for _, w in operands],
            out_specs=[spec(w) for _, w in outs],
            scratch_shapes=[pltpu.VMEM(sh, BF16) for sh in bundle.shapes]
            + [pltpu.SemaphoreType.DMA((max(landing_count(bundle), 1),))]
            + list(scratch),
        ),
        compiler_params=pltpu.CompilerParams(vmem_limit_bytes=64 * 2**20),
        cost_estimate=work(time),
        name=name,
    )(place, *landing, *[a for a, _ in operands])


VM = pltpu.VMEM
HB = pltpu.HBM


def like(shape, dtype):
    return jax.ShapeDtypeStruct(shape, dtype)


def turn(value, cos_full, sin_signed, half):
    swapped = jnp.concatenate([value[:, half:], value[:, :half]], axis=1)
    return value * cos_full + swapped * sin_signed


def padded(value):
    return jnp.concatenate([value, jnp.zeros((value.shape[0], LANES - HEAD_DIM), value.dtype)], axis=1)


def one_of_pair(block, width):
    return pl.BlockSpec((None, block, width), lambda i, p: (p[0] // 2, 0, 0))


def qkv_forward(place, bundle, landing, tokens, tokens_back, gain, inner, outer, cos, sin, ties):
    _, block, width = tokens.shape
    rows = 2 * block
    total = bundle.shapes[0][1]
    kv = (total - width) // 2
    wide = 8 * HEAD_DIM
    half = HEAD_DIM // 2

    def body(pr, land_refs, ins, outs, weights, sems, scratch):
        kept, *backs, gain_ref, inner_ref, outer_ref, cos_ref, sin_ref = ins
        q, kv_ref, hidden_ref, normed_ref, x_ref = outs
        (w,) = weights
        arriving = row_copies(tokens_back, backs, x_ref, scratch[0])
        for c in arriving:
            c.start()
        landing = Landing(pr, bundle, land_refs, weights, sems)
        x_ref[:block] = kept[...]
        for c in arriving:
            c.wait()
        x = x_ref[...].astype(F32)
        scale = lax.rsqrt(jnp.mean(x * x, axis=-1, keepdims=True) + EPSILON)
        normed_ref[...] = (x * scale * gain_ref[...].astype(F32)).astype(BF16)
        hidden_ref[...] = dot_nt(normed_ref[...], inner_ref[...]).astype(BF16)

        def columns(at):
            cols = pl.ds(at, wide)
            return dot(normed_ref[...], w[:, cols]) + dot(hidden_ref[...], outer_ref[:, cols])

        landing.wait(lambda key: key[1] < width)
        for i in range(width // wide):
            acc = columns(i * wide)
            for h in range(8):
                one = acc[:, h * HEAD_DIM : (h + 1) * HEAD_DIM]
                q[8 * i + h] = padded(turn(one, cos_ref[...], sin_ref[...], half)).astype(BF16)
        landing.wait()
        acc = columns(width)
        for h in range(8):
            one = acc[:, h * HEAD_DIM : (h + 1) * HEAD_DIM]
            kv_ref[h] = padded(turn(one, cos_ref[...], sin_ref[...], half)).astype(BF16)
        acc = columns(width + kv)
        for h in range(8):
            kv_ref[8 + h] = padded(acc[:, h * HEAD_DIM : (h + 1) * HEAD_DIM]).astype(BF16)

    heads = width // HEAD_DIM
    return kernel_call(
        body, place, bundle, landing,
        [(tokens, one_of_pair(block, width)), *((t[0], HB) for t in tokens_back), (gain, VM), (inner, VM), (outer, VM), (cos, VM), (sin, VM)],
        [
            (like((heads, rows, LANES), BF16), VM),
            (like((2 * kv // HEAD_DIM, rows, LANES), BF16), VM),
            (like((rows, inner.shape[0]), BF16), VM),
            (like((rows, width), BF16), VM),
            (like((rows, width), BF16), VM),
        ],
        [pltpu.SemaphoreType.DMA((len(tokens_back) * width // PANEL,))], "qkv_forward", time=EST, ties=ties,
    )


def out_forward(place, bundle, landing, heads_out, x, gain, inner, outer, cot, cot_back, inner_gl, drop_b):
    rows, width = x.shape
    heads = heads_out.shape[0]

    def body(pr, land_refs, ins, outs, weights, sems, scratch):
        heads_ref, x_ref, gain_ref, inner_ref, outer_ref, cot_kept, *cot_got, igl, db = ins
        middle, normed, attended, hidden, cot_ref, h_gl, h_d = outs
        arriving = row_copies(cot_back, cot_got, cot_ref, scratch[0])
        for c in arriving:
            c.start()
        landing = Landing(pr, bundle, land_refs, weights, sems)
        for h in range(heads):
            attended[:, h * HEAD_DIM : (h + 1) * HEAD_DIM] = heads_ref[h, :, :HEAD_DIM]
        hidden[...] = dot_nt(attended[...], inner_ref[...]).astype(BF16)
        cot_ref[: rows // 2] = cot_kept[...]
        for c in arriving:
            c.wait()
        h_d[...] = dot_nt(cot_ref[...], db[...]).astype(BF16)
        landing.wait()
        wide = width // 2
        squares = jnp.zeros((rows, 1), F32)
        for i in range(2):
            cols = pl.ds(i * wide, wide)
            branch = dot(attended[...], weights[0][:, cols]) + dot(hidden[...], outer_ref[:, cols])
            value = x_ref[:, cols].astype(F32) + branch
            middle[:, cols] = value
            squares += jnp.sum(value * value, axis=-1, keepdims=True)
        scale = lax.rsqrt(squares / width + EPSILON)
        normed[...] = (middle[...] * scale * gain_ref[...].astype(F32)).astype(BF16)
        h_gl[...] = dot_nt(normed[...], igl[...]).astype(BF16)

    return kernel_call(
        body, place, bundle, landing,
        [(heads_out, VM), (x, VM), (gain, VM), (inner, VM), (outer, VM),
         (cot, one_of_pair(rows // 2, width)), *((c[0], HB) for c in cot_back), (inner_gl, VM), (drop_b, VM)],
        [
            (like((rows, width), F32), VM),
            (like((rows, width), BF16), VM),
            (like((rows, width), BF16), VM),
            (like((rows, RANK), BF16), VM),
            (like((rows, width), BF16), VM),
            (like((rows, 2 * RANK), BF16), VM),
            (like((rows, RANK), BF16), VM),
        ],
        [pltpu.SemaphoreType.DMA((len(cot_back) * width // PANEL,))], "out_forward", time=EST,
    )


def mlp_chunk(place, bundle, landing, normed, cot, hidden_gl, hidden_d, outer_gl, drop_a, chunk, sums, name):
    rows, width = normed.shape
    units = bundle.shapes[1][0]
    steps = units // PANEL
    first = sums is None
    part = units // 4

    def body(pr, land_refs, ins, outs, weights, sems, scratch):
        normed_ref, cot_ref, hgl_ref, hd_ref, ogl, da = ins[:6]
        drop_sum, e_sum, thin, keep, send = outs
        (packed,) = scratch
        w_gl, w_d = weights
        landing = Landing(pr, bundle, land_refs, weights, sems)
        h_d = hd_ref[...]
        h_g, h_l = hgl_ref[:, :RANK], hgl_ref[:, RANK:]
        g_t, l_t, d_t = h_g.T, h_l.T, h_d.T
        for i in range(steps):
            landing.wait(lambda key: key[0] == 1 or key[1] < 2 * (i + 1) * PANEL)
            cols = slice(i * PANEL, (i + 1) * PANEL)
            both = pl.ds(2 * i * PANEL, 2 * PANEL)
            acts = dot(normed_ref[...], w_gl[:, both])
            gate = acts[:, :PANEL] + dot(h_g, ogl[:RANK, cols])
            lift = acts[:, PANEL:] + dot(h_l, ogl[RANK:, cols])
            a_grad = dot_nt(cot_ref[...], w_d[cols]) + dot(h_d, da[:, cols])
            sig = 1.0 / (1.0 + jnp.exp(-gate))
            silu = gate * sig
            active = (silu * lift).astype(BF16)
            gate_grad = (a_grad * lift * sig * (1.0 + gate * (1.0 - sig))).astype(BF16)
            lift_grad = (a_grad * silu).astype(BF16)
            grads = jnp.concatenate([gate_grad, lift_grad], axis=1)
            down = dot(active, w_d[cols])
            back = dot_nt(grads, w_gl[:, both])
            t0 = dot_nt(active, da[:, cols])
            t1 = dot_nt(gate_grad, ogl[:RANK, cols])
            t2 = dot_nt(lift_grad, ogl[RANK:, cols])
            if i == 0 and first:
                drop_sum[...] = down
                e_sum[...] = back
                thin[0], thin[1], thin[2] = t0, t1, t2
            elif i == 0:
                drop_sum[...] = ins[6][...] + down
                e_sum[...] = ins[7][...] + back
                thin[0], thin[1], thin[2] = ins[8][0] + t0, ins[8][1] + t1, ins[8][2] + t2
            else:
                drop_sum[...] += down
                e_sum[...] += back
                thin[0] += t0
                thin[1] += t1
                thin[2] += t2
            per = PANEL // part
            for j, g in enumerate((dot(g_t, gate_grad), dot(l_t, lift_grad), dot(d_t, active))):
                for o in range(per):
                    packed[i * per + o, :, j * part : (j + 1) * part] = g[:, o * part : (o + 1) * part]
        split_by_core(pr, packed, keep, send)

    at_chunk = lambda i, p: (chunk, 0, 0)
    operands = [
        (normed, VM), (cot, VM), (hidden_gl, VM), (hidden_d, VM),
        (outer_gl, pl.BlockSpec((None, *outer_gl.shape[1:]), at_chunk)),
        (drop_a, pl.BlockSpec((None, *drop_a.shape[1:]), at_chunk)),
    ]
    if not first:
        operands += [(s, VM) for s in sums]
    return kernel_call(
        body, place, bundle, landing, operands,
        [
            (like((rows, width), F32), VM),
            (like((rows, width), F32), VM),
            (like((3, rows, RANK), F32), VM),
            (like((2, RANK, 3 * part), F32), VM),
            (like((2, RANK, 3 * part), BF16), VM),
        ],
        [pltpu.VMEM((4, RANK, 3 * part), F32)], name, time=EST,
    )


def split_by_core(place_ref, whole, keep, send):
    core = place_ref[0] % 2
    for j in range(2):
        keep[j] = whole[core + 2 * j]
        send[j] = whole[1 - core + 2 * j].astype(BF16)


def out_backward(place, bundle, landing, sums, middle, cot, gain, normed, attended, hidden, factors, ties):
    rows, width = middle.shape
    heads = width // HEAD_DIM

    def body(pr, land_refs, ins, outs, weights, sems, scratch):
        drop_sum, e_sum, thin, middle_ref, cot_ref, gain_ref, normed_ref, att, hid, drop_b, igl, o_a, o_b = ins
        mixed_kept, mixed_back, mid_grad, out_heads, keep, send = outs
        (w,) = weights
        branch, whole = scratch
        landing = Landing(pr, bundle, land_refs, weights, sems)
        d_hid = thin[0].astype(BF16)
        gl_grad = jnp.concatenate([thin[1].astype(BF16), thin[2].astype(BF16)], axis=1)
        e_in = (e_sum[...] + dot(gl_grad, igl[...])) * gain_ref[...].astype(F32)
        mid = middle_ref[...]
        scale = lax.rsqrt(jnp.mean(mid * mid, axis=-1, keepdims=True) + EPSILON)
        n = mid * scale
        mean = jnp.mean(e_in * n, axis=-1, keepdims=True)
        mid_grad[...] = cot_ref[...].astype(F32) + scale * (e_in - n * mean)
        branch[...] = mid_grad[...].astype(BF16)
        hgrad = dot_nt(branch[...], o_b[...]).astype(BF16)
        landing.wait()
        wide = 8 * HEAD_DIM
        for i in range(heads // 8):
            part = slice(i * wide, (i + 1) * wide)
            grad = dot_nt(branch[...], w[part]) + dot(hgrad, o_a[:, part])
            for h in range(8):
                out_heads[8 * i + h] = padded(grad[:, h * HEAD_DIM : (h + 1) * HEAD_DIM]).astype(BF16)
        mixed = (mid + drop_sum[...] + dot(d_hid, drop_b[...])).astype(BF16)
        mixed_kept[...] = mixed[: rows // 2]
        mixed_back[...] = mixed[rows // 2 :]
        gl = dot(gl_grad.T, normed_ref[...])
        own = (
            dot(d_hid.T, cot_ref[...]), gl[:RANK], gl[RANK:],
            dot(hgrad.T, att[...]), dot(hid[...].T, branch[...]),
        )
        for t in range(4):
            for j, g in enumerate(own):
                at = j * quarter
                whole[t, :, at : at + quarter] = g[:, t * quarter : (t + 1) * quarter]
        split_by_core(pr, whole, keep, send)

    quarter = width // 4
    cols = 5 * quarter
    return kernel_call(
        body, place, bundle, landing,
        [(v, VM) for v in (*sums, middle, cot, gain, normed, attended, hidden, *factors)],
        [
            (like((2, rows // 2, width), BF16), one_of_pair(rows // 2, width)),
            (like((rows // 2, width), BF16), VM),
            (like((rows, width), F32), VM),
            (like((heads, rows, LANES), BF16), VM),
            (like((2, RANK, cols), F32), VM),
            (like((2, RANK, cols), BF16), VM),
        ],
        [pltpu.VMEM((rows, width), BF16), pltpu.VMEM((4, RANK, cols), F32)], "out_backward", time=15, ties=ties,
    )


def qkv_gradients(place, parts, cos, sin, normed, hidden, outer, ties):
    rows, width = normed.shape
    total = outer.shape[1]
    kv = (total - width) // 2
    half = HEAD_DIM // 2
    rank3 = outer.shape[0]
    quarter, kv_quarter = width // 4, kv // 4
    cols = 4 * quarter + 2 * kv_quarter
    q_count, kv_count = parts[0][0].shape[0], parts[0][1].shape[1]

    def body(pr, land_refs, ins, outs, weights, sems, scratch):
        *part_refs, cos_ref, sin_ref, nrm, hid, b = ins
        dq_refs, dkv_refs, got_refs = part_refs[0::3], part_refs[1::3], part_refs[2::3]
        g, hgrad_ref, keep, send = outs
        (whole,) = scratch
        for h in range(width // HEAD_DIM):
            ref, i = dq_refs[h // q_count], h % q_count
            g[:, h * HEAD_DIM : (h + 1) * HEAD_DIM] = ref[i, :, :HEAD_DIM]
        for h in range(kv // HEAD_DIM):
            dkv_ref, got_ref, i = dkv_refs[h // kv_count], got_refs[h // kv_count], h % kv_count
            one = (dkv_ref[0, i] + got_ref[0, i].astype(F32))[:, :HEAD_DIM]
            at = width + h * HEAD_DIM
            g[:, at : at + HEAD_DIM] = turn(one, cos_ref[...], -sin_ref[...], half).astype(BF16)
            at += kv
            g[:, at : at + HEAD_DIM] = (dkv_ref[1, i] + got_ref[1, i].astype(F32))[:, :HEAD_DIM].astype(BF16)
        hgrad_ref[...] = dot_nt(g[...], b[...]).astype(BF16)
        g_in = dot(hgrad_ref[...].T, nrm[...])
        g_out = dot(hid[...].T, g[...])
        for t in range(4):
            for i in range(3):
                whole[t, :, i * quarter : (i + 1) * quarter] = g_in[
                    i * RANK : (i + 1) * RANK, t * quarter : (t + 1) * quarter
                ]
            whole[t, :, 3 * quarter : 4 * quarter] = g_out[:RANK, t * quarter : (t + 1) * quarter]
            for i in range(2):
                at, start = 4 * quarter + i * kv_quarter, width + i * kv + t * kv_quarter
                whole[t, :, at : at + kv_quarter] = g_out[
                    (1 + i) * RANK : (2 + i) * RANK, start : start + kv_quarter
                ]
        split_by_core(pr, whole, keep, send)

    return kernel_call(
        body, place, NO_BUNDLE, [],
        [(v, VM) for v in (*[v for p in parts for v in p], cos, sin, normed, hidden, outer)],
        [
            (like((rows, total), BF16), VM),
            (like((rows, rank3), BF16), VM),
            (like((2, RANK, cols), F32), VM),
            (like((2, RANK, cols), BF16), VM),
        ],
        [pltpu.VMEM((4, RANK, cols), F32)], "qkv_gradients", time=1, ties=ties,
    )


def qkv_backward(place, bundle, landing, g, hgrad, x, mid_grad, gain, inner, ties):
    rows, width = x.shape
    total = bundle.shapes[0][1]
    block = rows // 2

    def body(pr, land_refs, ins, outs, weights, sems, scratch):
        g_ref, hg, x_ref, mg, gain_ref, a = ins
        kept, back = outs
        (w,) = weights
        landing = Landing(pr, bundle, land_refs, weights, sems)
        xf = x_ref[...].astype(F32)
        scale = lax.rsqrt(jnp.mean(xf * xf, axis=-1, keepdims=True) + EPSILON)
        n = xf * scale
        thin = dot(hg[...], a[...])
        landing.wait()
        e_in = (dot_nt(g_ref[...], w[...]) + thin) * gain_ref[...].astype(F32)
        mean = jnp.mean(e_in * n, axis=-1, keepdims=True)
        result = mg[...] + scale * (e_in - n * mean)
        kept[...] = result[:block]
        back[...] = result[block:].astype(BF16)

    return kernel_call(
        body, place, bundle, landing,
        [(v, VM) for v in (g, hgrad, x, mid_grad, gain, inner)],
        [(like((2, block, width), F32), one_of_pair(block, width)), (like((block, width), BF16), VM)],
        [], "qkv_backward", time=0.2, ties=ties,
    )


def complete(place, partial, back, ties, name):
    _, block, width = partial.shape

    def kernel(place_ref, partial_ref, back_ref, *rest):
        rest[-1][...] = back_ref[...].astype(partial.dtype)

    return pl.pallas_call(
        kernel,
        out_shape=jax.ShapeDtypeStruct(partial.shape, partial.dtype),
        grid_spec=pltpu.PrefetchScalarGridSpec(
            num_scalar_prefetch=1,
            grid=(1,),
            in_specs=[pl.BlockSpec(memory_space=pltpu.HBM), pl.BlockSpec(memory_space=pltpu.VMEM)]
            + [pl.BlockSpec(memory_space=pltpu.HBM)] * len(ties),
            out_specs=pl.BlockSpec((None, block, width), lambda i, p: (1 - p[0] // 2, 0, 0)),
        ),
        input_output_aliases={1: 0},
        compiler_params=pltpu.CompilerParams(vmem_limit_bytes=64 * 2**20),
        cost_estimate=work(0.5),
        name=name,
    )(place, partial, back, *ties)


def pack_factors(place, inners, outers):
    widths = [a.shape[0] for a in inners] + [b.shape[1] for b in outers]
    n = len(inners)
    mix = outers[0].shape[0]
    narrow = (n + 1, n + 2)

    def body(pr, land_refs, ins, outs, weights, sems, scratch):
        for which, out in enumerate(outs):
            row = lax.broadcasted_iota(jnp.int32, (RANK, mix), 0) + pr[3 + which] * RANK
            choose = (row == lax.broadcasted_iota(jnp.int32, (RANK, mix), 1)).astype(F32).astype(BF16)
            at = 0
            for i, ref in enumerate(ins):
                part = dot_nt(choose, ref[...]) if i < n or i in narrow else dot(choose, ref[...])
                out[:, at : at + widths[i]] = part.astype(BF16)
                at += widths[i]

    shape = (like((RANK, sum(widths)), BF16), VM)
    return kernel_call(
        body, place, NO_BUNDLE, [], [(v.T if i in narrow else v, VM) for i, v in enumerate((*inners, *outers))],
        [shape, shape], [], "pack_factors",
    )


def unpack_factors(place, slots, widths, chunks):
    inner_w, outer_w = widths[:7], widths[7:]
    width, kv = 4 * outer_w[0], 4 * outer_w[1]
    part = outer_w[4] // chunks
    starts = [sum(widths[:i]) for i in range(len(widths))]

    def body(pr, land_refs, ins, outs, weights, sems, scratch):
        iq, oq, io, oo, igl, ogl, da, db = outs
        (nat,) = scratch
        mine, two, got = ins
        nat[pr[0]] = mine[...]
        nat[pr[0] ^ 2] = two[...]
        nat[pr[0] ^ 1] = got[:RANK]
        nat[pr[0] ^ 3] = got[RANK:]
        oq[...] = jnp.zeros(oq.shape, BF16)
        for t in range(4):
            get = lambda i, a=0, n=None: nat[t, :, starts[i] + a : starts[i] + a + (n or widths[i])]
            w = inner_w[0]
            here = slice(t * w, (t + 1) * w)
            for i in range(3):
                iq[i * RANK : (i + 1) * RANK, here] = get(i)
            io[:, here] = get(3)
            igl[:RANK, here] = get(4)
            igl[RANK:, here] = get(5)
            base = 0
            for i in range(3):
                n = outer_w[i]
                oq[i * RANK : (i + 1) * RANK, base + t * n : base + (t + 1) * n] = get(7 + i)
                base += 4 * n
            oo[:, here] = get(10)
            db[:, here] = get(13)
            for u in range(chunks):
                there = slice(t * part, (t + 1) * part)
                ogl[u, :RANK, there] = get(11, u * part, part)
                ogl[u, RANK:, there] = get(12, u * part, part)
                da[u, :, there] = get(6, u * part, part)

    shapes = [
        (3 * RANK, width), (3 * RANK, width + 2 * kv), (RANK, width), (RANK, width), (2 * RANK, width),
        (chunks, 2 * RANK, 4 * part), (chunks, RANK, 4 * part), (RANK, width),
    ]
    return kernel_call(
        body, place, NO_BUNDLE, [], [(v, VM) for v in slots], [(like(sh, BF16), VM) for sh in shapes],
        [pltpu.VMEM((4, *slots[0].shape), BF16)], "unpack_factors",
    )


def fold_cores(place, sums, name, ties=()):
    n = len(sums)
    cols = sum(k.shape[2] for k, _ in sums)

    def body(pr, land_refs, ins, outs, weights, sems, scratch):
        chip = pr[0] // 2
        for out, which in zip(outs, (chip, 1 - chip)):
            at = 0
            for keep_ref, got_ref in zip(ins[:n], ins[n:]):
                w = keep_ref.shape[2]
                out[:, at : at + w] = (keep_ref[which] + got_ref[which].astype(F32)).astype(BF16)
                at += w
            out[:, cols:] = jnp.full((RANK, LANES), pr[3], jnp.int32).astype(F32).astype(BF16)

    shape = (like((RANK, cols + LANES), BF16), VM)
    return kernel_call(
        body, place, NO_BUNDLE, [], [(k, VM) for k, _ in sums] + [(g, VM) for _, g in sums],
        [shape, shape], [], name, ties=ties,
    )


def spread_sums(place, groups, pieces, mix, name, ties=()):
    count = sum(v.shape[0] for v in groups[0])
    tall = [len(g) > 1 for g in groups]

    def body(pr, land_refs, ins, outs, weights, sems, scratch):
        gots, at, held = [], 0, list(scratch)
        for g in groups:
            refs = ins[at : at + len(g)]
            at += len(g)
            if len(g) == 1:
                gots.append(refs[0])
                continue
            got, row = held.pop(0), 0
            for ref in refs:
                got[row : row + ref.shape[0]] = ref[...]
                row += ref.shape[0]
            gots.append(got)
        tag = gots[0][:, -LANES:].astype(F32).astype(jnp.int32) * RANK
        spot = tag + lax.broadcasted_iota(jnp.int32, (count, LANES), 0) % RANK
        choose = (spot == lax.broadcasted_iota(jnp.int32, (count, LANES), 1)).astype(F32).astype(BF16)
        choose_t = choose.T
        for out, (is_inner, runs) in zip(outs, pieces):
            at = 0
            for g, start, n in runs:
                if is_inner:
                    out[at : at + n] = dot_tn(gots[g][:, start : start + n], choose)
                else:
                    out[:, at : at + n] = dot(choose_t, gots[g][:, start : start + n])
                at += n

    outs = []
    for is_inner, runs in pieces:
        n = sum(c for _, _, c in runs)
        outs.append((like((n, mix) if is_inner else (mix, n), F32), VM))
    scratch = [pltpu.VMEM((count, g[0].shape[1]), BF16) for g, t in zip(groups, tall) if t]
    return kernel_call(
        body, place, NO_BUNDLE, [], [(v, VM) for g in groups for v in g], outs, scratch, name, ties=ties
    )


def local(
    tokens,
    cotangent,
    prefix_len,
    adapter_index,
    gain_attn,
    gain_mlp,
    query_weight,
    key_weight,
    value_weight,
    output_weight,
    gate_weight,
    lift_weight,
    drop_weight,
    *factors,
):
    _, block, width = tokens.shape
    rep, shard = lax.axis_index("rep"), lax.axis_index("shard")
    chip = shard // 2
    rows = 2 * block
    kv_width = KV_HEADS * HEAD_DIM
    where = jnp.stack([shard, rep % 4]).astype(jnp.int32)
    place = jnp.concatenate(
        [where, jnp.stack([prefix_len[chip], adapter_index[chip], adapter_index[1 - chip]])]
    )

    weights = (query_weight, key_weight, value_weight, output_weight, gate_weight, lift_weight, drop_weight)
    inners, outers = factors[0::2], factors[1::2]
    widths = [a.shape[0] for a in inners] + [b.shape[1] for b in outers]
    chunks = 4
    ff = gate_weight.shape[1]
    bundles = make_bundles(width, kv_width, ff, chunks, 4)
    positions = jnp.concatenate(
        [shard * block + jnp.arange(block), (shard ^ 2) * block + jnp.arange(block)]
    )
    cos_table, sine_table = rotary_tables(positions.astype(F32), HEAD_DIM)
    cos_full = jnp.concatenate([cos_table, cos_table], axis=1)
    sin_full = jnp.concatenate([-sine_table, sine_table], axis=1)
    gain_one, gain_two = gain_attn[None], gain_mlp[None]
    cos_t, sin_t = cos_table.T, sine_table.T

    relay = Relay(where, weights, bundles)
    half = block // 2
    near = {i: to_core(weights[i]) for i in (4, 5, 6)}
    relay.step()
    mine, others = pack_factors(place, inners, outers)
    slot_two = to_chip(others)
    (tokens_a,), _ = relay.step([(tokens, 0, half)], ties=(near[4], near[5], sin_full, cos_full, cos_t, sin_t, gain_one, gain_two, place))
    (tokens_b,), _ = relay.step([(tokens, half, half)], ties=(slot_two,))
    joined = join(mine, slot_two)
    got = to_core(joined)
    relay.step(ties=(near[6], got))
    inner_qkv, outer_qkv, inner_o, outer_o, inner_gl, outer_gl, drop_a, drop_b = unpack_factors(
        place, (mine, slot_two, got), widths, chunks
    )

    def landing(i):
        return landing_operands(bundles[i], weights, near, relay.here[i], relay.there[i])

    (cot_a,), begun = relay.step([(cotangent, 0, half)], ties=(inner_qkv,), across=False)
    queries, kv_own, hidden_qkv, normed_attn, x = qkv_forward(
        place, bundles[0], landing(0), tokens, (tokens_a, tokens_b), gain_one,
        inner_qkv, outer_qkv, cos_full, sin_full, begun[:1],
    )
    (cot_b,), begun = relay.step([(cotangent, half, half)], ties=(x,))
    kv_own = gate(kv_own, begun[:1])
    relay.across(1, begun[:1])
    kv_near = to_core(kv_own)
    heads_out, lse = attend(place, queries, kv_own, kv_near)
    middle, normed_mlp, attended, output_hidden, cot, hidden_gl, hidden_d = out_forward(
        place, bundles[1], landing(1), heads_out, x, gain_two, inner_o, outer_o,
        cotangent, (cot_a, cot_b), inner_gl, drop_b,
    )
    relay.step(ties=(normed_mlp,))
    sums, kept_sums = None, []
    for u in range(chunks):
        *sums, keep, send = mlp_chunk(
            place, bundles[2 + u], landing(2 + u), normed_mlp, cot, hidden_gl, hidden_d,
            outer_gl, drop_a, u, sums, f"mlp_{u}",
        )
        kept_sums.append((keep, to_core(send)))
        if u < 2:
            relay.step(ties=(keep,))
    early = fold_cores(place, kept_sums[:-1], "fold_early", (keep,))
    mixed_kept, mixed_back, middle_grad, grad_heads, keep, send = out_backward(
        place, bundles[1], landing(1), sums, middle, cot, gain_two, normed_mlp, attended,
        output_hidden, (drop_b, inner_gl, inner_o, outer_o), early[:1],
    )

    mixed_back = to_chip(mixed_back)
    early = join(early[0], to_chip(early[1]), ties=(grad_heads,))
    folded = fold_cores(place, [kept_sums[-1], (keep, to_core(send))], "fold_late")
    parts, halves = [], 2
    for i in range(halves):
        dq, dkv, dkv_send = attend_back(
            place, queries, kv_own, kv_near, grad_heads, lse, cos_t, sin_t, i, halves,
            folded if i else (early,),
        )
        if i:
            late = to_chip(folded[1])
            dkv_send = gate(dkv_send, (late, mixed_back))
        parts.append((dq, dkv, to_core(dkv_send)))
    early = lax.all_gather(early, "rep", axis=0, tiled=True)
    late_both = join(folded[0], late, ties=parts[0][:1])
    late = lax.all_gather(late_both, "rep", axis=0, tiled=True)
    g, hgrad, keep, send = qkv_gradients(
        place, parts, cos_full, sin_full, normed_attn, hidden_qkv, outer_qkv, (late_both,)
    )
    folded = fold_cores(place, [(keep, to_core(send))], "fold_first")
    other = to_chip(folded[1])
    both = join(folded[0], other)
    input_kept, input_back = qkv_backward(
        place, bundles[0], landing(0), g, hgrad, x, middle_grad, gain_one, inner_qkv, (both, early)
    )
    line = [both]
    for k in range(2, lax.axis_size("rep"), 2):
        line.append(move(both, lambda r, s, k=k: (r ^ k, s)))
    line = join(*line, ties=(input_back,))
    input_back = to_chip(gate(input_back, (line,)))
    first = [line, to_y(line)]
    mixed = complete(place, mixed_kept, mixed_back, (), "complete_mixed")

    mix = ADAPTERS * RANK
    w, kw = width // 4, kv_width // 4
    part = ff // 4 // chunks
    wide = 3 * part
    runs = lambda j: [
        (0, u * wide + j * part, part) if u < chunks - 1 else (1, j * part, part) for u in range(chunks)
    ]
    rest = lambda j: [(1, wide + j * w, w)]
    g_out, l_out, d_in, d_out, g_in, l_in, o_in, o_out = spread_sums(
        place, [[early], [late]],
        [(False, runs(0)), (False, runs(1)), (True, runs(2)), (False, rest(0)), (True, rest(1)),
         (True, rest(2)), (True, rest(3)), (False, rest(4))],
        mix, "spread_late",
    )
    q_in, k_in, v_in, q_out, k_out, v_out = spread_sums(
        place, [first],
        [(True, [(0, 0, w)]), (True, [(0, w, w)]), (True, [(0, 2 * w, w)]), (False, [(0, 3 * w, w)]),
         (True, [(0, 4 * w, kw)]), (True, [(0, 4 * w + kw, kw)])],
        mix, "spread_first", (o_out,),
    )
    k_out, v_out = k_out.T, v_out.T
    input_grad = complete(place, input_kept, input_back, (q_in,), "complete_input_grad")
    return (mixed, input_grad, q_in, q_out, k_in, k_out, v_in, v_out, o_in, o_out,
            g_in, g_out, l_in, l_out, d_in, d_out)


def solution(mesh):
    token_place = P("rep", "shard", None)
    row, col = P("shard", None), P(None, "shard")
    return jax.shard_map(
        local,
        mesh=mesh,
        in_specs=(token_place, token_place, P("rep"), P("rep"), P(), P()) + (row,) * 7 + (row, col) * 7,
        out_specs=(token_place, token_place) + (row, col) * 7,
        check_vma=False,
    )
```
